32 devices in a mesh: region: 8 (over y, x, core), grp: 4 (over z).
Axes of the slice: x: 2, y: 2, z: 4, core: 2. Of those that a mesh axis runs over, the one named last changes fastest.
Arguments:
- transmission: float32 [2, 640, 5120], P(None, 'grp', 'region'), may hold values from -3 to 3
- probe: bfloat16 [2, 8, 512, 512], P(None, None, 'grp'), may hold values from -1.5 to 1.5
- measured: float32 [8, 512, 512], P('region', 'grp'), may hold values from 0 to 2
- positions: int32 [8, 2], P('region'), may hold values from 0 to 128
- past_steps: float32 [4, 2, 640, 5120], P(None, None, 'grp', 'region'), may hold values from -40 to 40
- past_changes: float32 [3, 2, 640, 5120], P(None, None, 'grp', 'region'), may hold values from -240 to 240
- old_gradient: float32 [2, 640, 5120], P(None, 'grp', 'region'), may hold values from -40 to 40
Outputs:
- updated: float32 [2, 640, 5120], P(None, 'grp', 'region')
- gradient: float32 [2, 640, 5120], P(None, 'grp', 'region')
The draws below stay inside these ranges and needn't reach their ends.
All inputs are finite; a program needn't handle non-finite values.
Results may differ from the reference program's by a relative error of at most 0.019.
The reference program's roundings to bfloat16 on the way count: a program that leaves them out, or rounds other values in their place, can miss the bound.
Values may be sent and summed in bfloat16 or wider, within the bound.
No kernel may reach another device: no remote copies, remote signals or barrier semaphores. Data moves between devices by JAX's collectives and lax.ppermute only.
A program may use at most 64 MiB of HBM per device.

```python
import math
import jax
import jax.numpy as jnp
from jax import lax

N = 512
MODES = 8
FR = 1
SPAN = 128
HIST = 4
OBJ = 640
OBJ_ALL = 5120
FRAMES = 8
N_REGION = 8


TIKHONOV = 0.5


def row_col_scale(key):
    key_rows, key_cols = jax.random.split(key)
    trend = math.log(3.0)
    place = jnp.arange(OBJ_ALL, dtype=jnp.float32) / (OBJ_ALL - 1)
    row_part = jnp.exp(trend * place + jax.random.uniform(key_rows, (OBJ_ALL,), jnp.float32, -1.15, 1.15))
    col_part = jnp.exp(jax.random.uniform(key_cols, (OBJ,), jnp.float32, -1.15, 1.15))
    return col_part[:, None] * row_part[None, :]


def history(key):
    keys = [jax.random.fold_in(key, 101 + index) for index in range(10)]
    base = jnp.clip(0.7 * jax.random.normal(keys[0], (2, OBJ, OBJ_ALL), jnp.float32), -3.0, 3.0)
    scale = row_col_scale(keys[1])
    pull = jax.random.uniform(keys[2], (HIST, 1, 1, 1), jnp.float32, 0.1, 0.5)
    noise = jax.random.normal(keys[3], (HIST, 2, OBJ, OBJ_ALL), jnp.float32)
    steps_all = jnp.clip(scale * (0.5 * noise - pull * base), -40.0, 40.0)
    curve = jnp.exp(jax.random.uniform(keys[5], (2, OBJ, OBJ_ALL), jnp.float32, math.log(0.5), math.log(2.0)))
    weak_pair = jax.random.randint(keys[6], (), 0, HIST - 1)
    strong = jnp.exp(jax.random.uniform(keys[7], (HIST - 1,), jnp.float32, math.log(0.6), math.log(3.0)))
    weak = jnp.exp(jax.random.uniform(keys[8], (HIST - 1,), jnp.float32, math.log(0.03), math.log(0.12)))
    kappa = jnp.where(jnp.arange(HIST - 1) == weak_pair, weak, strong)
    changes = kappa[:, None, None, None] * curve * steps_all[:HIST - 1]
    extra = jax.random.normal(keys[9], (2, OBJ, OBJ_ALL), jnp.float32)
    older = jnp.clip(TIKHONOV * base + scale * (pull[HIST - 1] * curve * base + 0.3 * extra), -40.0, 40.0)
    return (base, steps_all, changes, older)


def draw_transmission(key, part):
    return history(key)[0]


def draw_past_steps(key, part):
    return history(key)[1]


def draw_past_changes(key, part):
    return history(key)[2]


def draw_old_gradient(key, part):
    return history(key)[3]


def draw_positions(key, part):
    key_all, key_pick, key_other = jax.random.split(key, 3)
    spots = jax.random.randint(key_all, (FRAMES, 2), 0, SPAN + 1)
    first = jax.random.randint(key_pick, (), 0, FRAMES)
    second = jax.random.randint(key_other, (), 0, FRAMES)
    spots = spots.at[first, 0].set(SPAN)
    spots = spots.at[second, 1].set(0)
    return spots.astype(jnp.int32)


def block_levels(stream_key, dims, cuts, least, high):
    def one(axis_at, parts):
        steps = jax.random.uniform(jax.random.fold_in(jax.random.fold_in(stream_key, 6), axis_at), (parts,), jnp.float32, least / len(cuts), high / len(cuts))
        return jnp.repeat(jnp.exp(steps), dims[axis_at] // parts).reshape((-1,) + (1,) * (len(dims) - axis_at - 1))

    level = one(*cuts[0])
    for cut in cuts[1:]:
        level = level * one(*cut)
    return level


def bell_draw(key, extent, deviation, limit, cuts=(), kind=jnp.bfloat16):
    drawn = jax.random.normal(key, extent, jnp.float32) * deviation
    if len(cuts) > 0:
        drawn = block_levels(key, extent, cuts, -0.22, 0.18) * drawn
    return jnp.clip(drawn, min=-limit, max=limit).astype(kind)


def setup_inputs(seed: int = 0) -> dict:
    splits = jax.random.split(jax.random.key(seed), 8)
    transmission = draw_transmission(jax.random.fold_in(splits[7], 71), 0)
    probe = bell_draw(splits[1], (2, MODES, N, N), 0.25, 1.5, ((2, 4),))
    measured = jnp.clip(2.0 * jax.random.uniform(splits[2], (FRAMES, N, N), jnp.float32) ** block_levels(splits[2], (FRAMES, N, N), ((0, 8), (1, 4)), -0.2, 0.2), 0.0, 2.0)
    positions = draw_positions(jax.random.fold_in(splits[7], 71), 0)
    past_steps = draw_past_steps(jax.random.fold_in(splits[7], 71), 0)
    past_changes = draw_past_changes(jax.random.fold_in(splits[7], 71), 0)
    old_gradient = draw_old_gradient(jax.random.fold_in(splits[7], 71), 0)
    return dict(transmission=transmission, probe=probe, measured=measured, positions=positions, past_steps=past_steps, past_changes=past_changes, old_gradient=old_gradient)


TWO_PI = 2.0 * math.pi
CURVE_FLOOR = 0.25
TIKHONOV = 0.5
EPSILON = 1e-06

def dft_tables(count):
    index = jnp.arange(count, dtype=jnp.int32)
    phase = (index[:, None] * index[None, :] % count).astype(jnp.float32) * (TWO_PI / count)
    factor = 1.0 / math.sqrt(count)
    return ((jnp.cos(phase) * factor).astype(jnp.bfloat16), (-jnp.sin(phase) * factor).astype(jnp.bfloat16))

def chirp_table(count):
    index = jnp.arange(count, dtype=jnp.int32)
    wavenumber = (index + count // 2) % count - count // 2
    phase = (wavenumber * wavenumber % (4 * count)).astype(jnp.float32) * (TWO_PI / (4 * count))
    return (jnp.cos(phase), -jnp.sin(phase))

def rotate(real_part, imag_part, turn_real, turn_imag):
    return (real_part * turn_real - imag_part * turn_imag, real_part * turn_imag + imag_part * turn_real)

def narrow(pair):
    return jnp.stack([pair[0], pair[1]]).astype(jnp.bfloat16)

def right_product(field, matrix_real, matrix_imag):

    def single(left, right):
        return jnp.einsum('...k,kj->...j', left.astype(jnp.float32), right.astype(jnp.float32), precision=lax.Precision.HIGHEST)
    return (single(field[0], matrix_real) - single(field[1], matrix_imag), single(field[0], matrix_imag) + single(field[1], matrix_real))

def left_product(matrix_real, matrix_imag, field):

    def single(left, right):
        return jnp.einsum('jk,...kc->...jc', left.astype(jnp.float32), right.astype(jnp.float32), precision=lax.Precision.HIGHEST)
    return (single(matrix_real, field[0]) - single(matrix_imag, field[1]), single(matrix_real, field[1]) + single(matrix_imag, field[0]))

def inner(left, right):
    return jnp.sum(left * right)

def reference(transmission, probe, measured, positions, past_steps, past_changes, old_gradient):
    fwd_real, fwd_imag = dft_tables(N)
    inv_imag = -fwd_imag
    chirp_real, chirp_imag = chirp_table(N)
    tiles = transmission.astype(jnp.bfloat16).reshape(2, OBJ, N_REGION, OBJ)
    probe_wide = probe.astype(jnp.float32)
    anchor = jnp.zeros((), jnp.int32)

    def one_frame(total, inputs):
        target, offset, frame = inputs
        region = (frame // FR).astype(jnp.int32)
        corner = (anchor, offset[1].astype(jnp.int32), region, offset[0].astype(jnp.int32))
        window = jnp.swapaxes(lax.dynamic_slice(tiles, corner, (2, N, 1, N))[:, :, 0, :], 1, 2).astype(jnp.float32)
        wave = narrow(rotate(probe_wide[0], probe_wide[1], window[0], window[1]))
        section = narrow(rotate(*right_product(wave, fwd_real, fwd_imag), chirp_real, chirp_imag))
        spread = narrow(right_product(section, fwd_real, inv_imag))
        section = narrow(rotate(*left_product(fwd_real, fwd_imag, spread), chirp_real[:, None], chirp_imag[:, None]))
        far_field = narrow(left_product(fwd_real, inv_imag, section)).astype(jnp.float32)
        misfit = lax.optimization_barrier(jnp.sum(far_field[0] * far_field[0] + far_field[1] * far_field[1], axis=0)) - target
        weighted = (misfit * far_field).astype(jnp.bfloat16)
        section = narrow(rotate(*left_product(fwd_real, fwd_imag, weighted), chirp_real[:, None], -chirp_imag[:, None]))
        returned = narrow(left_product(fwd_real, inv_imag, section))
        section = narrow(rotate(*right_product(returned, fwd_real, fwd_imag), chirp_real, -chirp_imag))
        back_real, back_imag = right_product(section, fwd_real, inv_imag)
        grad_real = 4.0 * lax.optimization_barrier(jnp.sum(probe_wide[0] * back_real + probe_wide[1] * back_imag, axis=0))
        grad_imag = 4.0 * lax.optimization_barrier(jnp.sum(probe_wide[0] * back_imag - probe_wide[1] * back_real, axis=0))
        frame_grad = jnp.swapaxes(jnp.stack([grad_real, grad_imag]), 1, 2)
        before = lax.dynamic_slice(total, corner, (2, N, 1, N))
        total = lax.dynamic_update_slice(total, before + frame_grad[:, :, None, :], corner)
        return (total, None)
    frame_ids = jnp.arange(FRAMES, dtype=jnp.int32)
    total, leftover = lax.scan(one_frame, jnp.zeros((2, OBJ, N_REGION, OBJ), jnp.float32), (measured, positions, frame_ids))
    gradient = total.reshape(2, OBJ, OBJ_ALL) + TIKHONOV * transmission
    steps_list = [past_steps[index] for index in range(HIST)]
    changes = [past_changes[index] for index in range(HIST - 1)] + [gradient - old_gradient]
    weights = [1.0 / jnp.maximum(inner(steps_list[index], changes[index]), CURVE_FLOOR * inner(steps_list[index], steps_list[index])) for index in range(HIST)]
    direction = gradient
    alphas = [None] * HIST
    for index in reversed(range(HIST)):
        alphas[index] = weights[index] * inner(steps_list[index], direction)
        direction = direction - alphas[index] * changes[index]
    last = HIST - 1
    scale = jnp.maximum(inner(steps_list[last], changes[last]), CURVE_FLOOR * inner(steps_list[last], steps_list[last])) / (inner(changes[last], changes[last]) + EPSILON)
    direction = scale * direction
    for index in range(HIST):
        beta = weights[index] * inner(changes[index], direction)
        direction = direction + (alphas[index] - beta) * steps_list[index]
    return (transmission - direction, gradient)
```

```python
import functools
import math

import jax
import jax.numpy as jnp
import ml_dtypes
import numpy as np
from jax import lax
from jax.experimental import pallas as pl
from jax.experimental.pallas import tpu as pltpu
from jax.sharding import PartitionSpec as P

TWO_PI = 2.0 * math.pi
CURVE_FLOOR = 0.25
TIKHONOV = 0.5
EPSILON = 1e-06
BF = jnp.bfloat16
F32 = jnp.float32
AXES = ("region", "grp")
LANES = 128
MIB = 1 << 20
HIST = 4


def dft_tables(count):
    index = jnp.arange(count, dtype=jnp.int32)
    phase = (index[:, None] * index[None, :] % count).astype(jnp.float32) * (TWO_PI / count)
    factor = 1.0 / math.sqrt(count)
    return (
        (jnp.cos(phase) * factor).astype(jnp.bfloat16),
        (-jnp.sin(phase) * factor).astype(jnp.bfloat16),
    )


def chirp_table(count):
    index = jnp.arange(count, dtype=jnp.int32)
    wavenumber = (index + count // 2) % count - count // 2
    phase = (wavenumber * wavenumber % (4 * count)).astype(jnp.float32) * (TWO_PI / (4 * count))
    return (jnp.cos(phase), -jnp.sin(phase))


def rotate(real_part, imag_part, turn_real, turn_imag):
    return (
        real_part * turn_real - imag_part * turn_imag,
        real_part * turn_imag + imag_part * turn_real,
    )


def narrow(pair):
    return jnp.stack([pair[0], pair[1]]).astype(jnp.bfloat16)


def right_product(field, matrix_real, matrix_imag):

    def single(left, right):
        return jnp.einsum("...k,kj->...j", left, right, preferred_element_type=jnp.float32)

    return (
        single(field[0], matrix_real) - single(field[1], matrix_imag),
        single(field[0], matrix_imag) + single(field[1], matrix_real),
    )


def left_product(matrix_real, matrix_imag, field):

    def single(left, right):
        return jnp.einsum("jk,...kc->...jc", left, right, preferred_element_type=jnp.float32)

    return (
        single(matrix_real, field[0]) - single(matrix_imag, field[1]),
        single(matrix_real, field[1]) + single(matrix_imag, field[0]),
    )


def general(transmission, probe, measured, positions, past_steps, past_changes, old_gradient):
    member = lax.axis_index("grp")
    frame_len = probe.shape[3]
    rows_here = probe.shape[2]
    tile_len = transmission.shape[2]
    anchor = jnp.zeros((), jnp.int32)
    fwd_real, fwd_imag = dft_tables(frame_len)
    inv_imag = -fwd_imag
    chirp_real, chirp_imag = chirp_table(frame_len)
    probe_wide = probe.astype(jnp.float32)
    tile = lax.all_gather(transmission.astype(jnp.bfloat16), "grp", axis=1, tiled=True)
    frame = 0
    first_row = positions[frame, 0] + member * rows_here
    window = jnp.swapaxes(
        lax.dynamic_slice(
            tile, (anchor, positions[frame, 1], first_row), (2, frame_len, rows_here)
        ),
        1,
        2,
    ).astype(jnp.float32)
    wave = narrow(rotate(probe_wide[0], probe_wide[1], window[0], window[1]))
    section = narrow(rotate(*right_product(wave, fwd_real, fwd_imag), chirp_real, chirp_imag))
    spread = narrow(right_product(section, fwd_real, inv_imag))
    section = narrow(
        rotate(
            *left_product(
                fwd_real,
                fwd_imag,
                lax.all_to_all(spread, "grp", split_axis=3, concat_axis=2, tiled=True),
            ),
            chirp_real[:, None],
            chirp_imag[:, None]
        )
    )
    far_field = narrow(left_product(fwd_real, inv_imag, section))
    near_rows = lax.all_to_all(far_field, "grp", split_axis=2, concat_axis=3, tiled=True)
    field_wide = near_rows.astype(jnp.float32)
    misfit = (
        jnp.sum(field_wide[0] * field_wide[0] + field_wide[1] * field_wide[1], axis=0)
        - measured[frame]
    )
    weighted = (misfit * field_wide).astype(jnp.bfloat16)
    section = narrow(
        rotate(
            *left_product(
                fwd_real,
                fwd_imag,
                lax.all_to_all(weighted, "grp", split_axis=3, concat_axis=2, tiled=True),
            ),
            chirp_real[:, None],
            -chirp_imag[:, None]
        )
    )
    returned = narrow(left_product(fwd_real, inv_imag, section))
    section = narrow(
        rotate(
            *right_product(
                lax.all_to_all(returned, "grp", split_axis=2, concat_axis=3, tiled=True),
                fwd_real,
                fwd_imag,
            ),
            chirp_real,
            -chirp_imag
        )
    )
    back_wave = jnp.stack(right_product(section, fwd_real, inv_imag))
    grad_real = 4.0 * jnp.sum(probe_wide[0] * back_wave[0] + probe_wide[1] * back_wave[1], axis=0)
    grad_imag = 4.0 * jnp.sum(probe_wide[0] * back_wave[1] - probe_wide[1] * back_wave[0], axis=0)
    frame_grads = [jnp.stack([grad_real, grad_imag])]
    scattered = jnp.zeros((2, tile_len, tile_len), jnp.float32)
    frame = 0
    corner = (anchor, positions[frame, 1], positions[frame, 0] + member * rows_here)
    scattered = lax.dynamic_update_slice(scattered, jnp.swapaxes(frame_grads[frame], 1, 2), corner)
    data_grad = lax.psum_scatter(
        scattered.astype(jnp.bfloat16), "grp", scatter_dimension=1, tiled=True
    ).astype(jnp.float32)
    gradient = data_grad + TIKHONOV * transmission
    depth = past_steps.shape[0]
    last = depth - 1
    change_new = gradient - old_gradient
    steps_list = [past_steps[index] for index in range(depth)]
    changes = [past_changes[index] for index in range(depth - 1)] + [change_new]
    alphas = [None] * depth
    curvature, self_dots, change_norm = lax.psum(
        (
            jnp.stack([jnp.sum(steps_list[index] * changes[index]) for index in range(depth)]),
            jnp.sum(past_steps * past_steps, axis=(1, 2, 3)),
            jnp.sum(change_new * change_new),
        ),
        ("region", "grp"),
    )
    weights = [
        1.0 / jnp.maximum(curvature[index], CURVE_FLOOR * self_dots[index])
        for index in range(depth)
    ]
    direction = gradient
    for index in reversed(range(depth)):
        alphas[index] = weights[index] * lax.psum(
            jnp.sum(steps_list[index] * direction), ("region", "grp")
        )
        direction = direction - alphas[index] * changes[index]
    scale = jnp.maximum(curvature[last], CURVE_FLOOR * self_dots[last]) / (change_norm + EPSILON)
    direction = scale * direction
    for index in range(depth):
        beta = weights[index] * lax.psum(jnp.sum(changes[index] * direction), ("region", "grp"))
        direction = direction + (alphas[index] - beta) * steps_list[index]
    return (transmission - direction, gradient)


def propagators(count):
    index = np.arange(count, dtype=np.int64)
    phase = (index[:, None] * index[None, :] % count).astype(np.float32) * np.float32(TWO_PI / count)
    factor = np.float32(1.0 / math.sqrt(count))
    table = (np.cos(phase) * factor).astype(ml_dtypes.bfloat16).astype(np.float64) + 1j * (
        -np.sin(phase) * factor
    ).astype(ml_dtypes.bfloat16).astype(np.float64)
    wavenumber = (index + count // 2) % count - count // 2
    chirp = np.exp(-1j * (wavenumber * wavenumber % (4 * count)) * (TWO_PI / (4 * count)))
    folded = (table * chirp[None, :]) @ np.conj(table)
    real, imag = folded.real, folded.imag
    right = np.block([[real, imag], [-imag, real]]).astype(ml_dtypes.bfloat16)
    return right, np.ascontiguousarray(right.T)


def dot(left, right, dims=((1,), (0,))):
    return lax.dot_general(left, right, (dims, ((), ())), preferred_element_type=F32)


def shift_table(rows, columns, row_base, column_base):
    row = lax.broadcasted_iota(jnp.int32, (rows, columns), 0) + row_base
    column = lax.broadcasted_iota(jnp.int32, (rows, columns), 1) + column_base
    return jnp.where(row == column, 1.0, 0.0).astype(BF)


def cut_kernel(pos_ref, tile_ref, out_ref):
    tile_len, frame_len = tile_ref.shape[2], out_ref.shape[2]
    table = shift_table(tile_len, frame_len, 0, pos_ref[0, 0])
    for part in range(2):
        out_ref[part] = dot(tile_ref[part].astype(BF), table).astype(BF)


def forward_kernel(
    place_ref, own_ref, side_ref, mates_ref, mine_ref, q0_ref, q1_ref, q2_ref, q3a_ref, q3b_ref, measured_ref,
    right_ref, left_ref, far_ref, probe_ref, send_ref, keep_ref, tile, window, turned,
):
    column, core, place, line, half = (place_ref[index] for index in range(5))
    piece_len = own_ref.shape[1]
    chunk, frame_len = mine_ref.shape[2], mine_ref.shape[3]
    modes = mine_ref.shape[1]
    piece = 2 * core + half
    for step, ref in ((0, own_ref), (1, side_ref), (2, mates_ref.at[0]), (3, mates_ref.at[1])):
        base = pl.multiple_of(lax.bitwise_xor(piece, step) * piece_len, piece_len)
        for part in range(2):
            tile[part, pl.ds(base, piece_len), :] = ref[part]
    table = shift_table(tile.shape[1], frame_len, 0, column)
    for part in range(2):
        window[part] = dot(tile[part], table, ((0,), (0,))).astype(BF)

    def rows_of(step):
        return pl.ds(pl.multiple_of(lax.bitwise_xor(place, step) * chunk, chunk), chunk)

    for part in range(2):
        for mode in range(modes):
            probe_ref[part, mode, rows_of(0), :] = mine_ref[part, mode]
    cut = q3a_ref.shape[0]
    for turn, ref in ((0, q0_ref), (1, q1_ref), (2, q2_ref), (3, None)):
        combo = lax.bitwise_xor(line, turn)
        part, mode = lax.rem(combo, 2), lax.div(combo, 2)
        for step in range(1, 4):
            start = (step - 1) * chunk
            if ref is not None:
                value = ref[start : start + chunk]
            elif start + chunk <= cut:
                value = q3a_ref[start : start + chunk]
            elif start >= cut:
                value = q3b_ref[start - cut : start - cut + chunk]
            else:
                value = jnp.concatenate([q3a_ref[start:cut], q3b_ref[: start + chunk - cut]], axis=0)
            probe_ref[part, mode, rows_of(step), :] = value

    block = frame_len // 2
    for mode in range(modes):

        @pl.loop(0, 2)
        def _(index):
            rows = pl.ds(pl.multiple_of(index * block, block), block)
            low_rows = pl.ds(pl.multiple_of(index * block + frame_len, block), block)
            pr, pi = probe_ref[0, mode, rows, :].astype(F32), probe_ref[1, mode, rows, :].astype(F32)
            wr, wi = window[0, rows, :].astype(F32), window[1, rows, :].astype(F32)
            wave = jnp.concatenate([(pr * wr - pi * wi).astype(BF), (pr * wi + pi * wr).astype(BF)], axis=1)
            result = dot(wave, right_ref[...]).astype(BF)
            turned[mode, rows, :] = result[:, :frame_len]
            turned[mode, low_rows, :] = result[:, frame_len:]

    for out, base in ((send_ref, (1 - core) * block), (keep_ref, core * block)):
        rows = pl.ds(pl.multiple_of(base, block), block)
        low_rows = pl.ds(pl.multiple_of(base + frame_len, block), block)
        total = jnp.zeros((block, frame_len), F32)
        for mode in range(modes):
            for part, part_rows in ((0, rows), (1, low_rows)):
                value = dot(left_ref[part_rows, :], turned[mode]).astype(BF)
                far_ref[mode, part, rows, :] = value
                wide = value.astype(F32)
                total = total + wide * wide
        out[...] = total
    own_rows = pl.ds(pl.multiple_of(half * chunk, chunk), chunk)
    keep_ref[own_rows, :] = keep_ref[own_rows, :] - measured_ref[...]


def backward_kernel(
    place_ref, far_ref, probe_ref, mine_ref, mates_ref, right_ref, left_ref,
    send_ref, side_ref, keep_ref, misfit, weighted, turned, grad,
):
    column, core, half = place_ref[0], place_ref[1], place_ref[4]
    modes, frame_len = far_ref.shape[0], far_ref.shape[3]
    block = frame_len // 2
    piece_len = keep_ref.shape[1]
    misfit[pl.ds(pl.multiple_of(core * block, block), block), :] = mine_ref[...]
    misfit[pl.ds(pl.multiple_of((1 - core) * block, block), block), :] = mates_ref[...]
    for mode in range(modes):
        for part in range(2):
            weighted[mode, part * frame_len : (part + 1) * frame_len, :] = (
                misfit[...] * far_ref[mode, part].astype(F32)
            ).astype(BF)
        for index in range(2):
            rows = slice(index * block, (index + 1) * block)
            for part in range(2):
                value = dot(right_ref[part * frame_len + index * block : part * frame_len + (index + 1) * block, :], weighted[mode])
                turned[mode, rows, part * frame_len : (part + 1) * frame_len] = value.astype(BF)

    @pl.loop(0, 2)
    def _(index):
        rows = pl.ds(pl.multiple_of(index * block, block), block)
        real, imag = jnp.zeros((block, frame_len), F32), jnp.zeros((block, frame_len), F32)
        for mode in range(modes):
            back = dot(turned[mode, rows, :], left_ref[...])
            br, bi = back[:, :frame_len], back[:, frame_len:]
            pr, pi = probe_ref[0, mode, rows, :].astype(F32), probe_ref[1, mode, rows, :].astype(F32)
            real = real + (pr * br + pi * bi)
            imag = imag + (pr * bi - pi * br)
        grad[0, rows, :] = (4.0 * real).astype(BF)
        grad[1, rows, :] = (4.0 * imag).astype(BF)

    for target, pair in ((0, 1 - core), (1, core)):
        for flip in range(2):
            base = (2 * pair + lax.bitwise_xor(half, 1 - flip)) * piece_len
            table = shift_table(piece_len, frame_len, base, column)
            for part in range(2):
                value = dot(table, grad[part], ((1,), (1,))).astype(BF)
                if target == 0:
                    send_ref[flip, part] = value
                elif flip == 0:
                    side_ref[part] = value
                else:
                    keep_ref[part] = value


PAIRS = [("sy", i, j) for j in range(HIST - 1) for i in range(HIST)]
PAIRS += [("ss", i, i) for i in range(HIST)]
PAIRS += [("yy", i, j) for j in range(HIST - 1) for i in range(j + 1)]
OLD_PAIRS = len(PAIRS)
PAIRS += [("sy", i, HIST - 1) for i in range(HIST)]
PAIRS += [("yy", i, HIST - 1) for i in range(HIST)]
PAIRS += [("sg", i, i) for i in range(HIST)]
PAIRS += [("yg", i, i) for i in range(HIST)]
SLOT = {pair: index for index, pair in enumerate(PAIRS)}


def folded(value):
    parts, rows, columns = value.shape
    total = jnp.sum(value.reshape(parts * rows // 8, 8, columns), axis=0)
    return sum(total[:, start : start + LANES] for start in range(0, columns, LANES))


def add_products(sums, first, slots, vectors):
    for slot, pair in slots:
        kind, i, j = pair
        left = vectors[kind[0]][i]
        right = vectors["g"][0] if kind[1] == "g" else vectors[kind[1]][j]
        value = folded(left * right)
        sums[slot] = jnp.where(first, value, sums[slot] + value)


def lane_row(sums, count):
    rows = [jnp.sum(sums[slot], axis=0, keepdims=True) for slot in range(count)]
    square = jnp.concatenate(rows + [jnp.zeros((LANES - count, LANES), F32)], axis=0)
    return jnp.sum(square.T, axis=0, keepdims=True)


def old_kernel(steps_ref, changes_ref, out_ref, sums):
    step = pl.program_id(0)
    vectors = {
        "s": [steps_ref[index] for index in range(HIST)],
        "y": [changes_ref[index] for index in range(HIST - 1)],
    }
    add_products(sums, step == 0, list(enumerate(PAIRS[:OLD_PAIRS])), vectors)

    @pl.when(step == pl.num_programs(0) - 1)
    def _():
        out_ref[...] = lane_row(sums, OLD_PAIRS)


def gradient_kernel(
    pos_ref, data_ref, transmission_ref, old_ref, steps_ref, changes_ref, row_ref, gradient_ref, out_ref, sums
):
    step = pl.program_id(0)
    table = shift_table(data_ref.shape[2], transmission_ref.shape[2], pos_ref[0, 0], 0)
    parts = [
        dot(data_ref[part], table) + TIKHONOV * transmission_ref[part] for part in range(2)
    ]
    gradient = jnp.stack(parts)
    gradient_ref[...] = gradient
    vectors = {
        "s": [steps_ref[index] for index in range(HIST)],
        "y": [changes_ref[index] for index in range(HIST - 1)] + [gradient - old_ref[...]],
        "g": [gradient],
    }
    slots = [(index, pair) for index, pair in enumerate(PAIRS[OLD_PAIRS:])]
    add_products(sums, step == 0, slots, vectors)

    @pl.when(step == pl.num_programs(0) - 1)
    def _():
        fresh = pltpu.roll(lane_row(sums, len(PAIRS) - OLD_PAIRS), OLD_PAIRS, 1)
        out_ref[...] = jnp.broadcast_to(fresh + row_ref[...], out_ref.shape)


def update_kernel(
    rows_ref, transmission_ref, gradient_ref, old_ref, steps_ref, changes_ref, out_ref, factors
):
    width = factors.shape[1]

    @pl.when(pl.program_id(0) == 0)
    def _():
        row = jnp.sum(rows_ref[...], axis=0, keepdims=True)
        lane = lax.broadcasted_iota(jnp.int32, row.shape, 1)

        def get(kind, i, j):
            if kind == "yy" and i > j:
                i, j = j, i
            picked = jnp.where(lane == SLOT[(kind, i, j)], row, 0.0)
            return jnp.broadcast_to(jnp.sum(picked, axis=1, keepdims=True), row.shape)

        last = HIST - 1
        floors = [
            jnp.maximum(get("sy", index, index), CURVE_FLOOR * get("ss", index, index)) for index in range(HIST)
        ]
        weights = [1.0 / floor for floor in floors]
        alphas = [None] * HIST
        for index in reversed(range(HIST)):
            value = get("sg", index, index)
            for later in range(index + 1, HIST):
                value = value - alphas[later] * get("sy", index, later)
            alphas[index] = weights[index] * value
        scale = floors[last] / (get("yy", last, last) + EPSILON)
        moves = []
        for index in range(HIST):
            value = get("yg", index, index)
            for other in range(HIST):
                value = value - alphas[other] * get("yy", index, other)
            value = scale * value
            for before in range(index):
                value = value + moves[before] * get("sy", before, index)
            moves.append(alphas[index] - weights[index] * value)
        table = [scale] + [-scale * alpha for alpha in alphas] + moves
        for index, value in enumerate(table):
            factors[index : index + 1, :] = jnp.concatenate([value] * (width // LANES), axis=1)

    def factor(index):
        return factors[index : index + 1, :]

    for part in range(2):
        gradient = gradient_ref[part]
        total = factor(0) * gradient + factor(HIST) * (gradient - old_ref[part])
        for index in range(HIST - 1):
            total = total + factor(1 + index) * changes_ref[index, part]
        for index in range(HIST):
            total = total + factor(1 + HIST + index) * steps_ref[index, part]
        out_ref[part] = transmission_ref[part] - total


def call(body, outs, scratch=(), limit=48, smem=(), count=0, cost=None):
    specs = [
        pl.BlockSpec(memory_space=pltpu.SMEM if index in smem else pltpu.VMEM) for index in range(count)
    ]
    return pl.pallas_call(
        body,
        out_shape=outs,
        in_specs=specs,
        out_specs=jax.tree.map(lambda _: pl.BlockSpec(memory_space=pltpu.VMEM), outs),
        scratch_shapes=list(scratch),
        compiler_params=pltpu.CompilerParams(vmem_limit_bytes=limit * MIB),
        cost_estimate=cost,
    )


def cost(flops, moved):
    return pl.CostEstimate(flops=int(flops), bytes_accessed=int(moved), transcendentals=0)


def routes(mesh, target):
    regions, members = mesh.shape["region"], mesh.shape["grp"]
    pairs = []
    for region in range(regions):
        for member in range(members):
            to_region, to_member = target(region, member)
            pairs.append((region * members + member, to_region * members + to_member))
    return pairs


def home(region, member):
    if region % 2 == member // 2:
        return region, member
    return region ^ 1, member ^ 2


def fast(mesh, transmission, probe, measured, positions, past_steps, past_changes, old_gradient):
    def send(value, target):
        return lax.ppermute(value, AXES, routes(mesh, target))

    near = lambda region, member: (region, member ^ 1)
    far = lambda region, member: (region, member ^ 2)
    cross = lambda region, member: (region, member ^ 3)
    mate = lambda region, member: (region ^ 1, member)
    along_x = lambda region, member: (region ^ 2, member)
    along_y = lambda region, member: (region ^ 4, member)

    region, member = lax.axis_index("region"), lax.axis_index("grp")
    core, half, line = region % 2, member % 2, (region // 2) % 4
    chunk, frame_len = probe.shape[2], probe.shape[3]
    piece_len, tile_len = transmission.shape[1], transmission.shape[2]
    size = jax.ShapeDtypeStruct

    part, which = line % 2, line // 2
    base = 4 * core + 2 * half
    other_base = 4 * core + 2 * (1 - half)

    def block(mode):
        return lax.dynamic_slice(probe, (part, mode, 0, 0), (1, 1, chunk, frame_len)).reshape(chunk, frame_len)

    same_block, flip_block = block(base + which), block(other_base + which)
    fetched = [send(flip_block, near), send(same_block, far), send(flip_block, cross)]
    mine = lax.dynamic_slice(probe, (0, base, 0, 0), (2, 2, chunk, frame_len))
    q0 = jnp.concatenate(fetched, axis=0)
    q1, q2 = send(q0, along_x), send(q0, along_y)
    cut = q0.shape[0] // 2
    q3a, q3b = send(q2[:cut], along_x), send(q1[cut:], along_y)

    piece = call(cut_kernel, size((2, piece_len, frame_len), BF), count=2, smem=(0,), limit=16)(
        positions, transmission
    )
    own = send(piece, home)
    side = send(own, near)
    mates = send(jnp.stack([own, side]), mate)
    target = send(measured[0], home)
    mate_positions = send(positions, mate)
    column = jnp.where(core == member // 2, positions[0, 1], mate_positions[0, 1])
    place = jnp.stack([column, core, member, line, half]).astype(jnp.int32)

    right, left = (jnp.asarray(table) for table in propagators(frame_len))
    half_len = frame_len // 2
    flops = 2 * 2 * 2 * frame_len * 4 * frame_len * frame_len
    field = size((2, 2, frame_len, frame_len), BF)
    partial = size((half_len, frame_len), F32)
    far_field, whole_probe, sent, kept = call(
        forward_kernel,
        (field, field, partial, partial),
        [
            pltpu.VMEM((2, tile_len, frame_len), BF),
            pltpu.VMEM((2, frame_len, frame_len), BF),
            pltpu.VMEM((2, 2 * frame_len, frame_len), BF),
        ],
        count=13,
        smem=(0,),
        cost=cost(flops, 16 * MIB),
    )(place, own, side, mates, mine, q0, q1, q2, q3a, q3b, target, right, left)

    chip = kept + send(sent, mate)
    misfit = chip + send(chip.astype(BF), near).astype(F32)
    mates_misfit = send(misfit, mate)

    piece_shape = size((2, piece_len, frame_len), BF)
    sent, kept_side, kept = call(
        backward_kernel,
        (size((2, 2, piece_len, frame_len), BF), piece_shape, piece_shape),
        [
            pltpu.VMEM((frame_len, frame_len), F32),
            pltpu.VMEM((2, 2 * frame_len, frame_len), BF),
            pltpu.VMEM((2, frame_len, 2 * frame_len), BF),
            pltpu.VMEM((2, frame_len, frame_len), BF),
        ],
        count=7,
        smem=(0,),
        cost=cost(flops, 12 * MIB),
    )(place, far_field, whole_probe, misfit, mates_misfit, right, left)
    met = send(sent, mate)
    add = lambda a, b: (a.astype(F32) + b.astype(F32)).astype(BF)
    data = add(add(kept, met[1]), send(add(kept_side, met[0]), near))
    data = send(data, home)

    steps = 5
    rows = piece_len // steps
    whole = lambda *dims: pl.BlockSpec(dims, lambda index: (0,) * len(dims))
    vector = pl.BlockSpec((2, rows, tile_len), lambda index: (0, index, 0))
    window = pl.BlockSpec((2, rows, frame_len), lambda index: (0, index, 0))
    history = lambda count: pl.BlockSpec((count, 2, rows, tile_len), lambda index: (0, 0, index, 0))
    params = pltpu.CompilerParams(vmem_limit_bytes=32 * MIB)
    moved = 4 * 2 * piece_len * tile_len
    old_row = pl.pallas_call(
        old_kernel,
        out_shape=size((1, LANES), F32),
        grid=(steps,),
        in_specs=[history(HIST), history(HIST - 1)],
        out_specs=whole(1, LANES),
        scratch_shapes=[pltpu.VMEM((OLD_PAIRS, 8, LANES), F32)],
        compiler_params=params,
        cost_estimate=cost(22 * moved, 7 * moved),
    )(past_steps, past_changes)
    devices = mesh.shape["region"] * mesh.shape["grp"]
    gradient, row = pl.pallas_call(
        gradient_kernel,
        out_shape=(size(transmission.shape, F32), size((devices, LANES), F32)),
        grid=(steps,),
        in_specs=[
            pl.BlockSpec(memory_space=pltpu.SMEM),
            window,
            vector,
            vector,
            history(HIST),
            history(HIST - 1),
            whole(1, LANES),
        ],
        out_specs=(vector, whole(devices, LANES)),
        scratch_shapes=[pltpu.VMEM((len(PAIRS) - OLD_PAIRS, 8, LANES), F32)],
        compiler_params=params,
        cost_estimate=cost(16 * moved, 10 * moved),
    )(positions, data, transmission, old_gradient, past_steps, past_changes, old_row)
    all_rows = lax.all_to_all(
        row.reshape(devices, 1, LANES), AXES, split_axis=0, concat_axis=0, tiled=True
    ).reshape(devices, LANES)
    updated = pl.pallas_call(
        update_kernel,
        out_shape=size(transmission.shape, F32),
        grid=(steps,),
        in_specs=[whole(devices, LANES), vector, vector, vector, history(HIST), history(HIST - 1)],
        out_specs=vector,
        scratch_shapes=[pltpu.VMEM((16, tile_len), F32)],
        compiler_params=params,
        cost_estimate=cost(10 * moved, 11 * moved),
    )(all_rows, transmission, gradient, old_gradient, past_steps, past_changes)
    return (updated, gradient)


def solution(mesh):
    split = mesh.shape["grp"] == 4 and mesh.shape["region"] == 8

    def shards(*args):
        probe, positions, past_steps = args[1], args[3], args[4]
        sized = probe.shape[1] == 8 and positions.shape[0] == 1 and past_steps.shape[0] == HIST
        if split and sized:
            return fast(mesh, *args)
        return general(*args)

    return jax.shard_map(
        shards,
        mesh=mesh,
        in_specs=(
            P(None, "grp", "region"),
            P(None, None, "grp", None),
            P("region", "grp", None),
            P("region", None),
            P(None, None, "grp", "region"),
            P(None, None, "grp", "region"),
            P(None, "grp", "region"),
        ),
        out_specs=(P(None, "grp", "region"), P(None, "grp", "region")),
        check_vma=False,
    )
```

```python
import math

import jax
import jax.numpy as jnp
import ml_dtypes
import numpy as np
from jax import lax
from jax.experimental import pallas as pl
from jax.experimental.pallas import tpu as pltpu
from jax.sharding import PartitionSpec as P

TWO_PI = 2.0 * math.pi
CURVE_FLOOR = 0.25
TIKHONOV = 0.5
EPSILON = 1e-06
BF = jnp.bfloat16
F32 = jnp.float32
AXES = ("region", "grp")
LANES = 128
MIB = 1 << 20
HIST = 4


def dft_tables(count):
    index = jnp.arange(count, dtype=jnp.int32)
    phase = (index[:, None] * index[None, :] % count).astype(jnp.float32) * (TWO_PI / count)
    factor = 1.0 / math.sqrt(count)
    return (
        (jnp.cos(phase) * factor).astype(jnp.bfloat16),
        (-jnp.sin(phase) * factor).astype(jnp.bfloat16),
    )


def chirp_table(count):
    index = jnp.arange(count, dtype=jnp.int32)
    wavenumber = (index + count // 2) % count - count // 2
    phase = (wavenumber * wavenumber % (4 * count)).astype(jnp.float32) * (TWO_PI / (4 * count))
    return (jnp.cos(phase), -jnp.sin(phase))


def rotate(real_part, imag_part, turn_real, turn_imag):
    return (
        real_part * turn_real - imag_part * turn_imag,
        real_part * turn_imag + imag_part * turn_real,
    )


def narrow(pair):
    return jnp.stack([pair[0], pair[1]]).astype(jnp.bfloat16)


def right_product(field, matrix_real, matrix_imag):

    def single(left, right):
        return jnp.einsum("...k,kj->...j", left, right, preferred_element_type=jnp.float32)

    return (
        single(field[0], matrix_real) - single(field[1], matrix_imag),
        single(field[0], matrix_imag) + single(field[1], matrix_real),
    )


def left_product(matrix_real, matrix_imag, field):

    def single(left, right):
        return jnp.einsum("jk,...kc->...jc", left, right, preferred_element_type=jnp.float32)

    return (
        single(matrix_real, field[0]) - single(matrix_imag, field[1]),
        single(matrix_real, field[1]) + single(matrix_imag, field[0]),
    )


def general(transmission, probe, measured, positions, past_steps, past_changes, old_gradient):
    member = lax.axis_index("grp")
    frame_len = probe.shape[3]
    rows_here = probe.shape[2]
    tile_len = transmission.shape[2]
    anchor = jnp.zeros((), jnp.int32)
    fwd_real, fwd_imag = dft_tables(frame_len)
    inv_imag = -fwd_imag
    chirp_real, chirp_imag = chirp_table(frame_len)
    probe_wide = probe.astype(jnp.float32)
    tile = lax.all_gather(transmission.astype(jnp.bfloat16), "grp", axis=1, tiled=True)
    frame = 0
    first_row = positions[frame, 0] + member * rows_here
    window = jnp.swapaxes(
        lax.dynamic_slice(
            tile, (anchor, positions[frame, 1], first_row), (2, frame_len, rows_here)
        ),
        1,
        2,
    ).astype(jnp.float32)
    wave = narrow(rotate(probe_wide[0], probe_wide[1], window[0], window[1]))
    section = narrow(rotate(*right_product(wave, fwd_real, fwd_imag), chirp_real, chirp_imag))
    spread = narrow(right_product(section, fwd_real, inv_imag))
    section = narrow(
        rotate(
            *left_product(
                fwd_real,
                fwd_imag,
                lax.all_to_all(spread, "grp", split_axis=3, concat_axis=2, tiled=True),
            ),
            chirp_real[:, None],
            chirp_imag[:, None]
        )
    )
    far_field = narrow(left_product(fwd_real, inv_imag, section))
    near_rows = lax.all_to_all(far_field, "grp", split_axis=2, concat_axis=3, tiled=True)
    field_wide = near_rows.astype(jnp.float32)
    misfit = (
        jnp.sum(field_wide[0] * field_wide[0] + field_wide[1] * field_wide[1], axis=0)
        - measured[frame]
    )
    weighted = (misfit * field_wide).astype(jnp.bfloat16)
    section = narrow(
        rotate(
            *left_product(
                fwd_real,
                fwd_imag,
                lax.all_to_all(weighted, "grp", split_axis=3, concat_axis=2, tiled=True),
            ),
            chirp_real[:, None],
            -chirp_imag[:, None]
        )
    )
    returned = narrow(left_product(fwd_real, inv_imag, section))
    section = narrow(
        rotate(
            *right_product(
                lax.all_to_all(returned, "grp", split_axis=2, concat_axis=3, tiled=True),
                fwd_real,
                fwd_imag,
            ),
            chirp_real,
            -chirp_imag
        )
    )
    back_wave = jnp.stack(right_product(section, fwd_real, inv_imag))
    grad_real = 4.0 * jnp.sum(probe_wide[0] * back_wave[0] + probe_wide[1] * back_wave[1], axis=0)
    grad_imag = 4.0 * jnp.sum(probe_wide[0] * back_wave[1] - probe_wide[1] * back_wave[0], axis=0)
    frame_grads = [jnp.stack([grad_real, grad_imag])]
    scattered = jnp.zeros((2, tile_len, tile_len), jnp.float32)
    frame = 0
    corner = (anchor, positions[frame, 1], positions[frame, 0] + member * rows_here)
    scattered = lax.dynamic_update_slice(scattered, jnp.swapaxes(frame_grads[frame], 1, 2), corner)
    data_grad = lax.psum_scatter(
        scattered.astype(jnp.bfloat16), "grp", scatter_dimension=1, tiled=True
    ).astype(jnp.float32)
    gradient = data_grad + TIKHONOV * transmission
    depth = past_steps.shape[0]
    last = depth - 1
    change_new = gradient - old_gradient
    steps_list = [past_steps[index] for index in range(depth)]
    changes = [past_changes[index] for index in range(depth - 1)] + [change_new]
    alphas = [None] * depth
    curvature, self_dots, change_norm = lax.psum(
        (
            jnp.stack([jnp.sum(steps_list[index] * changes[index]) for index in range(depth)]),
            jnp.sum(past_steps * past_steps, axis=(1, 2, 3)),
            jnp.sum(change_new * change_new),
        ),
        ("region", "grp"),
    )
    weights = [
        1.0 / jnp.maximum(curvature[index], CURVE_FLOOR * self_dots[index])
        for index in range(depth)
    ]
    direction = gradient
    for index in reversed(range(depth)):
        alphas[index] = weights[index] * lax.psum(
            jnp.sum(steps_list[index] * direction), ("region", "grp")
        )
        direction = direction - alphas[index] * changes[index]
    scale = jnp.maximum(curvature[last], CURVE_FLOOR * self_dots[last]) / (change_norm + EPSILON)
    direction = scale * direction
    for index in range(depth):
        beta = weights[index] * lax.psum(jnp.sum(changes[index] * direction), ("region", "grp"))
        direction = direction + (alphas[index] - beta) * steps_list[index]
    return (transmission - direction, gradient)


def propagator(count):
    index = np.arange(count, dtype=np.int64)
    phase = (index[:, None] * index[None, :] % count).astype(np.float32) * np.float32(TWO_PI / count)
    factor = np.float32(1.0 / math.sqrt(count))
    table = (np.cos(phase) * factor).astype(ml_dtypes.bfloat16).astype(np.float64) + 1j * (
        -np.sin(phase) * factor
    ).astype(ml_dtypes.bfloat16).astype(np.float64)
    wavenumber = (index + count // 2) % count - count // 2
    chirp = np.exp(-1j * (wavenumber * wavenumber % (4 * count)) * (TWO_PI / (4 * count)))
    folded = (table * chirp[None, :]) @ np.conj(table)
    folded = 0.5 * (folded + folded.T)
    real, imag = folded.real, folded.imag
    return np.block([[real, imag], [-imag, real]]).astype(ml_dtypes.bfloat16)


def dot(left, right, dims=((1,), (0,))):
    return lax.dot_general(left, right, (dims, ((), ())), preferred_element_type=F32)


def shift_table(rows, columns, row_base, column_base):
    row = lax.broadcasted_iota(jnp.int32, (rows, columns), 0) + row_base
    column = lax.broadcasted_iota(jnp.int32, (rows, columns), 1) + column_base
    return jnp.where(row == column, 1.0, 0.0).astype(BF)


def cut_kernel(pos_ref, tile_ref, out_ref):
    tile_len, frame_len = tile_ref.shape[2], out_ref.shape[2]
    table = shift_table(tile_len, frame_len, 0, pos_ref[0, 0])
    for part in range(2):
        out_ref[part] = dot(tile_ref[part].astype(BF), table).astype(BF)


def probe_kernel(place_ref, all_ref, q0_ref, q1_ref, q2_ref, q3a_ref, q3b_ref, probe_ref, sem):
    core, place, line, half = (place_ref[index] for index in range(4))
    chunk = all_ref.shape[2]

    def rows_of(step):
        return pl.ds(pl.multiple_of(lax.bitwise_xor(place, step) * chunk, chunk), chunk)

    copies = [
        pltpu.make_async_copy(
            all_ref.at[part, 4 * core + 2 * half + mode], probe_ref.at[part, mode, rows_of(0), :], sem.at[part, mode]
        )
        for part in range(2)
        for mode in range(2)
    ]
    for copy in copies:
        copy.start()
    cut = q3a_ref.shape[0]
    for turn, ref in ((0, q0_ref), (1, q1_ref), (2, q2_ref), (3, None)):
        combo = lax.bitwise_xor(line, turn)
        part, mode = lax.rem(combo, 2), lax.div(combo, 2)
        for step in range(1, 4):
            start = (step - 1) * chunk
            if ref is not None:
                value = ref[start : start + chunk]
            elif start + chunk <= cut:
                value = q3a_ref[start : start + chunk]
            elif start >= cut:
                value = q3b_ref[start - cut : start - cut + chunk]
            else:
                value = jnp.concatenate([q3a_ref[start:cut], q3b_ref[: start + chunk - cut]], axis=0)
            probe_ref[part, mode, rows_of(step), :] = value
    for copy in copies:
        copy.wait()


def forward_kernel(
    place_ref, pos_ref, mate_pos_ref, own_ref, side_ref, mate_own_ref, mate_side_ref, probe_ref, measured_ref,
    right_ref, far_ref, send_ref, keep_ref, tile, window_ref, wave, turned, total,
):
    core, half = place_ref[0], place_ref[3]
    chunk, frame_len = measured_ref.shape
    piece_len = own_ref.shape[1]
    piece = 2 * core + half
    for step, ref in enumerate((own_ref, side_ref, mate_own_ref, mate_side_ref)):
        base = pl.multiple_of(lax.bitwise_xor(piece, step) * piece_len, piece_len)
        for part in range(2):
            tile[part, pl.ds(base, piece_len), :] = ref[part]
    column = jnp.where(place_ref[4] == 1, pos_ref[0, 1], mate_pos_ref[0, 1])
    table = shift_table(tile.shape[1], frame_len, 0, column)
    for part in range(2):
        window_ref[part] = dot(tile[part], table, ((0,), (0,))).astype(BF)

    block = frame_len // 2
    for mode in range(2):
        rows = slice(mode * frame_len, (mode + 1) * frame_len)
        pr, pi = probe_ref[0, mode].astype(F32), probe_ref[1, mode].astype(F32)
        wr, wi = window_ref[0].astype(F32), window_ref[1].astype(F32)
        wave[rows, :frame_len] = (pr * wr - pi * wi).astype(BF)
        wave[rows, frame_len:] = (pr * wi + pi * wr).astype(BF)
    for part in range(2):
        for cell in range(2):
            start = part * frame_len + cell * block
            result = dot(wave[...], right_ref[:, start : start + block])
            result = (result if part == 0 else -result).astype(BF)
            for mode in range(2):
                columns = slice(mode * frame_len + cell * block, mode * frame_len + (cell + 1) * block)
                turned[part * frame_len : (part + 1) * frame_len, columns] = result[
                    mode * frame_len : (mode + 1) * frame_len
                ]
    for mode in range(2):
        for cell in range(2):
            start = mode * frame_len + cell * block
            columns = slice(cell * block, (cell + 1) * block)
            result = dot(right_ref[...], turned[:, start : start + block])
            real, imag = result[:frame_len].astype(BF), (-result[frame_len:]).astype(BF)
            far_ref[mode, 0, :, columns] = real
            far_ref[mode, 1, :, columns] = imag
            real, imag = real.astype(F32), imag.astype(F32)
            power = real * real + imag * imag
            if mode == 0:
                total[:, columns] = power
            else:
                total[:, columns] = total[:, columns] + power
    send_ref[...] = total[pl.ds(pl.multiple_of((1 - core) * block, block), block), :]
    keep_ref[...] = total[pl.ds(pl.multiple_of(core * block, block), block), :]
    own_rows = pl.ds(pl.multiple_of(half * chunk, chunk), chunk)
    keep_ref[own_rows, :] = keep_ref[own_rows, :] - measured_ref[...].astype(F32)


def backward_kernel(
    place_ref, pos_ref, mate_pos_ref, far_ref, probe_ref, mine_ref, mates_ref, right_ref,
    send_ref, side_ref, keep_ref, misfit, weighted, turned, grad, table,
):
    core, half = place_ref[0], place_ref[3]
    column = jnp.where(place_ref[4] == 1, pos_ref[0, 1], mate_pos_ref[0, 1])
    frame_len = far_ref.shape[3]
    block = frame_len // 2
    piece_len = keep_ref.shape[1]
    misfit[pl.ds(pl.multiple_of(core * block, block), block), :] = mine_ref[...]
    misfit[pl.ds(pl.multiple_of((1 - core) * block, block), block), :] = mates_ref[...]
    for mode in range(2):
        for part in range(2):
            weighted[part * frame_len : (part + 1) * frame_len, mode * frame_len : (mode + 1) * frame_len] = (
                misfit[...] * far_ref[mode, part].astype(F32)
            ).astype(BF)
    for mode in range(2):
        for cell in range(2):
            start = mode * frame_len + cell * block
            result = dot(right_ref[...], weighted[:, start : start + block])
            for part in range(2):
                columns = slice(part * frame_len + cell * block, part * frame_len + (cell + 1) * block)
                value = result[part * frame_len : (part + 1) * frame_len]
                turned[mode * frame_len : (mode + 1) * frame_len, columns] = (
                    value if part == 0 else -value
                ).astype(BF)
    for cell in range(2):
        columns = slice(cell * block, (cell + 1) * block)
        back = [
            dot(turned[...], right_ref[:, part * frame_len + cell * block : part * frame_len + (cell + 1) * block])
            for part in range(2)
        ]
        real, imag = 0.0, 0.0
        for mode in range(2):
            br, bi = (value[mode * frame_len : (mode + 1) * frame_len] for value in back)
            pr, pi = probe_ref[0, mode, :, columns].astype(F32), probe_ref[1, mode, :, columns].astype(F32)
            real = real + (pr * br - pi * bi)
            imag = imag + (pr * bi + pi * br)
        grad[0, :, columns] = (4.0 * real).astype(BF)
        grad[1, :, columns] = (-4.0 * imag).astype(BF)

    slots = [(1 - core, 1), (1 - core, 0), (core, 1), (core, 0)]
    for index, (pair, flip) in enumerate(slots):
        base = (2 * pair + lax.bitwise_xor(half, flip)) * piece_len
        table[index * piece_len : (index + 1) * piece_len, :] = shift_table(piece_len, frame_len, base, column)
    for part in range(2):
        value = dot(table[...], grad[part], ((1,), (1,))).astype(BF)
        send_ref[0, part] = value[:piece_len]
        send_ref[1, part] = value[piece_len : 2 * piece_len]
        side_ref[part] = value[2 * piece_len : 3 * piece_len]
        keep_ref[part] = value[3 * piece_len :]


PAIRS = [("sy", i, j) for j in range(HIST - 1) for i in range(HIST)]
PAIRS += [("ss", i, i) for i in range(HIST)]
PAIRS += [("yy", i, j) for j in range(HIST - 1) for i in range(j + 1)]
OLD_PAIRS = len(PAIRS)
PAIRS += [("sy", i, HIST - 1) for i in range(HIST)]
PAIRS += [("yy", i, HIST - 1) for i in range(HIST)]
PAIRS += [("sg", i, i) for i in range(HIST)]
PAIRS += [("yg", i, i) for i in range(HIST)]
SLOT = {pair: index for index, pair in enumerate(PAIRS)}


def folded(value):
    parts, rows, columns = value.shape
    total = jnp.sum(value.reshape(parts * rows // 8, 8, columns), axis=0)
    return sum(total[:, start : start + LANES] for start in range(0, columns, LANES))


def add_products(sums, first, slots, vectors):
    for slot, pair in slots:
        kind, i, j = pair
        left = vectors[kind[0]][i]
        right = vectors["g"][0] if kind[1] == "g" else vectors[kind[1]][j]
        value = folded(left * right)
        sums[slot] = value if first else sums[slot] + value


def lane_row(sums, count):
    rows = [jnp.sum(sums[slot], axis=0, keepdims=True) for slot in range(count)]
    square = jnp.concatenate(rows + [jnp.zeros((LANES - count, LANES), F32)], axis=0)
    return jnp.sum(square.T, axis=0, keepdims=True)


BLOCK = 32


def column_blocks(ref):
    return range(0, ref.shape[-2], BLOCK)


def old_kernel(steps_ref, changes_ref, out_ref, sums):
    for start in column_blocks(steps_ref):
        columns = slice(start, start + BLOCK)
        vectors = {
            "s": [steps_ref[index, :, columns] for index in range(HIST)],
            "y": [changes_ref[index, :, columns] for index in range(HIST - 1)],
        }
        add_products(sums, start == 0, enumerate(PAIRS[:OLD_PAIRS]), vectors)
    out_ref[...] = lane_row(sums, OLD_PAIRS)


def gradient_kernel(
    pos_ref, data_ref, transmission_ref, old_ref, steps_ref, changes_ref, row_ref, gradient_ref, again_ref, out_ref, sums
):
    table = shift_table(data_ref.shape[2], transmission_ref.shape[2], pos_ref[0, 0], 0)
    for start in column_blocks(transmission_ref):
        columns = slice(start, start + BLOCK)
        gradient = jnp.stack(
            [
                dot(data_ref[part, columns], table) + TIKHONOV * transmission_ref[part, columns]
                for part in range(2)
            ]
        )
        gradient_ref[:, columns] = gradient
        again_ref[:, columns] = gradient
        vectors = {
            "s": [steps_ref[index, :, columns] for index in range(HIST)],
            "y": [changes_ref[index, :, columns] for index in range(HIST - 1)]
            + [gradient - old_ref[:, columns]],
            "g": [gradient],
        }
        add_products(sums, start == 0, enumerate(PAIRS[OLD_PAIRS:]), vectors)
    fresh = pltpu.roll(lane_row(sums, len(PAIRS) - OLD_PAIRS), OLD_PAIRS, 1)
    out_ref[...] = jnp.broadcast_to(fresh + row_ref[...], out_ref.shape)


def update_kernel(rows_ref, transmission_ref, gradient_ref, old_ref, steps_ref, changes_ref, out_ref):
    row = jnp.sum(rows_ref[...], axis=0, keepdims=True)
    lane = lax.broadcasted_iota(jnp.int32, row.shape, 1)

    def get(kind, i, j):
        if kind == "yy" and i > j:
            i, j = j, i
        picked = jnp.where(lane == SLOT[(kind, i, j)], row, 0.0)
        return jnp.broadcast_to(jnp.sum(picked, axis=1, keepdims=True), row.shape)

    last = HIST - 1
    floors = [
        jnp.maximum(get("sy", index, index), CURVE_FLOOR * get("ss", index, index)) for index in range(HIST)
    ]
    weights = [1.0 / floor for floor in floors]
    alphas = [None] * HIST
    for index in reversed(range(HIST)):
        value = get("sg", index, index)
        for later in range(index + 1, HIST):
            value = value - alphas[later] * get("sy", index, later)
        alphas[index] = weights[index] * value
    scale = floors[last] / (get("yy", last, last) + EPSILON)
    moves = []
    for index in range(HIST):
        value = get("yg", index, index)
        for other in range(HIST):
            value = value - alphas[other] * get("yy", index, other)
        value = scale * value
        for before in range(index):
            value = value + moves[before] * get("sy", before, index)
        moves.append(alphas[index] - weights[index] * value)
    repeat = out_ref.shape[-1] // LANES
    wide = lambda value: jnp.concatenate([value] * repeat, axis=1)
    scale_row = wide(scale)
    change_rows = [wide(-scale * alpha) for alpha in alphas]
    step_rows = [wide(move) for move in moves]
    for part in range(2):
        for start in column_blocks(out_ref):
            columns = slice(start, start + BLOCK)
            gradient = gradient_ref[part, columns]
            total = scale_row * gradient + change_rows[last] * (gradient - old_ref[part, columns])
            for index in range(HIST - 1):
                total = total + change_rows[index] * changes_ref[index, part, columns]
            for index in range(HIST):
                total = total + step_rows[index] * steps_ref[index, part, columns]
            out_ref[part, columns] = transmission_ref[part, columns] - total


def call(body, outs, scratch=(), limit=48, smem=(), far=(), count=0, cost=None):
    space = lambda index: pltpu.SMEM if index in smem else pl.ANY if index in far else pltpu.VMEM
    specs = [pl.BlockSpec(memory_space=space(index)) for index in range(count)]
    return pl.pallas_call(
        body,
        out_shape=outs,
        in_specs=specs,
        out_specs=jax.tree.map(lambda _: pl.BlockSpec(memory_space=pltpu.VMEM), outs),
        scratch_shapes=list(scratch),
        compiler_params=pltpu.CompilerParams(vmem_limit_bytes=limit * MIB),
        cost_estimate=cost,
    )


def cost(flops, moved):
    return pl.CostEstimate(flops=int(flops), bytes_accessed=int(moved), transcendentals=0)


def home(region, member):
    return (region, member) if at_home(region, member) else (region ^ 1, member ^ 2)


def at_home(region, member):
    return region % 2 == member // 2


def away(region, member):
    return not at_home(region, member)


def fast(mesh, transmission, probe, measured, positions, past_steps, past_changes, old_gradient):
    regions, members = mesh.shape["region"], mesh.shape["grp"]
    barrier = lax.optimization_barrier

    def send(value, target, chosen=lambda region, member: True):
        pairs = []
        for region in range(regions):
            for member in range(members):
                if chosen(region, member):
                    to_region, to_member = target(region, member)
                    pairs.append((region * members + member, to_region * members + to_member))
        return lax.ppermute(value, AXES, pairs)

    near = lambda region, member: (region, member ^ 1)
    far = lambda region, member: (region, member ^ 2)
    cross = lambda region, member: (region, member ^ 3)
    mate = lambda region, member: (region ^ 1, member)
    along_x = lambda region, member: (region ^ 2, member)
    along_y = lambda region, member: (region ^ 4, member)
    diagonal = lambda region, member: (region ^ 6, member)
    home_near = lambda region, member: (region ^ 1, member ^ 3)

    region, member = lax.axis_index("region"), lax.axis_index("grp")
    core, half, line = region & 1, member & 1, (region >> 1) & 3
    is_home = core == (member >> 1)
    chunk, frame_len = probe.shape[2], probe.shape[3]
    piece_len, tile_len = transmission.shape[1], transmission.shape[2]
    size = jax.ShapeDtypeStruct
    place = jnp.stack([core, member, line, half, is_home.astype(jnp.int32)]).astype(jnp.int32)

    part, which = line & 1, line >> 1
    base = 4 * core + 2 * half
    other_base = 4 * core + 2 * (1 - half)

    def block(mode):
        return lax.dynamic_slice(probe, (part, mode, 0, 0), (1, 1, chunk, frame_len)).reshape(chunk, frame_len)

    same_block, flip_block = block(base + which), block(other_base + which)
    from_far, from_near = send(same_block, far), send(flip_block, near)
    from_cross = send(flip_block, cross)
    mate_positions = send(positions, mate)
    piece = call(cut_kernel, size((2, piece_len, frame_len), BF), count=2, smem=(0,), limit=16)(
        positions, transmission
    )
    measured_low, from_near = barrier((measured[0].astype(BF), from_near))
    target = send(measured_low, home)
    q0 = jnp.concatenate([from_near, from_far, from_cross], axis=0)
    piece, place, mate_positions, target, q0 = barrier((piece, place, mate_positions, target, q0))
    q1, q2 = send(q0, along_x), send(q0, along_y)
    own = send(piece, home)
    beside = send(piece, near, at_home)
    further = send(piece, home_near, away)
    cut = q0.shape[0] // 2
    q3a, q3b = send(q2[:cut], along_x), send(q1[cut:], along_y)
    own, beside, further, q3a, q3b = barrier((own, beside, further, q3a, q3b))
    side = jnp.where(is_home, beside, further)
    mate_own, mate_side = send(own, mate), send(side, mate)
    whole_probe = call(
        probe_kernel,
        size((2, 2, frame_len, frame_len), BF),
        [pltpu.SemaphoreType.DMA((2, 2))],
        count=7,
        smem=(0,),
        far=(1,),
        limit=16,
    )(place, probe, q0, q1, q2, q3a, q3b)

    right = jnp.asarray(propagator(frame_len))
    double = 2 * frame_len
    flops = 2 * 2 * double**3
    field = size((2, 2, frame_len, frame_len), BF)
    partial = size((frame_len // 2, frame_len), F32)
    far_field, sent, kept = call(
        forward_kernel,
        (field, partial, partial),
        [
            pltpu.VMEM((2, tile_len, frame_len), BF),
            pltpu.VMEM((2, frame_len, frame_len), BF),
            pltpu.VMEM((double, double), BF),
            pltpu.VMEM((double, double), BF),
            pltpu.VMEM((frame_len, frame_len), F32),
        ],
        count=10,
        smem=(0, 1, 2),
        limit=24,
        cost=cost(flops, 16 * MIB),
    )(place, positions, mate_positions, own, side, mate_own, mate_side, whole_probe, target, right)

    chip = kept + send(sent, mate)
    misfit = chip + send(chip.astype(BF), near).astype(F32)
    mates_misfit = send(misfit, mate)

    piece_shape = size((2, piece_len, frame_len), BF)
    sent, kept_side, kept = call(
        backward_kernel,
        (size((2, 2, piece_len, frame_len), BF), piece_shape, piece_shape),
        [
            pltpu.VMEM((frame_len, frame_len), F32),
            pltpu.VMEM((double, double), BF),
            pltpu.VMEM((double, double), BF),
            pltpu.VMEM((2, frame_len, frame_len), BF),
            pltpu.VMEM((4 * piece_len, frame_len), BF),
        ],
        count=8,
        smem=(0, 1, 2),
        limit=24,
        cost=cost(flops, 12 * MIB),
    )(place, positions, mate_positions, far_field, whole_probe, misfit, mates_misfit, right)
    met = send(sent, mate)
    add = lambda a, b: (a.astype(F32) + b.astype(F32)).astype(BF)
    kept_side, kept = add(kept_side, met[0]), add(kept, met[1])
    first, second = send(kept, home, away), send(kept_side, home_near, away)
    beside = send(kept_side, near, at_home)
    data = jnp.where(is_home, add(kept, beside), add(first, second))

    devices = regions * members
    moved = 4 * 2 * piece_len * tile_len
    old_row = call(
        old_kernel,
        size((1, LANES), F32),
        [pltpu.VMEM((OLD_PAIRS, 8, LANES), F32)],
        count=2,
        limit=16,
        cost=cost(22 * moved, 7 * moved),
    )(past_steps, past_changes)
    gradient, again, row = call(
        gradient_kernel,
        (size(transmission.shape, F32), size(transmission.shape, F32), size((devices, LANES), F32)),
        [pltpu.VMEM((len(PAIRS) - OLD_PAIRS, 8, LANES), F32)],
        count=7,
        smem=(0,),
        limit=16,
        cost=cost(16 * moved, 10 * moved),
    )(positions, data, transmission, old_gradient, past_steps, past_changes, old_row)
    all_rows = lax.all_to_all(
        row.reshape(devices, 1, LANES), AXES, split_axis=0, concat_axis=0, tiled=True
    ).reshape(devices, LANES)
    updated = call(
        update_kernel,
        size(transmission.shape, F32),
        count=6,
        limit=16,
        cost=cost(10 * moved, 11 * moved),
    )(all_rows, transmission, again, old_gradient, past_steps, past_changes)
    return (updated, gradient)


def solution(mesh):
    split = mesh.shape["grp"] == 4 and mesh.shape["region"] == 8

    def shards(*args):
        probe, positions, past_steps = args[1], args[3], args[4]
        sized = probe.shape[1] == 8 and positions.shape[0] == 1 and past_steps.shape[0] == HIST
        if split and sized:
            return fast(mesh, *args)
        return general(*args)

    return jax.shard_map(
        shards,
        mesh=mesh,
        in_specs=(
            P(None, "grp", "region"),
            P(None, None, "grp", None),
            P("region", "grp", None),
            P("region", None),
            P(None, None, "grp", "region"),
            P(None, None, "grp", "region"),
            P(None, "grp", "region"),
        ),
        out_specs=(P(None, "grp", "region"), P(None, "grp", "region")),
        check_vma=False,
    )
```

```python
import math

import jax
import jax.numpy as jnp
import ml_dtypes
import numpy as np
from jax import lax
from jax.experimental import pallas as pl
from jax.experimental.pallas import tpu as pltpu
from jax.sharding import PartitionSpec as P

TWO_PI = 2.0 * math.pi
CURVE_FLOOR = 0.25
TIKHONOV = 0.5
EPSILON = 1e-06
BF = jnp.bfloat16
F32 = jnp.float32
AXES = ("region", "grp")
LANES = 128
MIB = 1 << 20
HIST = 4


def dft_tables(count):
    index = jnp.arange(count, dtype=jnp.int32)
    phase = (index[:, None] * index[None, :] % count).astype(jnp.float32) * (TWO_PI / count)
    factor = 1.0 / math.sqrt(count)
    return (
        (jnp.cos(phase) * factor).astype(jnp.bfloat16),
        (-jnp.sin(phase) * factor).astype(jnp.bfloat16),
    )


def chirp_table(count):
    index = jnp.arange(count, dtype=jnp.int32)
    wavenumber = (index + count // 2) % count - count // 2
    phase = (wavenumber * wavenumber % (4 * count)).astype(jnp.float32) * (TWO_PI / (4 * count))
    return (jnp.cos(phase), -jnp.sin(phase))


def rotate(real_part, imag_part, turn_real, turn_imag):
    return (
        real_part * turn_real - imag_part * turn_imag,
        real_part * turn_imag + imag_part * turn_real,
    )


def narrow(pair):
    return jnp.stack([pair[0], pair[1]]).astype(jnp.bfloat16)


def right_product(field, matrix_real, matrix_imag):

    def single(left, right):
        return jnp.einsum("...k,kj->...j", left, right, preferred_element_type=jnp.float32)

    return (
        single(field[0], matrix_real) - single(field[1], matrix_imag),
        single(field[0], matrix_imag) + single(field[1], matrix_real),
    )


def left_product(matrix_real, matrix_imag, field):

    def single(left, right):
        return jnp.einsum("jk,...kc->...jc", left, right, preferred_element_type=jnp.float32)

    return (
        single(matrix_real, field[0]) - single(matrix_imag, field[1]),
        single(matrix_real, field[1]) + single(matrix_imag, field[0]),
    )


def general(transmission, probe, measured, positions, past_steps, past_changes, old_gradient):
    member = lax.axis_index("grp")
    frame_len = probe.shape[3]
    rows_here = probe.shape[2]
    tile_len = transmission.shape[2]
    anchor = jnp.zeros((), jnp.int32)
    fwd_real, fwd_imag = dft_tables(frame_len)
    inv_imag = -fwd_imag
    chirp_real, chirp_imag = chirp_table(frame_len)
    probe_wide = probe.astype(jnp.float32)
    tile = lax.all_gather(transmission.astype(jnp.bfloat16), "grp", axis=1, tiled=True)
    frame = 0
    first_row = positions[frame, 0] + member * rows_here
    window = jnp.swapaxes(
        lax.dynamic_slice(
            tile, (anchor, positions[frame, 1], first_row), (2, frame_len, rows_here)
        ),
        1,
        2,
    ).astype(jnp.float32)
    wave = narrow(rotate(probe_wide[0], probe_wide[1], window[0], window[1]))
    section = narrow(rotate(*right_product(wave, fwd_real, fwd_imag), chirp_real, chirp_imag))
    spread = narrow(right_product(section, fwd_real, inv_imag))
    section = narrow(
        rotate(
            *left_product(
                fwd_real,
                fwd_imag,
                lax.all_to_all(spread, "grp", split_axis=3, concat_axis=2, tiled=True),
            ),
            chirp_real[:, None],
            chirp_imag[:, None]
        )
    )
    far_field = narrow(left_product(fwd_real, inv_imag, section))
    near_rows = lax.all_to_all(far_field, "grp", split_axis=2, concat_axis=3, tiled=True)
    field_wide = near_rows.astype(jnp.float32)
    misfit = (
        jnp.sum(field_wide[0] * field_wide[0] + field_wide[1] * field_wide[1], axis=0)
        - measured[frame]
    )
    weighted = (misfit * field_wide).astype(jnp.bfloat16)
    section = narrow(
        rotate(
            *left_product(
                fwd_real,
                fwd_imag,
                lax.all_to_all(weighted, "grp", split_axis=3, concat_axis=2, tiled=True),
            ),
            chirp_real[:, None],
            -chirp_imag[:, None]
        )
    )
    returned = narrow(left_product(fwd_real, inv_imag, section))
    section = narrow(
        rotate(
            *right_product(
                lax.all_to_all(returned, "grp", split_axis=2, concat_axis=3, tiled=True),
                fwd_real,
                fwd_imag,
            ),
            chirp_real,
            -chirp_imag
        )
    )
    back_wave = jnp.stack(right_product(section, fwd_real, inv_imag))
    grad_real = 4.0 * jnp.sum(probe_wide[0] * back_wave[0] + probe_wide[1] * back_wave[1], axis=0)
    grad_imag = 4.0 * jnp.sum(probe_wide[0] * back_wave[1] - probe_wide[1] * back_wave[0], axis=0)
    frame_grads = [jnp.stack([grad_real, grad_imag])]
    scattered = jnp.zeros((2, tile_len, tile_len), jnp.float32)
    frame = 0
    corner = (anchor, positions[frame, 1], positions[frame, 0] + member * rows_here)
    scattered = lax.dynamic_update_slice(scattered, jnp.swapaxes(frame_grads[frame], 1, 2), corner)
    data_grad = lax.psum_scatter(
        scattered.astype(jnp.bfloat16), "grp", scatter_dimension=1, tiled=True
    ).astype(jnp.float32)
    gradient = data_grad + TIKHONOV * transmission
    depth = past_steps.shape[0]
    last = depth - 1
    change_new = gradient - old_gradient
    steps_list = [past_steps[index] for index in range(depth)]
    changes = [past_changes[index] for index in range(depth - 1)] + [change_new]
    alphas = [None] * depth
    curvature, self_dots, change_norm = lax.psum(
        (
            jnp.stack([jnp.sum(steps_list[index] * changes[index]) for index in range(depth)]),
            jnp.sum(past_steps * past_steps, axis=(1, 2, 3)),
            jnp.sum(change_new * change_new),
        ),
        ("region", "grp"),
    )
    weights = [
        1.0 / jnp.maximum(curvature[index], CURVE_FLOOR * self_dots[index])
        for index in range(depth)
    ]
    direction = gradient
    for index in reversed(range(depth)):
        alphas[index] = weights[index] * lax.psum(
            jnp.sum(steps_list[index] * direction), ("region", "grp")
        )
        direction = direction - alphas[index] * changes[index]
    scale = jnp.maximum(curvature[last], CURVE_FLOOR * self_dots[last]) / (change_norm + EPSILON)
    direction = scale * direction
    for index in range(depth):
        beta = weights[index] * lax.psum(jnp.sum(changes[index] * direction), ("region", "grp"))
        direction = direction + (alphas[index] - beta) * steps_list[index]
    return (transmission - direction, gradient)


def propagator(count):
    index = np.arange(count, dtype=np.int64)
    phase = (index[:, None] * index[None, :] % count).astype(np.float32) * np.float32(TWO_PI / count)
    factor = np.float32(1.0 / math.sqrt(count))
    table = (np.cos(phase) * factor).astype(ml_dtypes.bfloat16).astype(np.float64) + 1j * (
        -np.sin(phase) * factor
    ).astype(ml_dtypes.bfloat16).astype(np.float64)
    wavenumber = (index + count // 2) % count - count // 2
    chirp = np.exp(-1j * (wavenumber * wavenumber % (4 * count)) * (TWO_PI / (4 * count)))
    folded = (table * chirp[None, :]) @ np.conj(table)
    folded = 0.5 * (folded + folded.T)
    real, imag = folded.real, folded.imag
    return np.block([[real, imag], [-imag, real]]).astype(ml_dtypes.bfloat16)


def dot(left, right, dims=((1,), (0,))):
    return lax.dot_general(left, right, (dims, ((), ())), preferred_element_type=F32)


def shift_table(rows, columns, row_base, column_base):
    row = lax.broadcasted_iota(jnp.int32, (rows, columns), 0) + row_base
    column = lax.broadcasted_iota(jnp.int32, (rows, columns), 1) + column_base
    return jnp.where(row == column, 1.0, 0.0).astype(BF)


def cut_kernel(pos_ref, tile_ref, out_ref):
    tile_len, frame_len = tile_ref.shape[2], out_ref.shape[2]
    table = shift_table(tile_len, frame_len, 0, pos_ref[0, 0])
    for part in range(2):
        out_ref[part] = dot(tile_ref[part].astype(BF), table).astype(BF)


def probe_kernel(place_ref, all_ref, q0_ref, q1_ref, q2_ref, q3a_ref, q3b_ref, probe_ref, sem):
    core, place, line, half = (place_ref[index] for index in range(4))
    chunk = all_ref.shape[2]

    def rows_of(step):
        return pl.ds(pl.multiple_of(lax.bitwise_xor(place, step) * chunk, chunk), chunk)

    copies = [
        pltpu.make_async_copy(
            all_ref.at[part, 4 * core + 2 * half + mode], probe_ref.at[part, mode, rows_of(0), :], sem.at[part, mode]
        )
        for part in range(2)
        for mode in range(2)
    ]
    for copy in copies:
        copy.start()
    cut = q3a_ref.shape[0]
    for turn, ref in ((0, q0_ref), (1, q1_ref), (2, q2_ref), (3, None)):
        combo = lax.bitwise_xor(line, turn)
        part, mode = lax.rem(combo, 2), lax.div(combo, 2)
        for step in range(1, 4):
            start = (step - 1) * chunk
            if ref is not None:
                value = ref[start : start + chunk]
            elif start + chunk <= cut:
                value = q3a_ref[start : start + chunk]
            elif start >= cut:
                value = q3b_ref[start - cut : start - cut + chunk]
            else:
                value = jnp.concatenate([q3a_ref[start:cut], q3b_ref[: start + chunk - cut]], axis=0)
            probe_ref[part, mode, rows_of(step), :] = value
    for copy in copies:
        copy.wait()


def forward_kernel(
    place_ref, own_ref, side_ref, mate_own_ref, mate_side_ref, probe_ref, measured_ref,
    right_ref, turned_ref, far_ref, send_ref, tile, window_ref, wave, total,
):
    core, half = place_ref[0], place_ref[3]
    chunk, frame_len = measured_ref.shape
    piece_len = own_ref.shape[1]
    piece = 2 * core + half
    for step, ref in enumerate((own_ref, side_ref, mate_own_ref, mate_side_ref)):
        base = pl.multiple_of(lax.bitwise_xor(piece, step) * piece_len, piece_len)
        for part in range(2):
            tile[part, pl.ds(base, piece_len), :] = ref[part]
    column = place_ref[4]
    table = shift_table(tile.shape[1], frame_len, 0, column)
    for part in range(2):
        window_ref[part] = dot(tile[part], table, ((0,), (0,))).astype(BF)

    block = frame_len // 2
    for mode in range(2):
        rows = slice(mode * frame_len, (mode + 1) * frame_len)
        pr, pi = probe_ref[0, mode].astype(F32), probe_ref[1, mode].astype(F32)
        wr, wi = window_ref[0].astype(F32), window_ref[1].astype(F32)
        wave[rows, :frame_len] = (pr * wr - pi * wi).astype(BF)
        wave[rows, frame_len:] = (pr * wi + pi * wr).astype(BF)
    for part in range(2):
        for cell in range(2):
            start = part * frame_len + cell * block
            result = dot(wave[...], right_ref[:, start : start + block])
            result = (result if part == 0 else -result).astype(BF)
            for mode in range(2):
                turned_ref[mode, cell, part * frame_len : (part + 1) * frame_len, :] = result[
                    mode * frame_len : (mode + 1) * frame_len
                ]
    far_columns(1 - core, turned_ref, right_ref, far_ref, total)
    subtract(core, half, 1 - core, measured_ref, total)
    send_ref[...] = total[...].astype(BF)


def far_columns(cell, turned_ref, right_ref, far_ref, total):
    frame_len = total.shape[0]
    power = 0.0
    for mode in range(2):
        result = dot(right_ref[...], turned_ref[mode, cell])
        real, imag = result[:frame_len].astype(BF), (-result[frame_len:]).astype(BF)
        far_ref[mode, 0] = real
        far_ref[mode, 1] = imag
        real, imag = real.astype(F32), imag.astype(F32)
        power = power + (real * real + imag * imag)
    total[...] = power


def subtract(core, half, cell, measured_ref, total):
    chunk, block = measured_ref.shape[0], total.shape[1]
    rows = pl.ds(pl.multiple_of((2 * core + half) * chunk, chunk), chunk)
    wanted = jnp.where(cell == 0, measured_ref[:, :block], measured_ref[:, block:])
    total[rows, :] = total[rows, :] - wanted.astype(F32)


def rest_kernel(place_ref, turned_ref, measured_ref, right_ref, far_ref, total):
    core, half = place_ref[0], place_ref[3]
    far_columns(core, turned_ref, right_ref, far_ref, total)
    subtract(core, half, core, measured_ref, total)


def left_columns(misfit, far_ref, right_ref, weighted, store):
    frame_len, block = misfit.shape
    for mode in range(2):
        for part in range(2):
            weighted[part * frame_len : (part + 1) * frame_len, mode * block : (mode + 1) * block] = (
                misfit * far_ref[mode, part].astype(F32)
            ).astype(BF)
        result = dot(right_ref[...], weighted[:, mode * block : (mode + 1) * block])
        store(mode, 0, result[:frame_len].astype(BF))
        store(mode, 1, (-result[frame_len:]).astype(BF))


def own_kernel(far_ref, mine_ref, right_ref, out_ref, weighted):
    frame_len = mine_ref.shape[0]

    def store(mode, part, value):
        out_ref[part, mode * frame_len : (mode + 1) * frame_len, :] = value

    left_columns(mine_ref[...], far_ref, right_ref, weighted, store)


def backward_kernel(
    place_ref, far_ref, probe_ref, mates_ref, own_ref, right_ref,
    send_ref, side_ref, keep_ref, weighted, turned, grad, table,
):
    core, half = place_ref[0], place_ref[3]
    column = place_ref[4]
    frame_len, block = mates_ref.shape
    piece_len = keep_ref.shape[1]

    def lanes(part, cell):
        return pl.ds(pl.multiple_of(part * frame_len + cell * block, block), block)

    def store(mode, part, value):
        turned[mode * frame_len : (mode + 1) * frame_len, lanes(part, 1 - core)] = value

    left_columns(mates_ref[...].astype(F32), far_ref, right_ref, weighted, store)
    for part in range(2):
        turned[:, lanes(part, core)] = own_ref[part]
    for cell in range(2):
        columns = slice(cell * block, (cell + 1) * block)
        back = [
            dot(turned[...], right_ref[:, part * frame_len + cell * block : part * frame_len + (cell + 1) * block])
            for part in range(2)
        ]
        real, imag = 0.0, 0.0
        for mode in range(2):
            br, bi = (value[mode * frame_len : (mode + 1) * frame_len] for value in back)
            pr, pi = probe_ref[0, mode, :, columns].astype(F32), probe_ref[1, mode, :, columns].astype(F32)
            real = real + (pr * br - pi * bi)
            imag = imag + (pr * bi + pi * br)
        grad[0, :, columns] = (4.0 * real).astype(BF)
        grad[1, :, columns] = (-4.0 * imag).astype(BF)

    slots = [(1 - core, 1), (1 - core, 0), (core, 1), (core, 0)]
    for index, (pair, flip) in enumerate(slots):
        base = (2 * pair + lax.bitwise_xor(half, flip)) * piece_len
        table[index * piece_len : (index + 1) * piece_len, :] = shift_table(piece_len, frame_len, base, column)
    for part in range(2):
        value = dot(table[...], grad[part], ((1,), (1,))).astype(BF)
        send_ref[0, part] = value[:piece_len]
        send_ref[1, part] = value[piece_len : 2 * piece_len]
        side_ref[part] = value[2 * piece_len : 3 * piece_len]
        keep_ref[part] = value[3 * piece_len :]


PAIRS = [("sy", i, j) for j in range(HIST - 1) for i in range(HIST)]
PAIRS += [("ss", i, i) for i in range(HIST)]
PAIRS += [("yy", i, j) for j in range(HIST - 1) for i in range(j + 1)]
OLD_PAIRS = len(PAIRS)
PAIRS += [("sy", i, HIST - 1) for i in range(HIST)]
PAIRS += [("yy", i, HIST - 1) for i in range(HIST)]
PAIRS += [("sg", i, i) for i in range(HIST)]
PAIRS += [("yg", i, i) for i in range(HIST)]
SLOT = {pair: index for index, pair in enumerate(PAIRS)}


def folded(value):
    parts, rows, columns = value.shape
    total = jnp.sum(value.reshape(parts * rows // 8, 8, columns), axis=0)
    return sum(total[:, start : start + LANES] for start in range(0, columns, LANES))


def add_products(sums, first, slots, vectors):
    for slot, pair in slots:
        kind, i, j = pair
        left = vectors[kind[0]][i]
        right = vectors["g"][0] if kind[1] == "g" else vectors[kind[1]][j]
        value = folded(left * right)
        sums[slot] = value if first else sums[slot] + value


def lane_row(sums, count):
    rows = [jnp.sum(sums[slot], axis=0, keepdims=True) for slot in range(count)]
    square = jnp.concatenate(rows + [jnp.zeros((LANES - count, LANES), F32)], axis=0)
    return jnp.sum(square.T, axis=0, keepdims=True)


BLOCK = 32


def column_blocks(ref):
    return range(0, ref.shape[-2], BLOCK)


def old_kernel(steps_ref, changes_ref, out_ref, sums):
    for start in column_blocks(steps_ref):
        columns = slice(start, start + BLOCK)
        vectors = {
            "s": [steps_ref[index, :, columns] for index in range(HIST)],
            "y": [changes_ref[index, :, columns] for index in range(HIST - 1)],
        }
        add_products(sums, start == 0, enumerate(PAIRS[:OLD_PAIRS]), vectors)
    out_ref[...] = lane_row(sums, OLD_PAIRS)


def gradient_kernel(
    pos_ref, data_ref, transmission_ref, old_ref, steps_ref, changes_ref, row_ref, gradient_ref, out_ref, sums
):
    table = shift_table(data_ref.shape[2], transmission_ref.shape[2], pos_ref[0, 0], 0)
    for start in column_blocks(transmission_ref):
        columns = slice(start, start + BLOCK)
        gradient = jnp.stack(
            [
                dot(data_ref[part, columns], table) + TIKHONOV * transmission_ref[part, columns]
                for part in range(2)
            ]
        )
        gradient_ref[:, columns] = gradient
        vectors = {
            "s": [steps_ref[index, :, columns] for index in range(HIST)],
            "y": [changes_ref[index, :, columns] for index in range(HIST - 1)]
            + [gradient - old_ref[:, columns]],
            "g": [gradient],
        }
        add_products(sums, start == 0, enumerate(PAIRS[OLD_PAIRS:]), vectors)
    fresh = pltpu.roll(lane_row(sums, len(PAIRS) - OLD_PAIRS), OLD_PAIRS, 1)
    out_ref[...] = jnp.broadcast_to(fresh + row_ref[...], out_ref.shape)


def update_kernel(rows_ref, transmission_ref, gradient_ref, old_ref, steps_ref, changes_ref, out_ref, copy_ref):
    row = jnp.sum(rows_ref[...], axis=0, keepdims=True)
    lane = lax.broadcasted_iota(jnp.int32, row.shape, 1)

    def get(kind, i, j):
        if kind == "yy" and i > j:
            i, j = j, i
        picked = jnp.where(lane == SLOT[(kind, i, j)], row, 0.0)
        return jnp.broadcast_to(jnp.sum(picked, axis=1, keepdims=True), row.shape)

    last = HIST - 1
    floors = [
        jnp.maximum(get("sy", index, index), CURVE_FLOOR * get("ss", index, index)) for index in range(HIST)
    ]
    weights = [1.0 / floor for floor in floors]
    alphas = [None] * HIST
    for index in reversed(range(HIST)):
        value = get("sg", index, index)
        for later in range(index + 1, HIST):
            value = value - alphas[later] * get("sy", index, later)
        alphas[index] = weights[index] * value
    scale = floors[last] / (get("yy", last, last) + EPSILON)
    moves = []
    for index in range(HIST):
        value = get("yg", index, index)
        for other in range(HIST):
            value = value - alphas[other] * get("yy", index, other)
        value = scale * value
        for before in range(index):
            value = value + moves[before] * get("sy", before, index)
        moves.append(alphas[index] - weights[index] * value)
    repeat = out_ref.shape[-1] // LANES
    wide = lambda value: jnp.concatenate([value] * repeat, axis=1)
    scale_row = wide(scale)
    change_rows = [wide(-scale * alpha) for alpha in alphas]
    step_rows = [wide(move) for move in moves]
    for part in range(2):
        for start in column_blocks(out_ref):
            columns = slice(start, start + BLOCK)
            gradient = gradient_ref[part, columns]
            copy_ref[part, columns] = gradient
            total = scale_row * gradient + change_rows[last] * (gradient - old_ref[part, columns])
            for index in range(HIST - 1):
                total = total + change_rows[index] * changes_ref[index, part, columns]
            for index in range(HIST):
                total = total + step_rows[index] * steps_ref[index, part, columns]
            out_ref[part, columns] = transmission_ref[part, columns] - total


def call(body, outs, scratch=(), limit=48, smem=(), far=(), count=0, cost=None):
    space = lambda index: pltpu.SMEM if index in smem else pl.ANY if index in far else pltpu.VMEM
    specs = [pl.BlockSpec(memory_space=space(index)) for index in range(count)]
    return pl.pallas_call(
        body,
        out_shape=outs,
        in_specs=specs,
        out_specs=jax.tree.map(lambda _: pl.BlockSpec(memory_space=pltpu.VMEM), outs),
        scratch_shapes=list(scratch),
        compiler_params=pltpu.CompilerParams(vmem_limit_bytes=limit * MIB),
        cost_estimate=cost,
    )


def cost(flops, moved):
    return pl.CostEstimate(flops=int(flops), bytes_accessed=int(moved), transcendentals=0)


def home(region, member):
    return (region, member) if at_home(region, member) else (region ^ 1, member ^ 2)


def at_home(region, member):
    return region % 2 == member // 2


def away(region, member):
    return not at_home(region, member)


def fast(mesh, transmission, probe, measured, positions, past_steps, past_changes, old_gradient):
    regions, members = mesh.shape["region"], mesh.shape["grp"]
    barrier = lax.optimization_barrier

    def send(value, target, chosen=lambda region, member: True):
        pairs = []
        for region in range(regions):
            for member in range(members):
                if chosen(region, member):
                    to_region, to_member = target(region, member)
                    pairs.append((region * members + member, to_region * members + to_member))
        return lax.ppermute(value, AXES, pairs)

    near = lambda region, member: (region, member ^ 1)
    far = lambda region, member: (region, member ^ 2)
    cross = lambda region, member: (region, member ^ 3)
    mate = lambda region, member: (region ^ 1, member)
    along_x = lambda region, member: (region ^ 2, member)
    along_y = lambda region, member: (region ^ 4, member)
    diagonal = lambda region, member: (region ^ 6, member)
    home_near = lambda region, member: (region ^ 1, member ^ 3)

    region, member = lax.axis_index("region"), lax.axis_index("grp")
    core, half, line = region & 1, member & 1, (region >> 1) & 3
    is_home = core == (member >> 1)
    chunk, frame_len = probe.shape[2], probe.shape[3]
    piece_len, tile_len = transmission.shape[1], transmission.shape[2]
    size = jax.ShapeDtypeStruct

    part, which = line & 1, line >> 1
    base = 4 * core + 2 * half
    other_base = 4 * core + 2 * (1 - half)

    def block(mode):
        return lax.dynamic_slice(probe, (part, mode, 0, 0), (1, 1, chunk, frame_len)).reshape(chunk, frame_len)

    same_block, flip_block = block(base + which), block(other_base + which)
    from_far, from_near = send(same_block, far), send(flip_block, near)
    from_cross = send(flip_block, cross)
    mate_positions = send(positions, mate)
    piece = call(cut_kernel, size((2, piece_len, frame_len), BF), count=2, smem=(0,), limit=16)(
        positions, transmission
    )
    measured_low, from_near = barrier((measured[0].astype(BF), from_near))
    target = send(measured_low, home)
    q0 = jnp.concatenate([from_near, from_far, from_cross], axis=0)
    column = jnp.where(is_home, positions[0, 1], mate_positions[0, 1])
    place = jnp.stack([core, member, line, half, column]).astype(jnp.int32)
    piece, place, target, q0 = barrier((piece, place, target, q0))
    q1, q2 = send(q0, along_x), send(q0, along_y)
    own = send(piece, home)
    beside = send(piece, near, at_home)
    further = send(piece, home_near, away)
    cut = q0.shape[0] // 2
    q3a, q3b = send(q2[:cut], along_x), send(q1[cut:], along_y)
    own, beside, further, q3a, q3b = barrier((own, beside, further, q3a, q3b))
    side = jnp.where(is_home, beside, further)
    mate_own, mate_side = send(own, mate), send(side, mate)
    whole_probe = call(
        probe_kernel,
        size((2, 2, frame_len, frame_len), BF),
        [pltpu.SemaphoreType.DMA((2, 2))],
        count=7,
        smem=(0,),
        far=(1,),
        limit=16,
    )(place, probe, q0, q1, q2, q3a, q3b)

    right = jnp.asarray(propagator(frame_len))
    double = 2 * frame_len
    flops = 2 * 2 * double**3
    half_len = frame_len // 2
    half_field = size((2, 2, frame_len, half_len), BF)
    turned, mates_far, sent = call(
        forward_kernel,
        (size((2, 2, double, half_len), BF), half_field, size((frame_len, half_len), BF)),
        [
            pltpu.VMEM((2, tile_len, frame_len), BF),
            pltpu.VMEM((2, frame_len, frame_len), BF),
            pltpu.VMEM((double, double), BF),
            pltpu.VMEM((frame_len, half_len), F32),
        ],
        count=8,
        smem=(0,),
        limit=24,
        cost=cost(3 * flops // 4, 16 * MIB),
    )(place, own, side, mate_own, mate_side, whole_probe, target, right)
    met = send(sent, mate)
    own_far, kept = call(
        rest_kernel,
        (half_field, size((frame_len, half_len), F32)),
        count=4,
        smem=(0,),
        limit=24,
        cost=cost(flops // 4, 4 * MIB),
    )(place, turned, target, right)

    chip = kept + met.astype(F32)
    misfit = chip + send(chip.astype(BF), near).astype(F32)
    mates_misfit = send(misfit.astype(BF), mate)
    own_left = call(
        own_kernel,
        size((2, double, half_len), BF),
        [pltpu.VMEM((double, frame_len), BF)],
        count=3,
        limit=24,
        cost=cost(flops // 4, 4 * MIB),
    )(own_far, misfit, right)

    piece_shape = size((2, piece_len, frame_len), BF)
    sent, kept_side, kept = call(
        backward_kernel,
        (size((2, 2, piece_len, frame_len), BF), piece_shape, piece_shape),
        [
            pltpu.VMEM((double, frame_len), BF),
            pltpu.VMEM((double, double), BF),
            pltpu.VMEM((2, frame_len, frame_len), BF),
            pltpu.VMEM((4 * piece_len, frame_len), BF),
        ],
        count=6,
        smem=(0,),
        limit=24,
        cost=cost(3 * flops // 4, 12 * MIB),
    )(place, mates_far, whole_probe, mates_misfit, own_left, right)
    met = send(sent, mate)
    add = lambda a, b: (a.astype(F32) + b.astype(F32)).astype(BF)
    kept_side, kept = add(kept_side, met[0]), add(kept, met[1])
    first, second = send(kept, home, away), send(kept_side, home_near, away)
    beside = send(kept_side, near, at_home)
    data = jnp.where(is_home, add(kept, beside), add(first, second))

    devices = regions * members
    moved = 4 * 2 * piece_len * tile_len
    old_row = call(
        old_kernel,
        size((1, LANES), F32),
        [pltpu.VMEM((OLD_PAIRS, 8, LANES), F32)],
        count=2,
        limit=16,
        cost=cost(22 * moved, 7 * moved),
    )(past_steps, past_changes)
    gradient, row = call(
        gradient_kernel,
        (size(transmission.shape, F32), size((devices, LANES), F32)),
        [pltpu.VMEM((len(PAIRS) - OLD_PAIRS, 8, LANES), F32)],
        count=7,
        smem=(0,),
        limit=16,
        cost=cost(16 * moved, 10 * moved),
    )(positions, data, transmission, old_gradient, past_steps, past_changes, old_row)
    all_rows = lax.all_to_all(
        row.reshape(devices, 1, LANES), AXES, split_axis=0, concat_axis=0, tiled=True
    ).reshape(devices, LANES)
    return call(
        update_kernel,
        (size(transmission.shape, F32), size(transmission.shape, F32)),
        count=6,
        limit=16,
        cost=cost(10 * moved, 11 * moved),
    )(all_rows, transmission, gradient, old_gradient, past_steps, past_changes)


def solution(mesh):
    split = mesh.shape["grp"] == 4 and mesh.shape["region"] == 8

    def shards(*args):
        probe, positions, past_steps = args[1], args[3], args[4]
        sized = probe.shape[1] == 8 and positions.shape[0] == 1 and past_steps.shape[0] == HIST
        if split and sized:
            return fast(mesh, *args)
        return general(*args)

    return jax.shard_map(
        shards,
        mesh=mesh,
        in_specs=(
            P(None, "grp", "region"),
            P(None, None, "grp", None),
            P("region", "grp", None),
            P("region", None),
            P(None, None, "grp", "region"),
            P(None, None, "grp", "region"),
            P(None, "grp", "region"),
        ),
        out_specs=(P(None, "grp", "region"), P(None, "grp", "region")),
        check_vma=False,
    )
```

```python
import math

import jax
import jax.numpy as jnp
import ml_dtypes
import numpy as np
from jax import lax
from jax.experimental import pallas as pl
from jax.experimental.pallas import tpu as pltpu
from jax.sharding import PartitionSpec as P

TWO_PI = 2.0 * math.pi
CURVE_FLOOR = 0.25
TIKHONOV = 0.5
EPSILON = 1e-06
BF = jnp.bfloat16
F32 = jnp.float32
AXES = ("region", "grp")
LANES = 128
MIB = 1 << 20
HIST = 4


def dft_tables(count):
    index = jnp.arange(count, dtype=jnp.int32)
    phase = (index[:, None] * index[None, :] % count).astype(jnp.float32) * (TWO_PI / count)
    factor = 1.0 / math.sqrt(count)
    return (
        (jnp.cos(phase) * factor).astype(jnp.bfloat16),
        (-jnp.sin(phase) * factor).astype(jnp.bfloat16),
    )


def chirp_table(count):
    index = jnp.arange(count, dtype=jnp.int32)
    wavenumber = (index + count // 2) % count - count // 2
    phase = (wavenumber * wavenumber % (4 * count)).astype(jnp.float32) * (TWO_PI / (4 * count))
    return (jnp.cos(phase), -jnp.sin(phase))


def rotate(real_part, imag_part, turn_real, turn_imag):
    return (
        real_part * turn_real - imag_part * turn_imag,
        real_part * turn_imag + imag_part * turn_real,
    )


def narrow(pair):
    return jnp.stack([pair[0], pair[1]]).astype(jnp.bfloat16)


def right_product(field, matrix_real, matrix_imag):

    def single(left, right):
        return jnp.einsum("...k,kj->...j", left, right, preferred_element_type=jnp.float32)

    return (
        single(field[0], matrix_real) - single(field[1], matrix_imag),
        single(field[0], matrix_imag) + single(field[1], matrix_real),
    )


def left_product(matrix_real, matrix_imag, field):

    def single(left, right):
        return jnp.einsum("jk,...kc->...jc", left, right, preferred_element_type=jnp.float32)

    return (
        single(matrix_real, field[0]) - single(matrix_imag, field[1]),
        single(matrix_real, field[1]) + single(matrix_imag, field[0]),
    )


def general(transmission, probe, measured, positions, past_steps, past_changes, old_gradient):
    member = lax.axis_index("grp")
    frame_len = probe.shape[3]
    rows_here = probe.shape[2]
    tile_len = transmission.shape[2]
    anchor = jnp.zeros((), jnp.int32)
    fwd_real, fwd_imag = dft_tables(frame_len)
    inv_imag = -fwd_imag
    chirp_real, chirp_imag = chirp_table(frame_len)
    probe_wide = probe.astype(jnp.float32)
    tile = lax.all_gather(transmission.astype(jnp.bfloat16), "grp", axis=1, tiled=True)
    frame = 0
    first_row = positions[frame, 0] + member * rows_here
    window = jnp.swapaxes(
        lax.dynamic_slice(
            tile, (anchor, positions[frame, 1], first_row), (2, frame_len, rows_here)
        ),
        1,
        2,
    ).astype(jnp.float32)
    wave = narrow(rotate(probe_wide[0], probe_wide[1], window[0], window[1]))
    section = narrow(rotate(*right_product(wave, fwd_real, fwd_imag), chirp_real, chirp_imag))
    spread = narrow(right_product(section, fwd_real, inv_imag))
    section = narrow(
        rotate(
            *left_product(
                fwd_real,
                fwd_imag,
                lax.all_to_all(spread, "grp", split_axis=3, concat_axis=2, tiled=True),
            ),
            chirp_real[:, None],
            chirp_imag[:, None]
        )
    )
    far_field = narrow(left_product(fwd_real, inv_imag, section))
    near_rows = lax.all_to_all(far_field, "grp", split_axis=2, concat_axis=3, tiled=True)
    field_wide = near_rows.astype(jnp.float32)
    misfit = (
        jnp.sum(field_wide[0] * field_wide[0] + field_wide[1] * field_wide[1], axis=0)
        - measured[frame]
    )
    weighted = (misfit * field_wide).astype(jnp.bfloat16)
    section = narrow(
        rotate(
            *left_product(
                fwd_real,
                fwd_imag,
                lax.all_to_all(weighted, "grp", split_axis=3, concat_axis=2, tiled=True),
            ),
            chirp_real[:, None],
            -chirp_imag[:, None]
        )
    )
    returned = narrow(left_product(fwd_real, inv_imag, section))
    section = narrow(
        rotate(
            *right_product(
                lax.all_to_all(returned, "grp", split_axis=2, concat_axis=3, tiled=True),
                fwd_real,
                fwd_imag,
            ),
            chirp_real,
            -chirp_imag
        )
    )
    back_wave = jnp.stack(right_product(section, fwd_real, inv_imag))
    grad_real = 4.0 * jnp.sum(probe_wide[0] * back_wave[0] + probe_wide[1] * back_wave[1], axis=0)
    grad_imag = 4.0 * jnp.sum(probe_wide[0] * back_wave[1] - probe_wide[1] * back_wave[0], axis=0)
    frame_grads = [jnp.stack([grad_real, grad_imag])]
    scattered = jnp.zeros((2, tile_len, tile_len), jnp.float32)
    frame = 0
    corner = (anchor, positions[frame, 1], positions[frame, 0] + member * rows_here)
    scattered = lax.dynamic_update_slice(scattered, jnp.swapaxes(frame_grads[frame], 1, 2), corner)
    data_grad = lax.psum_scatter(
        scattered.astype(jnp.bfloat16), "grp", scatter_dimension=1, tiled=True
    ).astype(jnp.float32)
    gradient = data_grad + TIKHONOV * transmission
    depth = past_steps.shape[0]
    last = depth - 1
    change_new = gradient - old_gradient
    steps_list = [past_steps[index] for index in range(depth)]
    changes = [past_changes[index] for index in range(depth - 1)] + [change_new]
    alphas = [None] * depth
    curvature, self_dots, change_norm = lax.psum(
        (
            jnp.stack([jnp.sum(steps_list[index] * changes[index]) for index in range(depth)]),
            jnp.sum(past_steps * past_steps, axis=(1, 2, 3)),
            jnp.sum(change_new * change_new),
        ),
        ("region", "grp"),
    )
    weights = [
        1.0 / jnp.maximum(curvature[index], CURVE_FLOOR * self_dots[index])
        for index in range(depth)
    ]
    direction = gradient
    for index in reversed(range(depth)):
        alphas[index] = weights[index] * lax.psum(
            jnp.sum(steps_list[index] * direction), ("region", "grp")
        )
        direction = direction - alphas[index] * changes[index]
    scale = jnp.maximum(curvature[last], CURVE_FLOOR * self_dots[last]) / (change_norm + EPSILON)
    direction = scale * direction
    for index in range(depth):
        beta = weights[index] * lax.psum(jnp.sum(changes[index] * direction), ("region", "grp"))
        direction = direction + (alphas[index] - beta) * steps_list[index]
    return (transmission - direction, gradient)


def propagator(count):
    index = np.arange(count, dtype=np.int64)
    phase = (index[:, None] * index[None, :] % count).astype(np.float32) * np.float32(TWO_PI / count)
    factor = np.float32(1.0 / math.sqrt(count))
    table = (np.cos(phase) * factor).astype(ml_dtypes.bfloat16).astype(np.float64) + 1j * (
        -np.sin(phase) * factor
    ).astype(ml_dtypes.bfloat16).astype(np.float64)
    wavenumber = (index + count // 2) % count - count // 2
    chirp = np.exp(-1j * (wavenumber * wavenumber % (4 * count)) * (TWO_PI / (4 * count)))
    folded = (table * chirp[None, :]) @ np.conj(table)
    folded = 0.5 * (folded + folded.T)
    real, imag = folded.real, folded.imag
    return np.stack([real, imag - real, real + imag]).astype(ml_dtypes.bfloat16)


def dot(left, right, dims=((1,), (0,))):
    return lax.dot_general(left, right, (dims, ((), ())), preferred_element_type=F32)


def join(sums, reals, imags):
    return sums - imags, sums + reals


def summed(real, imag):
    return (real.astype(F32) + imag.astype(F32)).astype(BF)


def shift_table(rows, columns, row_base, column_base):
    row = lax.broadcasted_iota(jnp.int32, (rows, columns), 0) + row_base
    column = lax.broadcasted_iota(jnp.int32, (rows, columns), 1) + column_base
    return jnp.where(row == column, 1.0, 0.0).astype(BF)


def cut_kernel(pos_ref, tile_ref, out_ref):
    tile_len, frame_len = tile_ref.shape[2], out_ref.shape[2]
    table = shift_table(tile_len, frame_len, 0, pos_ref[0, 0])
    for part in range(2):
        out_ref[part] = dot(tile_ref[part].astype(BF), table).astype(BF)


def probe_kernel(place_ref, all_ref, q0_ref, q1_ref, q2_ref, q3a_ref, q3b_ref, probe_ref, sem):
    core, place, line, half = (place_ref[index] for index in range(4))
    chunk = all_ref.shape[2]

    def rows_of(step):
        return pl.ds(pl.multiple_of(lax.bitwise_xor(place, step) * chunk, chunk), chunk)

    copies = [
        pltpu.make_async_copy(
            all_ref.at[part, 4 * core + 2 * half + mode], probe_ref.at[part, mode, rows_of(0), :], sem.at[part, mode]
        )
        for part in range(2)
        for mode in range(2)
    ]
    for copy in copies:
        copy.start()
    cut = q3a_ref.shape[0]
    for turn, ref in ((0, q0_ref), (1, q1_ref), (2, q2_ref), (3, None)):
        combo = lax.bitwise_xor(line, turn)
        part, mode = lax.rem(combo, 2), lax.div(combo, 2)
        for step in range(1, 4):
            start = (step - 1) * chunk
            if ref is not None:
                value = ref[start : start + chunk]
            elif start + chunk <= cut:
                value = q3a_ref[start : start + chunk]
            elif start >= cut:
                value = q3b_ref[start - cut : start - cut + chunk]
            else:
                value = jnp.concatenate([q3a_ref[start:cut], q3b_ref[: start + chunk - cut]], axis=0)
            probe_ref[part, mode, rows_of(step), :] = value
    for copy in copies:
        copy.wait()


def forward_kernel(
    place_ref, own_ref, side_ref, mate_own_ref, mate_side_ref, probe_ref, measured_ref,
    right_ref, turned_ref, far_ref, send_ref, tile, window_ref, wave, total,
):
    core, half = place_ref[0], place_ref[3]
    chunk, frame_len = measured_ref.shape
    piece_len = own_ref.shape[1]
    piece = 2 * core + half
    for step, ref in enumerate((own_ref, side_ref, mate_own_ref, mate_side_ref)):
        base = pl.multiple_of(lax.bitwise_xor(piece, step) * piece_len, piece_len)
        for part in range(2):
            tile[part, pl.ds(base, piece_len), :] = ref[part]
    column = place_ref[4]
    table = shift_table(tile.shape[1], frame_len, 0, column)
    for part in range(2):
        window_ref[part] = dot(tile[part], table, ((0,), (0,))).astype(BF)

    block = frame_len // 2
    for mode in range(2):
        rows = slice(mode * frame_len, (mode + 1) * frame_len)
        pr, pi = probe_ref[0, mode].astype(F32), probe_ref[1, mode].astype(F32)
        wr, wi = window_ref[0].astype(F32), window_ref[1].astype(F32)
        real, imag = (pr * wr - pi * wi).astype(BF), (pr * wi + pi * wr).astype(BF)
        wave[0, rows], wave[1, rows], wave[2, rows] = summed(real, imag), real, imag
    for cell in range(2):
        columns = slice(cell * block, (cell + 1) * block)
        real, imag = join(*(dot(wave[index], right_ref[index, :, columns]) for index in range(3)))
        real, imag = real.astype(BF), imag.astype(BF)
        total_part = summed(real, imag)
        for mode in range(2):
            rows = slice(mode * frame_len, (mode + 1) * frame_len)
            for index, value in enumerate((total_part, real, imag)):
                turned_ref[mode, cell, index] = value[rows]
    far_columns(1 - core, turned_ref, right_ref, far_ref, total)
    subtract(core, half, 1 - core, measured_ref, total)
    send_ref[...] = total[...].astype(BF)


def far_columns(cell, turned_ref, right_ref, far_ref, total):
    frame_len = total.shape[0]
    power = 0.0
    for mode in range(2):
        real, imag = join(*(dot(right_ref[index], turned_ref[mode, cell, index]) for index in range(3)))
        real, imag = real.astype(BF), imag.astype(BF)
        far_ref[mode, 0] = real
        far_ref[mode, 1] = imag
        real, imag = real.astype(F32), imag.astype(F32)
        power = power + (real * real + imag * imag)
    total[...] = power


def subtract(core, half, cell, measured_ref, total):
    chunk, block = measured_ref.shape[0], total.shape[1]
    rows = pl.ds(pl.multiple_of((2 * core + half) * chunk, chunk), chunk)
    wanted = jnp.where(cell == 0, measured_ref[:, :block], measured_ref[:, block:])
    total[rows, :] = total[rows, :] - wanted.astype(F32)


def rest_kernel(place_ref, turned_ref, measured_ref, right_ref, far_ref, total):
    core, half = place_ref[0], place_ref[3]
    far_columns(core, turned_ref, right_ref, far_ref, total)
    subtract(core, half, core, measured_ref, total)


def left_columns(misfit, far_ref, right_ref, store):
    for mode in range(2):
        real = (misfit * far_ref[mode, 0].astype(F32)).astype(BF)
        imag = (-misfit * far_ref[mode, 1].astype(F32)).astype(BF)
        pieces = (summed(real, imag), real, imag)
        real, imag = join(*(dot(right_ref[index], value) for index, value in enumerate(pieces)))
        real, imag = real.astype(BF), imag.astype(BF)
        for index, value in enumerate((summed(real, imag), real, imag)):
            store(mode, index, value)


def own_kernel(far_ref, mine_ref, right_ref, out_ref):
    frame_len = mine_ref.shape[0]

    def store(mode, part, value):
        out_ref[part, mode * frame_len : (mode + 1) * frame_len, :] = value

    left_columns(mine_ref[...], far_ref, right_ref, store)


def backward_kernel(
    place_ref, far_ref, probe_ref, mates_ref, own_ref, right_ref,
    send_ref, side_ref, keep_ref, turned, grad, table,
):
    core, half = place_ref[0], place_ref[3]
    column = place_ref[4]
    frame_len, block = mates_ref.shape
    piece_len = keep_ref.shape[1]

    def lanes(cell):
        return pl.ds(pl.multiple_of(cell * block, block), block)

    def store(mode, index, value):
        turned[index, mode * frame_len : (mode + 1) * frame_len, lanes(1 - core)] = value

    left_columns(mates_ref[...].astype(F32), far_ref, right_ref, store)
    for index in range(3):
        turned[index, :, lanes(core)] = own_ref[index]
    for cell in range(2):
        columns = slice(cell * block, (cell + 1) * block)
        back = join(*(dot(turned[index], right_ref[index, :, columns]) for index in range(3)))
        real, imag = 0.0, 0.0
        for mode in range(2):
            br, bi = (value[mode * frame_len : (mode + 1) * frame_len] for value in back)
            pr, pi = probe_ref[0, mode, :, columns].astype(F32), probe_ref[1, mode, :, columns].astype(F32)
            real = real + (pr * br - pi * bi)
            imag = imag + (pr * bi + pi * br)
        grad[0, :, columns] = (4.0 * real).astype(BF)
        grad[1, :, columns] = (-4.0 * imag).astype(BF)

    slots = [(1 - core, 1), (1 - core, 0), (core, 1), (core, 0)]
    for index, (pair, flip) in enumerate(slots):
        base = (2 * pair + lax.bitwise_xor(half, flip)) * piece_len
        table[index * piece_len : (index + 1) * piece_len, :] = shift_table(piece_len, frame_len, base, column)
    for part in range(2):
        value = dot(table[...], grad[part], ((1,), (1,))).astype(BF)
        send_ref[0, part] = value[:piece_len]
        send_ref[1, part] = value[piece_len : 2 * piece_len]
        side_ref[part] = value[2 * piece_len : 3 * piece_len]
        keep_ref[part] = value[3 * piece_len :]


PAIRS = [("sy", i, j) for j in range(HIST - 1) for i in range(HIST)]
PAIRS += [("ss", i, i) for i in range(HIST)]
PAIRS += [("yy", i, j) for j in range(HIST - 1) for i in range(j + 1)]
OLD_PAIRS = len(PAIRS)
PAIRS += [("sy", i, HIST - 1) for i in range(HIST)]
PAIRS += [("yy", i, HIST - 1) for i in range(HIST)]
PAIRS += [("sg", i, i) for i in range(HIST)]
PAIRS += [("yg", i, i) for i in range(HIST)]
SLOT = {pair: index for index, pair in enumerate(PAIRS)}


def folded(value):
    parts, rows, columns = value.shape
    total = jnp.sum(value.reshape(parts * rows // 8, 8, columns), axis=0)
    return sum(total[:, start : start + LANES] for start in range(0, columns, LANES))


def add_products(sums, first, slots, vectors):
    for slot, pair in slots:
        kind, i, j = pair
        left = vectors[kind[0]][i]
        right = vectors["g"][0] if kind[1] == "g" else vectors[kind[1]][j]
        value = folded(left * right)
        sums[slot] = value if first else sums[slot] + value


def lane_row(sums, count):
    rows = [jnp.sum(sums[slot], axis=0, keepdims=True) for slot in range(count)]
    square = jnp.concatenate(rows + [jnp.zeros((LANES - count, LANES), F32)], axis=0)
    return jnp.sum(square.T, axis=0, keepdims=True)


BLOCK = 32


def column_blocks(ref):
    return range(0, ref.shape[-2], BLOCK)


def old_kernel(steps_ref, changes_ref, out_ref, sums):
    for start in column_blocks(steps_ref):
        columns = slice(start, start + BLOCK)
        vectors = {
            "s": [steps_ref[index, :, columns] for index in range(HIST)],
            "y": [changes_ref[index, :, columns] for index in range(HIST - 1)],
        }
        add_products(sums, start == 0, enumerate(PAIRS[:OLD_PAIRS]), vectors)
    out_ref[...] = lane_row(sums, OLD_PAIRS)


def gradient_kernel(
    pos_ref, data_ref, transmission_ref, old_ref, steps_ref, changes_ref, row_ref, gradient_ref, out_ref, sums
):
    table = shift_table(data_ref.shape[2], transmission_ref.shape[2], pos_ref[0, 0], 0)
    parts, piece_len, frame_len = data_ref.shape
    placed = dot(data_ref[...].reshape(parts * piece_len, frame_len), table)
    gradient_ref[...] = placed.reshape(transmission_ref.shape) + TIKHONOV * transmission_ref[...]
    for start in column_blocks(transmission_ref):
        columns = slice(start, start + BLOCK)
        gradient = gradient_ref[:, columns]
        vectors = {
            "s": [steps_ref[index, :, columns] for index in range(HIST)],
            "y": [changes_ref[index, :, columns] for index in range(HIST - 1)]
            + [gradient - old_ref[:, columns]],
            "g": [gradient],
        }
        add_products(sums, start == 0, enumerate(PAIRS[OLD_PAIRS:]), vectors)
    fresh = pltpu.roll(lane_row(sums, len(PAIRS) - OLD_PAIRS), OLD_PAIRS, 1)
    out_ref[...] = jnp.broadcast_to(fresh + row_ref[...], out_ref.shape)


def update_kernel(
    rows_ref, transmission_ref, gradient_ref, old_ref, steps_ref, changes_ref, updated_ref, copy_ref, out_ref, sem
):
    copies = [pltpu.make_async_copy(gradient_ref, copy_ref, sem.at[2])]
    copies[0].start()
    row = jnp.sum(rows_ref[...], axis=0, keepdims=True)
    lane = lax.broadcasted_iota(jnp.int32, row.shape, 1)

    def get(kind, i, j):
        if kind == "yy" and i > j:
            i, j = j, i
        picked = jnp.where(lane == SLOT[(kind, i, j)], row, 0.0)
        return jnp.broadcast_to(jnp.sum(picked, axis=1, keepdims=True), row.shape)

    last = HIST - 1
    floors = [
        jnp.maximum(get("sy", index, index), CURVE_FLOOR * get("ss", index, index)) for index in range(HIST)
    ]
    weights = [1.0 / floor for floor in floors]
    alphas = [None] * HIST
    for index in reversed(range(HIST)):
        value = get("sg", index, index)
        for later in range(index + 1, HIST):
            value = value - alphas[later] * get("sy", index, later)
        alphas[index] = weights[index] * value
    scale = floors[last] / (get("yy", last, last) + EPSILON)
    moves = []
    for index in range(HIST):
        value = get("yg", index, index)
        for other in range(HIST):
            value = value - alphas[other] * get("yy", index, other)
        value = scale * value
        for before in range(index):
            value = value + moves[before] * get("sy", before, index)
        moves.append(alphas[index] - weights[index] * value)
    repeat = out_ref.shape[-1] // LANES
    wide = lambda value: jnp.concatenate([value] * repeat, axis=1)
    scale_row = wide(scale)
    change_rows = [wide(-scale * alpha) for alpha in alphas]
    step_rows = [wide(move) for move in moves]
    for part in range(2):
        for start in column_blocks(out_ref):
            columns = slice(start, start + BLOCK)
            gradient = gradient_ref[part, columns]
            total = scale_row * gradient + change_rows[last] * (gradient - old_ref[part, columns])
            for index in range(HIST - 1):
                total = total + change_rows[index] * changes_ref[index, part, columns]
            for index in range(HIST):
                total = total + step_rows[index] * steps_ref[index, part, columns]
            out_ref[part, columns] = transmission_ref[part, columns] - total
        copies.append(pltpu.make_async_copy(out_ref.at[part], updated_ref.at[part], sem.at[part]))
        copies[-1].start()
    for copy in copies:
        copy.wait()


def call(body, outs, scratch=(), limit=48, smem=(), far=(), count=0, cost=None, out_space=pltpu.VMEM):
    space = lambda index: pltpu.SMEM if index in smem else pl.ANY if index in far else pltpu.VMEM
    specs = [pl.BlockSpec(memory_space=space(index)) for index in range(count)]
    return pl.pallas_call(
        body,
        out_shape=outs,
        in_specs=specs,
        out_specs=jax.tree.map(lambda _: pl.BlockSpec(memory_space=out_space), outs),
        scratch_shapes=list(scratch),
        compiler_params=pltpu.CompilerParams(vmem_limit_bytes=limit * MIB),
        cost_estimate=cost,
    )


def cost(flops, moved):
    return pl.CostEstimate(flops=int(flops), bytes_accessed=int(moved), transcendentals=0)


def home(region, member):
    return (region, member) if at_home(region, member) else (region ^ 1, member ^ 2)


def at_home(region, member):
    return region % 2 == member // 2


def away(region, member):
    return not at_home(region, member)


def fast(mesh, transmission, probe, measured, positions, past_steps, past_changes, old_gradient):
    regions, members = mesh.shape["region"], mesh.shape["grp"]
    barrier = lax.optimization_barrier

    def send(value, target, chosen=lambda region, member: True):
        pairs = []
        for region in range(regions):
            for member in range(members):
                if chosen(region, member):
                    to_region, to_member = target(region, member)
                    pairs.append((region * members + member, to_region * members + to_member))
        return lax.ppermute(value, AXES, pairs)

    near = lambda region, member: (region, member ^ 1)
    far = lambda region, member: (region, member ^ 2)
    cross = lambda region, member: (region, member ^ 3)
    mate = lambda region, member: (region ^ 1, member)
    along_x = lambda region, member: (region ^ 2, member)
    along_y = lambda region, member: (region ^ 4, member)
    diagonal = lambda region, member: (region ^ 6, member)
    home_near = lambda region, member: (region ^ 1, member ^ 3)

    region, member = lax.axis_index("region"), lax.axis_index("grp")
    core, half, line = region & 1, member & 1, (region >> 1) & 3
    is_home = core == (member >> 1)
    chunk, frame_len = probe.shape[2], probe.shape[3]
    piece_len, tile_len = transmission.shape[1], transmission.shape[2]
    size = jax.ShapeDtypeStruct

    part, which = line & 1, line >> 1
    base = 4 * core + 2 * half
    other_base = 4 * core + 2 * (1 - half)

    def block(mode):
        return lax.dynamic_slice(probe, (part, mode, 0, 0), (1, 1, chunk, frame_len)).reshape(chunk, frame_len)

    same_block, flip_block = block(base + which), block(other_base + which)
    from_far, from_near = send(same_block, far), send(flip_block, near)
    from_cross = send(flip_block, cross)
    mate_positions = send(positions, mate)
    piece = call(cut_kernel, size((2, piece_len, frame_len), BF), count=2, smem=(0,), limit=16)(
        positions, transmission
    )
    measured_low, from_near = barrier((measured[0].astype(BF), from_near))
    target = send(measured_low, home)
    q0 = jnp.concatenate([from_near, from_far, from_cross], axis=0)
    column = jnp.where(is_home, positions[0, 1], mate_positions[0, 1])
    place = jnp.stack([core, member, line, half, column]).astype(jnp.int32)
    piece, place, target, q0 = barrier((piece, place, target, q0))
    q1, q2 = send(q0, along_x), send(q0, along_y)
    own = send(piece, home)
    beside = send(piece, near, at_home)
    further = send(piece, home_near, away)
    cut = q0.shape[0] // 2
    q3a, q3b = send(q2[:cut], along_x), send(q1[cut:], along_y)
    own, beside, further, q3a, q3b = barrier((own, beside, further, q3a, q3b))
    side = jnp.where(is_home, beside, further)
    mate_own, mate_side = send(own, mate), send(side, mate)
    whole_probe = call(
        probe_kernel,
        size((2, 2, frame_len, frame_len), BF),
        [pltpu.SemaphoreType.DMA((2, 2))],
        count=7,
        smem=(0,),
        far=(1,),
        limit=16,
    )(place, probe, q0, q1, q2, q3a, q3b)

    right = jnp.asarray(propagator(frame_len))
    double = 2 * frame_len
    flops = 2 * 2 * double**3
    half_len = frame_len // 2
    half_field = size((2, 2, frame_len, half_len), BF)
    turned, mates_far, sent = call(
        forward_kernel,
        (size((2, 2, 3, frame_len, half_len), BF), half_field, size((frame_len, half_len), BF)),
        [
            pltpu.VMEM((2, tile_len, frame_len), BF),
            pltpu.VMEM((2, frame_len, frame_len), BF),
            pltpu.VMEM((3, double, frame_len), BF),
            pltpu.VMEM((frame_len, half_len), F32),
        ],
        count=8,
        smem=(0,),
        limit=24,
        cost=cost(3 * flops // 4, 16 * MIB),
    )(place, own, side, mate_own, mate_side, whole_probe, target, right)
    met = send(sent, mate)
    own_far, kept = call(
        rest_kernel,
        (half_field, size((frame_len, half_len), F32)),
        count=4,
        smem=(0,),
        limit=24,
        cost=cost(flops // 4, 4 * MIB),
    )(place, turned, target, right)

    chip = kept + met.astype(F32)
    misfit = chip + send(chip.astype(BF), near).astype(F32)
    mates_misfit = send(misfit.astype(BF), mate)
    own_left = call(
        own_kernel,
        size((3, double, half_len), BF),
        count=3,
        limit=24,
        cost=cost(flops // 4, 4 * MIB),
    )(own_far, misfit, right)

    piece_shape = size((2, piece_len, frame_len), BF)
    sent, kept_side, kept = call(
        backward_kernel,
        (size((2, 2, piece_len, frame_len), BF), piece_shape, piece_shape),
        [
            pltpu.VMEM((3, double, frame_len), BF),
            pltpu.VMEM((2, frame_len, frame_len), BF),
            pltpu.VMEM((4 * piece_len, frame_len), BF),
        ],
        count=6,
        smem=(0,),
        limit=24,
        cost=cost(3 * flops // 4, 12 * MIB),
    )(place, mates_far, whole_probe, mates_misfit, own_left, right)
    met = send(sent, mate)
    add = lambda a, b: (a.astype(F32) + b.astype(F32)).astype(BF)
    kept_side, kept = add(kept_side, met[0]), add(kept, met[1])
    first, second = send(kept, home, away), send(kept_side, home_near, away)
    beside = send(kept_side, near, at_home)
    data = jnp.where(is_home, add(kept, beside), add(first, second))

    devices = regions * members
    moved = 4 * 2 * piece_len * tile_len
    old_row = call(
        old_kernel,
        size((1, LANES), F32),
        [pltpu.VMEM((OLD_PAIRS, 8, LANES), F32)],
        count=2,
        limit=16,
        cost=cost(22 * moved, 7 * moved),
    )(past_steps, past_changes)
    gradient, row = call(
        gradient_kernel,
        (size(transmission.shape, F32), size((devices, LANES), F32)),
        [pltpu.VMEM((len(PAIRS) - OLD_PAIRS, 8, LANES), F32)],
        count=7,
        smem=(0,),
        limit=16,
        cost=cost(16 * moved, 10 * moved),
    )(positions, data, transmission, old_gradient, past_steps, past_changes, old_row)
    all_rows = lax.all_to_all(
        row.reshape(devices, 1, LANES), AXES, split_axis=0, concat_axis=0, tiled=True
    ).reshape(devices, LANES)
    return call(
        update_kernel,
        (size(transmission.shape, F32), size(transmission.shape, F32)),
        [pltpu.VMEM(transmission.shape, F32), pltpu.SemaphoreType.DMA((3,))],
        count=6,
        limit=16,
        cost=cost(10 * moved, 11 * moved),
        out_space=pl.ANY,
    )(all_rows, transmission, gradient, old_gradient, past_steps, past_changes)


def solution(mesh):
    split = mesh.shape["grp"] == 4 and mesh.shape["region"] == 8

    def shards(*args):
        probe, positions, past_steps = args[1], args[3], args[4]
        sized = probe.shape[1] == 8 and positions.shape[0] == 1 and past_steps.shape[0] == HIST
        if split and sized:
            return fast(mesh, *args)
        return general(*args)

    return jax.shard_map(
        shards,
        mesh=mesh,
        in_specs=(
            P(None, "grp", "region"),
            P(None, None, "grp", None),
            P("region", "grp", None),
            P("region", None),
            P(None, None, "grp", "region"),
            P(None, None, "grp", "region"),
            P(None, "grp", "region"),
        ),
        out_specs=(P(None, "grp", "region"), P(None, "grp", "region")),
        check_vma=False,
    )
```

```python
import math

import jax
import jax.numpy as jnp
import ml_dtypes
import numpy as np
from jax import lax
from jax.experimental import pallas as pl
from jax.experimental.pallas import tpu as pltpu
from jax.sharding import PartitionSpec as P

TWO_PI = 2.0 * math.pi
CURVE_FLOOR = 0.25
TIKHONOV = 0.5
EPSILON = 1e-06
BF = jnp.bfloat16
F32 = jnp.float32
AXES = ("region", "grp")
LANES = 128
MIB = 1 << 20
HIST = 4


def dft_tables(count):
    index = jnp.arange(count, dtype=jnp.int32)
    phase = (index[:, None] * index[None, :] % count).astype(jnp.float32) * (TWO_PI / count)
    factor = 1.0 / math.sqrt(count)
    return (
        (jnp.cos(phase) * factor).astype(jnp.bfloat16),
        (-jnp.sin(phase) * factor).astype(jnp.bfloat16),
    )


def chirp_table(count):
    index = jnp.arange(count, dtype=jnp.int32)
    wavenumber = (index + count // 2) % count - count // 2
    phase = (wavenumber * wavenumber % (4 * count)).astype(jnp.float32) * (TWO_PI / (4 * count))
    return (jnp.cos(phase), -jnp.sin(phase))


def rotate(real_part, imag_part, turn_real, turn_imag):
    return (
        real_part * turn_real - imag_part * turn_imag,
        real_part * turn_imag + imag_part * turn_real,
    )


def narrow(pair):
    return jnp.stack([pair[0], pair[1]]).astype(jnp.bfloat16)


def right_product(field, matrix_real, matrix_imag):

    def single(left, right):
        return jnp.einsum("...k,kj->...j", left, right, preferred_element_type=jnp.float32)

    return (
        single(field[0], matrix_real) - single(field[1], matrix_imag),
        single(field[0], matrix_imag) + single(field[1], matrix_real),
    )


def left_product(matrix_real, matrix_imag, field):

    def single(left, right):
        return jnp.einsum("jk,...kc->...jc", left, right, preferred_element_type=jnp.float32)

    return (
        single(matrix_real, field[0]) - single(matrix_imag, field[1]),
        single(matrix_real, field[1]) + single(matrix_imag, field[0]),
    )


def general(transmission, probe, measured, positions, past_steps, past_changes, old_gradient):
    member = lax.axis_index("grp")
    frame_len = probe.shape[3]
    rows_here = probe.shape[2]
    tile_len = transmission.shape[2]
    anchor = jnp.zeros((), jnp.int32)
    fwd_real, fwd_imag = dft_tables(frame_len)
    inv_imag = -fwd_imag
    chirp_real, chirp_imag = chirp_table(frame_len)
    probe_wide = probe.astype(jnp.float32)
    tile = lax.all_gather(transmission.astype(jnp.bfloat16), "grp", axis=1, tiled=True)
    frame = 0
    first_row = positions[frame, 0] + member * rows_here
    window = jnp.swapaxes(
        lax.dynamic_slice(
            tile, (anchor, positions[frame, 1], first_row), (2, frame_len, rows_here)
        ),
        1,
        2,
    ).astype(jnp.float32)
    wave = narrow(rotate(probe_wide[0], probe_wide[1], window[0], window[1]))
    section = narrow(rotate(*right_product(wave, fwd_real, fwd_imag), chirp_real, chirp_imag))
    spread = narrow(right_product(section, fwd_real, inv_imag))
    section = narrow(
        rotate(
            *left_product(
                fwd_real,
                fwd_imag,
                lax.all_to_all(spread, "grp", split_axis=3, concat_axis=2, tiled=True),
            ),
            chirp_real[:, None],
            chirp_imag[:, None]
        )
    )
    far_field = narrow(left_product(fwd_real, inv_imag, section))
    near_rows = lax.all_to_all(far_field, "grp", split_axis=2, concat_axis=3, tiled=True)
    field_wide = near_rows.astype(jnp.float32)
    misfit = (
        jnp.sum(field_wide[0] * field_wide[0] + field_wide[1] * field_wide[1], axis=0)
        - measured[frame]
    )
    weighted = (misfit * field_wide).astype(jnp.bfloat16)
    section = narrow(
        rotate(
            *left_product(
                fwd_real,
                fwd_imag,
                lax.all_to_all(weighted, "grp", split_axis=3, concat_axis=2, tiled=True),
            ),
            chirp_real[:, None],
            -chirp_imag[:, None]
        )
    )
    returned = narrow(left_product(fwd_real, inv_imag, section))
    section = narrow(
        rotate(
            *right_product(
                lax.all_to_all(returned, "grp", split_axis=2, concat_axis=3, tiled=True),
                fwd_real,
                fwd_imag,
            ),
            chirp_real,
            -chirp_imag
        )
    )
    back_wave = jnp.stack(right_product(section, fwd_real, inv_imag))
    grad_real = 4.0 * jnp.sum(probe_wide[0] * back_wave[0] + probe_wide[1] * back_wave[1], axis=0)
    grad_imag = 4.0 * jnp.sum(probe_wide[0] * back_wave[1] - probe_wide[1] * back_wave[0], axis=0)
    frame_grads = [jnp.stack([grad_real, grad_imag])]
    scattered = jnp.zeros((2, tile_len, tile_len), jnp.float32)
    frame = 0
    corner = (anchor, positions[frame, 1], positions[frame, 0] + member * rows_here)
    scattered = lax.dynamic_update_slice(scattered, jnp.swapaxes(frame_grads[frame], 1, 2), corner)
    data_grad = lax.psum_scatter(
        scattered.astype(jnp.bfloat16), "grp", scatter_dimension=1, tiled=True
    ).astype(jnp.float32)
    gradient = data_grad + TIKHONOV * transmission
    depth = past_steps.shape[0]
    last = depth - 1
    change_new = gradient - old_gradient
    steps_list = [past_steps[index] for index in range(depth)]
    changes = [past_changes[index] for index in range(depth - 1)] + [change_new]
    alphas = [None] * depth
    curvature, self_dots, change_norm = lax.psum(
        (
            jnp.stack([jnp.sum(steps_list[index] * changes[index]) for index in range(depth)]),
            jnp.sum(past_steps * past_steps, axis=(1, 2, 3)),
            jnp.sum(change_new * change_new),
        ),
        ("region", "grp"),
    )
    weights = [
        1.0 / jnp.maximum(curvature[index], CURVE_FLOOR * self_dots[index])
        for index in range(depth)
    ]
    direction = gradient
    for index in reversed(range(depth)):
        alphas[index] = weights[index] * lax.psum(
            jnp.sum(steps_list[index] * direction), ("region", "grp")
        )
        direction = direction - alphas[index] * changes[index]
    scale = jnp.maximum(curvature[last], CURVE_FLOOR * self_dots[last]) / (change_norm + EPSILON)
    direction = scale * direction
    for index in range(depth):
        beta = weights[index] * lax.psum(jnp.sum(changes[index] * direction), ("region", "grp"))
        direction = direction + (alphas[index] - beta) * steps_list[index]
    return (transmission - direction, gradient)


def propagator(count):
    index = np.arange(count, dtype=np.int64)
    phase = (index[:, None] * index[None, :] % count).astype(np.float32) * np.float32(TWO_PI / count)
    factor = np.float32(1.0 / math.sqrt(count))
    table = (np.cos(phase) * factor).astype(ml_dtypes.bfloat16).astype(np.float64) + 1j * (
        -np.sin(phase) * factor
    ).astype(ml_dtypes.bfloat16).astype(np.float64)
    wavenumber = (index + count // 2) % count - count // 2
    chirp = np.exp(-1j * (wavenumber * wavenumber % (4 * count)) * (TWO_PI / (4 * count)))
    folded = (table * chirp[None, :]) @ np.conj(table)
    folded = 0.5 * (folded + folded.T)
    real, imag = folded.real, folded.imag
    return np.stack([real, imag - real, real + imag]).astype(ml_dtypes.bfloat16)


def dot(left, right, dims=((1,), (0,))):
    return lax.dot_general(left, right, (dims, ((), ())), preferred_element_type=F32)


def join(sums, reals, imags):
    return sums - imags, sums + reals


def summed(real, imag):
    return (real.astype(F32) + imag.astype(F32)).astype(BF)


def shift_table(rows, columns, row_base, column_base):
    row = lax.broadcasted_iota(jnp.int32, (rows, columns), 0) + row_base
    column = lax.broadcasted_iota(jnp.int32, (rows, columns), 1) + column_base
    return jnp.where(row == column, 1.0, 0.0).astype(BF)


def cut_kernel(pos_ref, tile_ref, out_ref):
    tile_len, frame_len = tile_ref.shape[2], out_ref.shape[2]
    table = shift_table(tile_len, frame_len, 0, pos_ref[0, 0])
    for part in range(2):
        out_ref[part] = dot(tile_ref[part].astype(BF), table).astype(BF)


def probe_kernel(place_ref, all_ref, q0_ref, q1_ref, q2_ref, q3a_ref, q3b_ref, probe_ref, sem):
    core, place, line, half = (place_ref[index] for index in range(4))
    chunk = all_ref.shape[2]

    def rows_of(step):
        return pl.ds(pl.multiple_of(lax.bitwise_xor(place, step) * chunk, chunk), chunk)

    copies = [
        pltpu.make_async_copy(
            all_ref.at[part, 4 * core + 2 * half + mode], probe_ref.at[part, mode, rows_of(0), :], sem.at[part, mode]
        )
        for part in range(2)
        for mode in range(2)
    ]
    for copy in copies:
        copy.start()
    cut = q3a_ref.shape[0]
    for turn, ref in ((0, q0_ref), (1, q1_ref), (2, q2_ref), (3, None)):
        combo = lax.bitwise_xor(line, turn)
        part, mode = lax.rem(combo, 2), lax.div(combo, 2)
        for step in range(1, 4):
            start = (step - 1) * chunk
            if ref is not None:
                value = ref[start : start + chunk]
            elif start + chunk <= cut:
                value = q3a_ref[start : start + chunk]
            elif start >= cut:
                value = q3b_ref[start - cut : start - cut + chunk]
            else:
                value = jnp.concatenate([q3a_ref[start:cut], q3b_ref[: start + chunk - cut]], axis=0)
            probe_ref[part, mode, rows_of(step), :] = value
    for copy in copies:
        copy.wait()


def forward_kernel(
    place_ref, own_ref, side_ref, mate_own_ref, mate_side_ref, probe_ref, measured_ref,
    right_ref, turned_ref, far_ref, send_ref, tile, window_ref, wave, total,
):
    core, half = place_ref[0], place_ref[3]
    chunk, frame_len = measured_ref.shape
    piece_len = own_ref.shape[1]
    piece = 2 * core + half
    for step, ref in enumerate((own_ref, side_ref, mate_own_ref, mate_side_ref)):
        base = pl.multiple_of(lax.bitwise_xor(piece, step) * piece_len, piece_len)
        for part in range(2):
            tile[part, pl.ds(base, piece_len), :] = ref[part]
    column = place_ref[4]
    table = shift_table(tile.shape[1], frame_len, 0, column)
    for part in range(2):
        window_ref[part] = dot(tile[part], table, ((0,), (0,))).astype(BF)

    block = frame_len // 2
    for mode in range(2):
        rows = slice(mode * frame_len, (mode + 1) * frame_len)
        pr, pi = probe_ref[0, mode].astype(F32), probe_ref[1, mode].astype(F32)
        wr, wi = window_ref[0].astype(F32), window_ref[1].astype(F32)
        real, imag = (pr * wr - pi * wi).astype(BF), (pr * wi + pi * wr).astype(BF)
        wave[0, rows], wave[1, rows], wave[2, rows] = summed(real, imag), real, imag
    for cell in range(2):
        columns = slice(cell * block, (cell + 1) * block)
        real, imag = join(*(dot(wave[index], right_ref[index, :, columns]) for index in range(3)))
        real, imag = real.astype(BF), imag.astype(BF)
        total_part = summed(real, imag)
        for mode in range(2):
            rows = slice(mode * frame_len, (mode + 1) * frame_len)
            for index, value in enumerate((total_part, real, imag)):
                turned_ref[mode, cell, index] = value[rows]
    far_columns(1 - core, turned_ref, right_ref, far_ref, total)
    subtract(core, half, 1 - core, measured_ref, total)
    send_ref[...] = total[...].astype(BF)


def far_columns(cell, turned_ref, right_ref, far_ref, total):
    frame_len = total.shape[0]
    power = 0.0
    for mode in range(2):
        real, imag = join(*(dot(right_ref[index], turned_ref[mode, cell, index]) for index in range(3)))
        real, imag = real.astype(BF), imag.astype(BF)
        far_ref[mode, 0] = real
        far_ref[mode, 1] = imag
        real, imag = real.astype(F32), imag.astype(F32)
        power = power + (real * real + imag * imag)
    total[...] = power


def subtract(core, half, cell, measured_ref, total):
    chunk, block = measured_ref.shape[0], total.shape[1]
    rows = pl.ds(pl.multiple_of((2 * core + half) * chunk, chunk), chunk)
    wanted = jnp.where(cell == 0, measured_ref[:, :block], measured_ref[:, block:])
    total[rows, :] = total[rows, :] - wanted.astype(F32)


def rest_kernel(place_ref, turned_ref, measured_ref, right_ref, far_ref, total):
    core, half = place_ref[0], place_ref[3]
    far_columns(core, turned_ref, right_ref, far_ref, total)
    subtract(core, half, core, measured_ref, total)


def left_columns(misfit, far_ref, right_ref, store):
    for mode in range(2):
        real = (misfit * far_ref[mode, 0].astype(F32)).astype(BF)
        imag = (-misfit * far_ref[mode, 1].astype(F32)).astype(BF)
        pieces = (summed(real, imag), real, imag)
        real, imag = join(*(dot(right_ref[index], value) for index, value in enumerate(pieces)))
        real, imag = real.astype(BF), imag.astype(BF)
        for index, value in enumerate((summed(real, imag), real, imag)):
            store(mode, index, value)


def own_kernel(far_ref, mine_ref, right_ref, out_ref):
    frame_len = mine_ref.shape[0]

    def store(mode, part, value):
        out_ref[part, mode * frame_len : (mode + 1) * frame_len, :] = value

    left_columns(mine_ref[...], far_ref, right_ref, store)


def backward_kernel(
    place_ref, far_ref, probe_ref, mates_ref, own_ref, right_ref,
    send_ref, side_ref, keep_ref, turned, grad, table,
):
    core, half = place_ref[0], place_ref[3]
    column = place_ref[4]
    frame_len, block = mates_ref.shape
    piece_len = keep_ref.shape[1]

    def lanes(cell):
        return pl.ds(pl.multiple_of(cell * block, block), block)

    def store(mode, index, value):
        turned[index, mode * frame_len : (mode + 1) * frame_len, lanes(1 - core)] = value

    left_columns(mates_ref[...].astype(F32), far_ref, right_ref, store)
    for index in range(3):
        turned[index, :, lanes(core)] = own_ref[index]
    for cell in range(2):
        columns = slice(cell * block, (cell + 1) * block)
        back = join(*(dot(turned[index], right_ref[index, :, columns]) for index in range(3)))
        real, imag = 0.0, 0.0
        for mode in range(2):
            br, bi = (value[mode * frame_len : (mode + 1) * frame_len] for value in back)
            pr, pi = probe_ref[0, mode, :, columns].astype(F32), probe_ref[1, mode, :, columns].astype(F32)
            real = real + (pr * br - pi * bi)
            imag = imag + (pr * bi + pi * br)
        grad[0, :, columns] = (4.0 * real).astype(BF)
        grad[1, :, columns] = (-4.0 * imag).astype(BF)

    slots = [(1 - core, 1), (1 - core, 0), (core, 1), (core, 0)]
    for index, (pair, flip) in enumerate(slots):
        base = (2 * pair + lax.bitwise_xor(half, flip)) * piece_len
        table[index * piece_len : (index + 1) * piece_len, :] = shift_table(piece_len, frame_len, base, column)
    for part in range(2):
        value = dot(table[...], grad[part], ((1,), (1,))).astype(BF)
        send_ref[0, part] = value[:piece_len]
        send_ref[1, part] = value[piece_len : 2 * piece_len]
        side_ref[part] = value[2 * piece_len : 3 * piece_len]
        keep_ref[part] = value[3 * piece_len :]


PAIRS = [("sy", i, j) for j in range(HIST - 1) for i in range(HIST)]
PAIRS += [("ss", i, i) for i in range(HIST)]
PAIRS += [("yy", i, j) for j in range(HIST - 1) for i in range(j + 1)]
OLD_PAIRS = len(PAIRS)
PAIRS += [("sy", i, HIST - 1) for i in range(HIST)]
PAIRS += [("yy", i, HIST - 1) for i in range(HIST)]
PAIRS += [("sg", i, i) for i in range(HIST)]
PAIRS += [("yg", i, i) for i in range(HIST)]
SLOT = {pair: index for index, pair in enumerate(PAIRS)}


def folded(value):
    parts, rows, columns = value.shape
    total = jnp.sum(value.reshape(parts * rows // 8, 8, columns), axis=0)
    return sum(total[:, start : start + LANES] for start in range(0, columns, LANES))


def add_products(sums, first, slots, vectors):
    for slot, pair in slots:
        kind, i, j = pair
        left = vectors[kind[0]][i]
        right = vectors["g"][0] if kind[1] == "g" else vectors[kind[1]][j]
        value = folded(left * right)
        sums[slot] = value if first else sums[slot] + value


def lane_row(sums, count):
    rows = [jnp.sum(sums[slot], axis=0, keepdims=True) for slot in range(count)]
    square = jnp.concatenate(rows + [jnp.zeros((LANES - count, LANES), F32)], axis=0)
    return jnp.sum(square.T, axis=0, keepdims=True)


BLOCK = 32


def column_blocks(ref):
    return range(0, ref.shape[-2], BLOCK)


def old_kernel(steps_ref, changes_ref, out_ref, sums):
    for start in column_blocks(steps_ref):
        columns = slice(start, start + BLOCK)
        vectors = {
            "s": [steps_ref[index, :, columns] for index in range(HIST)],
            "y": [changes_ref[index, :, columns] for index in range(HIST - 1)],
        }
        add_products(sums, start == 0, enumerate(PAIRS[:OLD_PAIRS]), vectors)
    out_ref[...] = lane_row(sums, OLD_PAIRS)


def gradient_kernel(
    pos_ref, data_ref, transmission_ref, old_ref, steps_ref, changes_ref, row_ref, gradient_ref, out_ref, sums
):
    table = shift_table(data_ref.shape[2], transmission_ref.shape[2], pos_ref[0, 0], 0)
    parts, piece_len, frame_len = data_ref.shape
    placed = dot(data_ref[...].reshape(parts * piece_len, frame_len), table)
    gradient_ref[...] = placed.reshape(transmission_ref.shape) + TIKHONOV * transmission_ref[...]
    for start in column_blocks(transmission_ref):
        columns = slice(start, start + BLOCK)
        gradient = gradient_ref[:, columns]
        vectors = {
            "s": [steps_ref[index, :, columns] for index in range(HIST)],
            "y": [changes_ref[index, :, columns] for index in range(HIST - 1)]
            + [gradient - old_ref[:, columns]],
            "g": [gradient],
        }
        add_products(sums, start == 0, enumerate(PAIRS[OLD_PAIRS:]), vectors)
    fresh = pltpu.roll(lane_row(sums, len(PAIRS) - OLD_PAIRS), OLD_PAIRS, 1)
    out_ref[...] = jnp.broadcast_to(fresh + row_ref[...], out_ref.shape)


def update_kernel(
    rows_ref, transmission_ref, gradient_ref, old_ref, steps_ref, changes_ref, updated_ref, copy_ref, out_ref, sem
):
    copies = [pltpu.make_async_copy(gradient_ref, copy_ref, sem.at[2])]
    copies[0].start()
    row = jnp.sum(rows_ref[...], axis=0, keepdims=True)
    lane = lax.broadcasted_iota(jnp.int32, row.shape, 1)

    def get(kind, i, j):
        if kind == "yy" and i > j:
            i, j = j, i
        picked = jnp.where(lane == SLOT[(kind, i, j)], row, 0.0)
        return jnp.broadcast_to(jnp.sum(picked, axis=1, keepdims=True), row.shape)

    last = HIST - 1
    floors = [
        jnp.maximum(get("sy", index, index), CURVE_FLOOR * get("ss", index, index)) for index in range(HIST)
    ]
    weights = [1.0 / floor for floor in floors]
    alphas = [None] * HIST
    for index in reversed(range(HIST)):
        value = get("sg", index, index)
        for later in range(index + 1, HIST):
            value = value - alphas[later] * get("sy", index, later)
        alphas[index] = weights[index] * value
    scale = floors[last] / (get("yy", last, last) + EPSILON)
    moves = []
    for index in range(HIST):
        value = get("yg", index, index)
        for other in range(HIST):
            value = value - alphas[other] * get("yy", index, other)
        value = scale * value
        for before in range(index):
            value = value + moves[before] * get("sy", before, index)
        moves.append(alphas[index] - weights[index] * value)
    repeat = out_ref.shape[-1] // LANES
    wide = lambda value: jnp.concatenate([value] * repeat, axis=1)
    scale_row = wide(scale)
    change_rows = [wide(-scale * alpha) for alpha in alphas]
    step_rows = [wide(move) for move in moves]
    for part in range(2):
        for start in column_blocks(out_ref):
            columns = slice(start, start + BLOCK)
            gradient = gradient_ref[part, columns]
            total = scale_row * gradient + change_rows[last] * (gradient - old_ref[part, columns])
            for index in range(HIST - 1):
                total = total + change_rows[index] * changes_ref[index, part, columns]
            for index in range(HIST):
                total = total + step_rows[index] * steps_ref[index, part, columns]
            out_ref[part, columns] = transmission_ref[part, columns] - total
        copies.append(pltpu.make_async_copy(out_ref.at[part], updated_ref.at[part], sem.at[part]))
        copies[-1].start()
    for copy in copies:
        copy.wait()


def call(body, outs, scratch=(), limit=48, smem=(), far=(), count=0, cost=None, out_space=pltpu.VMEM):
    space = lambda index: pltpu.SMEM if index in smem else pl.ANY if index in far else pltpu.VMEM
    specs = [pl.BlockSpec(memory_space=space(index)) for index in range(count)]
    return pl.pallas_call(
        body,
        out_shape=outs,
        in_specs=specs,
        out_specs=jax.tree.map(lambda _: pl.BlockSpec(memory_space=out_space), outs),
        scratch_shapes=list(scratch),
        compiler_params=pltpu.CompilerParams(vmem_limit_bytes=limit * MIB),
        cost_estimate=cost,
    )


def cost(flops, moved):
    return pl.CostEstimate(flops=int(flops), bytes_accessed=int(moved), transcendentals=0)


def home(region, member):
    return (region, member) if at_home(region, member) else (region ^ 1, member ^ 2)


def at_home(region, member):
    return region % 2 == member // 2


def beside(region, member):
    return (region, member ^ 1) if at_home(region, member) else (region ^ 1, member ^ 3)


def fast(mesh, transmission, probe, measured, positions, past_steps, past_changes, old_gradient):
    regions, members = mesh.shape["region"], mesh.shape["grp"]
    barrier = lax.optimization_barrier

    def send(value, target):
        pairs = []
        for region in range(regions):
            for member in range(members):
                to_region, to_member = target(region, member)
                pairs.append((region * members + member, to_region * members + to_member))
        return lax.ppermute(value, AXES, pairs)

    near = lambda region, member: (region, member ^ 1)
    far = lambda region, member: (region, member ^ 2)
    cross = lambda region, member: (region, member ^ 3)
    mate = lambda region, member: (region ^ 1, member)
    along_x = lambda region, member: (region ^ 2, member)
    along_y = lambda region, member: (region ^ 4, member)
    diagonal = lambda region, member: (region ^ 6, member)

    region, member = lax.axis_index("region"), lax.axis_index("grp")
    core, half, line = region & 1, member & 1, (region >> 1) & 3
    is_home = core == (member >> 1)
    chunk, frame_len = probe.shape[2], probe.shape[3]
    piece_len, tile_len = transmission.shape[1], transmission.shape[2]
    size = jax.ShapeDtypeStruct

    part, which = line & 1, line >> 1
    base = 4 * core + 2 * half
    other_base = 4 * core + 2 * (1 - half)

    def block(mode):
        return lax.dynamic_slice(probe, (part, mode, 0, 0), (1, 1, chunk, frame_len)).reshape(chunk, frame_len)

    same_block, flip_block = block(base + which), block(other_base + which)
    from_far, from_near = send(same_block, far), send(flip_block, near)
    from_cross = send(flip_block, cross)
    mate_positions = send(positions, mate)
    piece = call(cut_kernel, size((2, piece_len, frame_len), BF), count=2, smem=(0,), limit=16)(
        positions, transmission
    )
    measured_low, from_near = barrier((measured[0].astype(BF), from_near))
    target = send(measured_low, home)
    q0 = jnp.concatenate([from_near, from_far, from_cross], axis=0)
    column = jnp.where(is_home, positions[0, 1], mate_positions[0, 1])
    place = jnp.stack([core, member, line, half, column]).astype(jnp.int32)
    piece, place, target, q0 = barrier((piece, place, target, q0))
    q1, q2 = send(q0, along_x), send(q0, along_y)
    own = send(piece, home)
    side = send(piece, beside)
    cut = q0.shape[0] // 2
    q3a, q3b = send(q2[:cut], along_x), send(q1[cut:], along_y)
    own, side, q3a, q3b = barrier((own, side, q3a, q3b))
    mate_own, mate_side = send(own, mate), send(side, mate)
    whole_probe = call(
        probe_kernel,
        size((2, 2, frame_len, frame_len), BF),
        [pltpu.SemaphoreType.DMA((2, 2))],
        count=7,
        smem=(0,),
        far=(1,),
        limit=16,
    )(place, probe, q0, q1, q2, q3a, q3b)

    right = jnp.asarray(propagator(frame_len))
    double = 2 * frame_len
    flops = 2 * 2 * double**3
    half_len = frame_len // 2
    half_field = size((2, 2, frame_len, half_len), BF)
    turned, mates_far, sent = call(
        forward_kernel,
        (size((2, 2, 3, frame_len, half_len), BF), half_field, size((frame_len, half_len), BF)),
        [
            pltpu.VMEM((2, tile_len, frame_len), BF),
            pltpu.VMEM((2, frame_len, frame_len), BF),
            pltpu.VMEM((3, double, frame_len), BF),
            pltpu.VMEM((frame_len, half_len), F32),
        ],
        count=8,
        smem=(0,),
        limit=24,
        cost=cost(3 * flops // 4, 16 * MIB),
    )(place, own, side, mate_own, mate_side, whole_probe, target, right)
    met = send(sent, mate)
    own_far, kept = call(
        rest_kernel,
        (half_field, size((frame_len, half_len), F32)),
        count=4,
        smem=(0,),
        limit=24,
        cost=cost(flops // 4, 4 * MIB),
    )(place, turned, target, right)

    chip = kept + met.astype(F32)
    misfit = chip + send(chip.astype(BF), near).astype(F32)
    mates_misfit = send(misfit.astype(BF), mate)
    own_left = call(
        own_kernel,
        size((3, double, half_len), BF),
        count=3,
        limit=24,
        cost=cost(flops // 4, 4 * MIB),
    )(own_far, misfit, right)

    piece_shape = size((2, piece_len, frame_len), BF)
    sent, kept_side, kept = call(
        backward_kernel,
        (size((2, 2, piece_len, frame_len), BF), piece_shape, piece_shape),
        [
            pltpu.VMEM((3, double, frame_len), BF),
            pltpu.VMEM((2, frame_len, frame_len), BF),
            pltpu.VMEM((4 * piece_len, frame_len), BF),
        ],
        count=6,
        smem=(0,),
        limit=24,
        cost=cost(3 * flops // 4, 12 * MIB),
    )(place, mates_far, whole_probe, mates_misfit, own_left, right)
    met = send(sent, mate)
    add = lambda a, b: (a.astype(F32) + b.astype(F32)).astype(BF)
    kept_side, kept = add(kept_side, met[0]), add(kept, met[1])
    data = add(send(kept, home), send(kept_side, beside))

    devices = regions * members
    moved = 4 * 2 * piece_len * tile_len
    old_row = call(
        old_kernel,
        size((1, LANES), F32),
        [pltpu.VMEM((OLD_PAIRS, 8, LANES), F32)],
        count=2,
        limit=16,
        cost=cost(22 * moved, 7 * moved),
    )(past_steps, past_changes)
    gradient, row = call(
        gradient_kernel,
        (size(transmission.shape, F32), size((devices, LANES), F32)),
        [pltpu.VMEM((len(PAIRS) - OLD_PAIRS, 8, LANES), F32)],
        count=7,
        smem=(0,),
        limit=16,
        cost=cost(16 * moved, 10 * moved),
    )(positions, data, transmission, old_gradient, past_steps, past_changes, old_row)
    all_rows = lax.all_to_all(
        row.reshape(devices, 1, LANES), AXES, split_axis=0, concat_axis=0, tiled=True
    ).reshape(devices, LANES)
    return call(
        update_kernel,
        (size(transmission.shape, F32), size(transmission.shape, F32)),
        [pltpu.VMEM(transmission.shape, F32), pltpu.SemaphoreType.DMA((3,))],
        count=6,
        limit=16,
        cost=cost(10 * moved, 11 * moved),
        out_space=pl.ANY,
    )(all_rows, transmission, gradient, old_gradient, past_steps, past_changes)


def solution(mesh):
    split = mesh.shape["grp"] == 4 and mesh.shape["region"] == 8

    def shards(*args):
        probe, positions, past_steps = args[1], args[3], args[4]
        sized = probe.shape[1] == 8 and positions.shape[0] == 1 and past_steps.shape[0] == HIST
        if split and sized:
            return fast(mesh, *args)
        return general(*args)

    return jax.shard_map(
        shards,
        mesh=mesh,
        in_specs=(
            P(None, "grp", "region"),
            P(None, None, "grp", None),
            P("region", "grp", None),
            P("region", None),
            P(None, None, "grp", "region"),
            P(None, None, "grp", "region"),
            P(None, "grp", "region"),
        ),
        out_specs=(P(None, "grp", "region"), P(None, "grp", "region")),
        check_vma=False,
    )
```

```python
import math

import jax
import jax.numpy as jnp
import ml_dtypes
import numpy as np
from jax import lax
from jax.experimental import pallas as pl
from jax.experimental.pallas import tpu as pltpu
from jax.sharding import PartitionSpec as P

TWO_PI = 2.0 * math.pi
CURVE_FLOOR = 0.25
TIKHONOV = 0.5
EPSILON = 1e-06
BF = jnp.bfloat16
F32 = jnp.float32
AXES = ("region", "grp")
LANES = 128
MIB = 1 << 20
HIST = 4


def dft_tables(count):
    index = jnp.arange(count, dtype=jnp.int32)
    phase = (index[:, None] * index[None, :] % count).astype(jnp.float32) * (TWO_PI / count)
    factor = 1.0 / math.sqrt(count)
    return (
        (jnp.cos(phase) * factor).astype(jnp.bfloat16),
        (-jnp.sin(phase) * factor).astype(jnp.bfloat16),
    )


def chirp_table(count):
    index = jnp.arange(count, dtype=jnp.int32)
    wavenumber = (index + count // 2) % count - count // 2
    phase = (wavenumber * wavenumber % (4 * count)).astype(jnp.float32) * (TWO_PI / (4 * count))
    return (jnp.cos(phase), -jnp.sin(phase))


def rotate(real_part, imag_part, turn_real, turn_imag):
    return (
        real_part * turn_real - imag_part * turn_imag,
        real_part * turn_imag + imag_part * turn_real,
    )


def narrow(pair):
    return jnp.stack([pair[0], pair[1]]).astype(jnp.bfloat16)


def right_product(field, matrix_real, matrix_imag):

    def single(left, right):
        return jnp.einsum("...k,kj->...j", left, right, preferred_element_type=jnp.float32)

    return (
        single(field[0], matrix_real) - single(field[1], matrix_imag),
        single(field[0], matrix_imag) + single(field[1], matrix_real),
    )


def left_product(matrix_real, matrix_imag, field):

    def single(left, right):
        return jnp.einsum("jk,...kc->...jc", left, right, preferred_element_type=jnp.float32)

    return (
        single(matrix_real, field[0]) - single(matrix_imag, field[1]),
        single(matrix_real, field[1]) + single(matrix_imag, field[0]),
    )


def general(transmission, probe, measured, positions, past_steps, past_changes, old_gradient):
    member = lax.axis_index("grp")
    frame_len = probe.shape[3]
    rows_here = probe.shape[2]
    tile_len = transmission.shape[2]
    anchor = jnp.zeros((), jnp.int32)
    fwd_real, fwd_imag = dft_tables(frame_len)
    inv_imag = -fwd_imag
    chirp_real, chirp_imag = chirp_table(frame_len)
    probe_wide = probe.astype(jnp.float32)
    tile = lax.all_gather(transmission.astype(jnp.bfloat16), "grp", axis=1, tiled=True)
    frame = 0
    first_row = positions[frame, 0] + member * rows_here
    window = jnp.swapaxes(
        lax.dynamic_slice(
            tile, (anchor, positions[frame, 1], first_row), (2, frame_len, rows_here)
        ),
        1,
        2,
    ).astype(jnp.float32)
    wave = narrow(rotate(probe_wide[0], probe_wide[1], window[0], window[1]))
    section = narrow(rotate(*right_product(wave, fwd_real, fwd_imag), chirp_real, chirp_imag))
    spread = narrow(right_product(section, fwd_real, inv_imag))
    section = narrow(
        rotate(
            *left_product(
                fwd_real,
                fwd_imag,
                lax.all_to_all(spread, "grp", split_axis=3, concat_axis=2, tiled=True),
            ),
            chirp_real[:, None],
            chirp_imag[:, None]
        )
    )
    far_field = narrow(left_product(fwd_real, inv_imag, section))
    near_rows = lax.all_to_all(far_field, "grp", split_axis=2, concat_axis=3, tiled=True)
    field_wide = near_rows.astype(jnp.float32)
    misfit = (
        jnp.sum(field_wide[0] * field_wide[0] + field_wide[1] * field_wide[1], axis=0)
        - measured[frame]
    )
    weighted = (misfit * field_wide).astype(jnp.bfloat16)
    section = narrow(
        rotate(
            *left_product(
                fwd_real,
                fwd_imag,
                lax.all_to_all(weighted, "grp", split_axis=3, concat_axis=2, tiled=True),
            ),
            chirp_real[:, None],
            -chirp_imag[:, None]
        )
    )
    returned = narrow(left_product(fwd_real, inv_imag, section))
    section = narrow(
        rotate(
            *right_product(
                lax.all_to_all(returned, "grp", split_axis=2, concat_axis=3, tiled=True),
                fwd_real,
                fwd_imag,
            ),
            chirp_real,
            -chirp_imag
        )
    )
    back_wave = jnp.stack(right_product(section, fwd_real, inv_imag))
    grad_real = 4.0 * jnp.sum(probe_wide[0] * back_wave[0] + probe_wide[1] * back_wave[1], axis=0)
    grad_imag = 4.0 * jnp.sum(probe_wide[0] * back_wave[1] - probe_wide[1] * back_wave[0], axis=0)
    frame_grads = [jnp.stack([grad_real, grad_imag])]
    scattered = jnp.zeros((2, tile_len, tile_len), jnp.float32)
    frame = 0
    corner = (anchor, positions[frame, 1], positions[frame, 0] + member * rows_here)
    scattered = lax.dynamic_update_slice(scattered, jnp.swapaxes(frame_grads[frame], 1, 2), corner)
    data_grad = lax.psum_scatter(
        scattered.astype(jnp.bfloat16), "grp", scatter_dimension=1, tiled=True
    ).astype(jnp.float32)
    gradient = data_grad + TIKHONOV * transmission
    depth = past_steps.shape[0]
    last = depth - 1
    change_new = gradient - old_gradient
    steps_list = [past_steps[index] for index in range(depth)]
    changes = [past_changes[index] for index in range(depth - 1)] + [change_new]
    alphas = [None] * depth
    curvature, self_dots, change_norm = lax.psum(
        (
            jnp.stack([jnp.sum(steps_list[index] * changes[index]) for index in range(depth)]),
            jnp.sum(past_steps * past_steps, axis=(1, 2, 3)),
            jnp.sum(change_new * change_new),
        ),
        ("region", "grp"),
    )
    weights = [
        1.0 / jnp.maximum(curvature[index], CURVE_FLOOR * self_dots[index])
        for index in range(depth)
    ]
    direction = gradient
    for index in reversed(range(depth)):
        alphas[index] = weights[index] * lax.psum(
            jnp.sum(steps_list[index] * direction), ("region", "grp")
        )
        direction = direction - alphas[index] * changes[index]
    scale = jnp.maximum(curvature[last], CURVE_FLOOR * self_dots[last]) / (change_norm + EPSILON)
    direction = scale * direction
    for index in range(depth):
        beta = weights[index] * lax.psum(jnp.sum(changes[index] * direction), ("region", "grp"))
        direction = direction + (alphas[index] - beta) * steps_list[index]
    return (transmission - direction, gradient)


def propagator(count):
    index = np.arange(count, dtype=np.int64)
    phase = (index[:, None] * index[None, :] % count).astype(np.float32) * np.float32(TWO_PI / count)
    factor = np.float32(1.0 / math.sqrt(count))
    table = (np.cos(phase) * factor).astype(ml_dtypes.bfloat16).astype(np.float64) + 1j * (
        -np.sin(phase) * factor
    ).astype(ml_dtypes.bfloat16).astype(np.float64)
    wavenumber = (index + count // 2) % count - count // 2
    chirp = np.exp(-1j * (wavenumber * wavenumber % (4 * count)) * (TWO_PI / (4 * count)))
    folded = (table * chirp[None, :]) @ np.conj(table)
    folded = 0.5 * (folded + folded.T)
    real, imag = folded.real, folded.imag
    return np.stack([real, imag - real, real + imag]).astype(ml_dtypes.bfloat16)


def dot(left, right, dims=((1,), (0,))):
    return lax.dot_general(left, right, (dims, ((), ())), preferred_element_type=F32)


def join(sums, reals, imags):
    return sums - imags, sums + reals


def summed(real, imag):
    return (real.astype(F32) + imag.astype(F32)).astype(BF)


def shift_table(rows, columns, row_base, column_base):
    row = lax.broadcasted_iota(jnp.int32, (rows, columns), 0) + row_base
    column = lax.broadcasted_iota(jnp.int32, (rows, columns), 1) + column_base
    return jnp.where(row == column, 1.0, 0.0).astype(BF)


def cut_kernel(pos_ref, tile_ref, out_ref):
    tile_len, frame_len = tile_ref.shape[2], out_ref.shape[2]
    table = shift_table(tile_len, frame_len, 0, pos_ref[0, 0])
    for part in range(2):
        out_ref[part] = dot(tile_ref[part].astype(BF), table).astype(BF)


def probe_kernel(place_ref, all_ref, q0_ref, q1_ref, q2_ref, q3a_ref, q3b_ref, probe_ref, sem):
    core, place, line, half = (place_ref[index] for index in range(4))
    chunk = all_ref.shape[2]

    def rows_of(step):
        return pl.ds(pl.multiple_of(lax.bitwise_xor(place, step) * chunk, chunk), chunk)

    copies = [
        pltpu.make_async_copy(
            all_ref.at[part, 4 * core + 2 * half + mode], probe_ref.at[part, mode, rows_of(0), :], sem.at[part, mode]
        )
        for part in range(2)
        for mode in range(2)
    ]
    for copy in copies:
        copy.start()
    cut = q3a_ref.shape[0]
    for turn, ref in ((0, q0_ref), (1, q1_ref), (2, q2_ref), (3, None)):
        combo = lax.bitwise_xor(line, turn)
        part, mode = lax.rem(combo, 2), lax.div(combo, 2)
        for step in range(1, 4):
            start = (step - 1) * chunk
            if ref is not None:
                value = ref[start : start + chunk]
            elif start + chunk <= cut:
                value = q3a_ref[start : start + chunk]
            elif start >= cut:
                value = q3b_ref[start - cut : start - cut + chunk]
            else:
                value = jnp.concatenate([q3a_ref[start:cut], q3b_ref[: start + chunk - cut]], axis=0)
            probe_ref[part, mode, rows_of(step), :] = value
    for copy in copies:
        copy.wait()


def forward_kernel(
    place_ref, own_ref, side_ref, mate_own_ref, mate_side_ref, probe_ref, measured_ref,
    right_ref, turned_ref, far_ref, send_ref, tile, window_ref, wave, total,
):
    core, half = place_ref[0], place_ref[3]
    chunk, frame_len = measured_ref.shape
    piece_len = own_ref.shape[1]
    piece = 2 * core + half
    for step, ref in enumerate((own_ref, side_ref, mate_own_ref, mate_side_ref)):
        base = pl.multiple_of(lax.bitwise_xor(piece, step) * piece_len, piece_len)
        for part in range(2):
            tile[part, pl.ds(base, piece_len), :] = ref[part]
    column = place_ref[4]
    table = shift_table(tile.shape[1], frame_len, 0, column)
    for part in range(2):
        window_ref[part] = dot(tile[part], table, ((0,), (0,))).astype(BF)

    block = frame_len // 2
    for mode in range(2):
        rows = slice(mode * frame_len, (mode + 1) * frame_len)
        pr, pi = probe_ref[0, mode].astype(F32), probe_ref[1, mode].astype(F32)
        wr, wi = window_ref[0].astype(F32), window_ref[1].astype(F32)
        real, imag = (pr * wr - pi * wi).astype(BF), (pr * wi + pi * wr).astype(BF)
        wave[0, rows], wave[1, rows], wave[2, rows] = summed(real, imag), real, imag
    for cell in range(2):
        columns = slice(cell * block, (cell + 1) * block)
        real, imag = join(*(dot(wave[index], right_ref[index, :, columns]) for index in range(3)))
        real, imag = real.astype(BF), imag.astype(BF)
        total_part = summed(real, imag)
        for mode in range(2):
            rows = slice(mode * frame_len, (mode + 1) * frame_len)
            for index, value in enumerate((total_part, real, imag)):
                turned_ref[mode, cell, index] = value[rows]
    far_columns(1 - core, turned_ref, right_ref, far_ref, total)
    subtract(core, half, 1 - core, measured_ref, total)
    send_ref[...] = total[...].astype(BF)


def far_columns(cell, turned_ref, right_ref, far_ref, total):
    frame_len = total.shape[0]
    power = 0.0
    for mode in range(2):
        real, imag = join(*(dot(right_ref[index], turned_ref[mode, cell, index]) for index in range(3)))
        real, imag = real.astype(BF), imag.astype(BF)
        far_ref[mode, 0] = real
        far_ref[mode, 1] = imag
        real, imag = real.astype(F32), imag.astype(F32)
        power = power + (real * real + imag * imag)
    total[...] = power


def subtract(core, half, cell, measured_ref, total):
    chunk, block = measured_ref.shape[0], total.shape[1]
    rows = pl.ds(pl.multiple_of((2 * core + half) * chunk, chunk), chunk)
    wanted = jnp.where(cell == 0, measured_ref[:, :block], measured_ref[:, block:])
    total[rows, :] = total[rows, :] - wanted.astype(F32)


def rest_kernel(place_ref, turned_ref, measured_ref, right_ref, far_ref, total):
    core, half = place_ref[0], place_ref[3]
    far_columns(core, turned_ref, right_ref, far_ref, total)
    subtract(core, half, core, measured_ref, total)


def left_columns(misfit, far_ref, right_ref, store):
    for mode in range(2):
        real = (misfit * far_ref[mode, 0].astype(F32)).astype(BF)
        imag = (-misfit * far_ref[mode, 1].astype(F32)).astype(BF)
        pieces = (summed(real, imag), real, imag)
        real, imag = join(*(dot(right_ref[index], value) for index, value in enumerate(pieces)))
        real, imag = real.astype(BF), imag.astype(BF)
        for index, value in enumerate((summed(real, imag), real, imag)):
            store(mode, index, value)


def own_kernel(far_ref, mine_ref, right_ref, out_ref):
    frame_len = mine_ref.shape[0]

    def store(mode, part, value):
        out_ref[part, mode * frame_len : (mode + 1) * frame_len, :] = value

    left_columns(mine_ref[...], far_ref, right_ref, store)


def backward_kernel(
    place_ref, far_ref, probe_ref, mates_ref, own_ref, right_ref,
    send_ref, side_ref, keep_ref, turned, grad, table,
):
    core, half = place_ref[0], place_ref[3]
    column = place_ref[4]
    frame_len, block = mates_ref.shape
    piece_len = keep_ref.shape[1]

    def lanes(cell):
        return pl.ds(pl.multiple_of(cell * block, block), block)

    def store(mode, index, value):
        turned[index, mode * frame_len : (mode + 1) * frame_len, lanes(1 - core)] = value

    left_columns(mates_ref[...].astype(F32), far_ref, right_ref, store)
    for index in range(3):
        turned[index, :, lanes(core)] = own_ref[index]
    for cell in range(2):
        columns = slice(cell * block, (cell + 1) * block)
        back = join(*(dot(turned[index], right_ref[index, :, columns]) for index in range(3)))
        real, imag = 0.0, 0.0
        for mode in range(2):
            br, bi = (value[mode * frame_len : (mode + 1) * frame_len] for value in back)
            pr, pi = probe_ref[0, mode, :, columns].astype(F32), probe_ref[1, mode, :, columns].astype(F32)
            real = real + (pr * br - pi * bi)
            imag = imag + (pr * bi + pi * br)
        grad[0, :, columns] = (4.0 * real).astype(BF)
        grad[1, :, columns] = (-4.0 * imag).astype(BF)

    slots = [(1 - core, 1), (1 - core, 0), (core, 1), (core, 0)]
    for index, (pair, flip) in enumerate(slots):
        base = (2 * pair + lax.bitwise_xor(half, flip)) * piece_len
        table[index * piece_len : (index + 1) * piece_len, :] = shift_table(piece_len, frame_len, base, column)
    for part in range(2):
        value = dot(table[...], grad[part], ((1,), (1,))).astype(BF)
        send_ref[0, part] = value[:piece_len]
        send_ref[1, part] = value[piece_len : 2 * piece_len]
        side_ref[part] = value[2 * piece_len : 3 * piece_len]
        keep_ref[part] = value[3 * piece_len :]


PAIRS = [("sy", i, j) for j in range(HIST - 1) for i in range(HIST)]
PAIRS += [("ss", i, i) for i in range(HIST)]
PAIRS += [("yy", i, j) for j in range(HIST - 1) for i in range(j + 1)]
OLD_PAIRS = len(PAIRS)
PAIRS += [("sy", i, HIST - 1) for i in range(HIST)]
PAIRS += [("yy", i, HIST - 1) for i in range(HIST)]
PAIRS += [("sg", i, i) for i in range(HIST)]
PAIRS += [("yg", i, i) for i in range(HIST)]
SLOT = {pair: index for index, pair in enumerate(PAIRS)}


def folded(value):
    parts, rows, columns = value.shape
    total = jnp.sum(value.reshape(parts * rows // 8, 8, columns), axis=0)
    return sum(total[:, start : start + LANES] for start in range(0, columns, LANES))


def add_products(sums, first, slots, vectors):
    for slot, pair in slots:
        kind, i, j = pair
        left = vectors[kind[0]][i]
        right = vectors["g"][0] if kind[1] == "g" else vectors[kind[1]][j]
        value = folded(left * right)
        sums[slot] = value if first else sums[slot] + value


def lane_row(sums, count):
    rows = [jnp.sum(sums[slot], axis=0, keepdims=True) for slot in range(count)]
    square = jnp.concatenate(rows + [jnp.zeros((LANES - count, LANES), F32)], axis=0)
    return jnp.sum(square.T, axis=0, keepdims=True)


BLOCK = 32


def column_blocks(ref):
    return range(0, ref.shape[-2], BLOCK)


def old_kernel(steps_ref, changes_ref, out_ref, sums):
    for start in column_blocks(steps_ref):
        columns = slice(start, start + BLOCK)
        vectors = {
            "s": [steps_ref[index, :, columns] for index in range(HIST)],
            "y": [changes_ref[index, :, columns] for index in range(HIST - 1)],
        }
        add_products(sums, start == 0, enumerate(PAIRS[:OLD_PAIRS]), vectors)
    out_ref[...] = lane_row(sums, OLD_PAIRS)


def gradient_kernel(
    pos_ref, data_ref, transmission_ref, old_ref, steps_ref, changes_ref, row_ref, gradient_ref, out_ref, sums
):
    table = shift_table(data_ref.shape[2], transmission_ref.shape[2], pos_ref[0, 0], 0)
    parts, piece_len, frame_len = data_ref.shape
    placed = dot(data_ref[...].reshape(parts * piece_len, frame_len), table)
    gradient_ref[...] = placed.reshape(transmission_ref.shape) + TIKHONOV * transmission_ref[...]
    for start in column_blocks(transmission_ref):
        columns = slice(start, start + BLOCK)
        gradient = gradient_ref[:, columns]
        vectors = {
            "s": [steps_ref[index, :, columns] for index in range(HIST)],
            "y": [changes_ref[index, :, columns] for index in range(HIST - 1)]
            + [gradient - old_ref[:, columns]],
            "g": [gradient],
        }
        add_products(sums, start == 0, enumerate(PAIRS[OLD_PAIRS:]), vectors)
    fresh = pltpu.roll(lane_row(sums, len(PAIRS) - OLD_PAIRS), OLD_PAIRS, 1)
    out_ref[...] = jnp.broadcast_to(fresh + row_ref[...], out_ref.shape)


def update_kernel(
    rows_ref, transmission_ref, gradient_ref, old_ref, steps_ref, changes_ref, updated_ref, copy_ref, out_ref, sem
):
    copies = [pltpu.make_async_copy(gradient_ref, copy_ref, sem.at[2])]
    copies[0].start()
    row = jnp.sum(rows_ref[...], axis=0, keepdims=True)
    lane = lax.broadcasted_iota(jnp.int32, row.shape, 1)

    def get(kind, i, j):
        if kind == "yy" and i > j:
            i, j = j, i
        picked = jnp.where(lane == SLOT[(kind, i, j)], row, 0.0)
        return jnp.broadcast_to(jnp.sum(picked, axis=1, keepdims=True), row.shape)

    last = HIST - 1
    floors = [
        jnp.maximum(get("sy", index, index), CURVE_FLOOR * get("ss", index, index)) for index in range(HIST)
    ]
    weights = [1.0 / floor for floor in floors]
    alphas = [None] * HIST
    for index in reversed(range(HIST)):
        value = get("sg", index, index)
        for later in range(index + 1, HIST):
            value = value - alphas[later] * get("sy", index, later)
        alphas[index] = weights[index] * value
    scale = floors[last] / (get("yy", last, last) + EPSILON)
    moves = []
    for index in range(HIST):
        value = get("yg", index, index)
        for other in range(HIST):
            value = value - alphas[other] * get("yy", index, other)
        value = scale * value
        for before in range(index):
            value = value + moves[before] * get("sy", before, index)
        moves.append(alphas[index] - weights[index] * value)
    repeat = out_ref.shape[-1] // LANES
    wide = lambda value: jnp.concatenate([value] * repeat, axis=1)
    scale_row = wide(scale)
    change_rows = [wide(-scale * alpha) for alpha in alphas]
    step_rows = [wide(move) for move in moves]
    for part in range(2):
        for start in column_blocks(out_ref):
            columns = slice(start, start + BLOCK)
            gradient = gradient_ref[part, columns]
            total = scale_row * gradient + change_rows[last] * (gradient - old_ref[part, columns])
            for index in range(HIST - 1):
                total = total + change_rows[index] * changes_ref[index, part, columns]
            for index in range(HIST):
                total = total + step_rows[index] * steps_ref[index, part, columns]
            out_ref[part, columns] = transmission_ref[part, columns] - total
        copies.append(pltpu.make_async_copy(out_ref.at[part], updated_ref.at[part], sem.at[part]))
        copies[-1].start()
    for copy in copies:
        copy.wait()


def call(body, outs, scratch=(), limit=48, smem=(), far=(), count=0, cost=None, out_space=pltpu.VMEM):
    space = lambda index: pltpu.SMEM if index in smem else pl.ANY if index in far else pltpu.VMEM
    specs = [pl.BlockSpec(memory_space=space(index)) for index in range(count)]
    return pl.pallas_call(
        body,
        out_shape=outs,
        in_specs=specs,
        out_specs=jax.tree.map(lambda _: pl.BlockSpec(memory_space=out_space), outs),
        scratch_shapes=list(scratch),
        compiler_params=pltpu.CompilerParams(vmem_limit_bytes=limit * MIB),
        cost_estimate=cost,
    )


def cost(flops, moved):
    return pl.CostEstimate(flops=int(flops), bytes_accessed=int(moved), transcendentals=0)


def home(region, member):
    return (region, member) if at_home(region, member) else (region ^ 1, member ^ 2)


def at_home(region, member):
    return region % 2 == member // 2


def beside(region, member):
    return (region, member ^ 1) if at_home(region, member) else (region ^ 1, member ^ 3)


def fast(mesh, transmission, probe, measured, positions, past_steps, past_changes, old_gradient):
    regions, members = mesh.shape["region"], mesh.shape["grp"]
    barrier = lax.optimization_barrier

    def send(value, target):
        pairs = []
        for region in range(regions):
            for member in range(members):
                to_region, to_member = target(region, member)
                pairs.append((region * members + member, to_region * members + to_member))
        return lax.ppermute(value, AXES, pairs)

    near = lambda region, member: (region, member ^ 1)
    far = lambda region, member: (region, member ^ 2)
    cross = lambda region, member: (region, member ^ 3)
    mate = lambda region, member: (region ^ 1, member)
    along_x = lambda region, member: (region ^ 2, member)
    along_y = lambda region, member: (region ^ 4, member)
    diagonal = lambda region, member: (region ^ 6, member)

    region, member = lax.axis_index("region"), lax.axis_index("grp")
    core, half, line = region & 1, member & 1, (region >> 1) & 3
    is_home = core == (member >> 1)
    chunk, frame_len = probe.shape[2], probe.shape[3]
    piece_len, tile_len = transmission.shape[1], transmission.shape[2]
    size = jax.ShapeDtypeStruct

    part, which = line & 1, line >> 1
    base = 4 * core + 2 * half
    other_base = 4 * core + 2 * (1 - half)

    def block(mode):
        return lax.dynamic_slice(probe, (part, mode, 0, 0), (1, 1, chunk, frame_len)).reshape(chunk, frame_len)

    same_block, flip_block = block(base + which), block(other_base + which)
    from_far, from_near = send(same_block, far), send(flip_block, near)
    from_cross = send(flip_block, cross)
    mate_positions = send(positions, mate)
    piece = call(cut_kernel, size((2, piece_len, frame_len), BF), count=2, smem=(0,), limit=12, cost=cost(0, 0))(
        positions, transmission
    )
    q0 = jnp.concatenate([from_near, from_far, from_cross], axis=0)
    column = jnp.where(is_home, positions[0, 1], mate_positions[0, 1])
    place = jnp.stack([core, member, line, half, column]).astype(jnp.int32)
    place, measured_low, q0 = barrier((place, measured[0].astype(BF), q0))
    q1, q2 = send(q0, along_x), send(q0, along_y)
    target = send(measured_low, home)
    own = send(piece, home)
    side = send(piece, beside)
    cut = q0.shape[0] // 2
    q3a, q3b = send(q2[:cut], along_x), send(q1[cut:], along_y)
    own, target = barrier((own, target))
    mate_own = send(own, mate)
    mate_own, side, q3a, q3b = barrier((mate_own, side, q3a, q3b))
    mate_side = send(side, mate)
    whole_probe = call(
        probe_kernel,
        size((2, 2, frame_len, frame_len), BF),
        [pltpu.SemaphoreType.DMA((2, 2))],
        count=7,
        smem=(0,),
        far=(1,),
        limit=12,
    )(place, probe, q0, q1, q2, q3a, q3b)

    right = jnp.asarray(propagator(frame_len))
    double = 2 * frame_len
    flops = 2 * 2 * double**3
    half_len = frame_len // 2
    half_field = size((2, 2, frame_len, half_len), BF)
    turned, mates_far, sent = call(
        forward_kernel,
        (size((2, 2, 3, frame_len, half_len), BF), half_field, size((frame_len, half_len), BF)),
        [
            pltpu.VMEM((2, tile_len, frame_len), BF),
            pltpu.VMEM((2, frame_len, frame_len), BF),
            pltpu.VMEM((3, double, frame_len), BF),
            pltpu.VMEM((frame_len, half_len), F32),
        ],
        count=8,
        smem=(0,),
        limit=20,
        cost=cost(3 * flops // 4, 16 * MIB),
    )(place, own, side, mate_own, mate_side, whole_probe, target, right)
    met = send(sent, mate)
    own_far, kept = call(
        rest_kernel,
        (half_field, size((frame_len, half_len), F32)),
        count=4,
        smem=(0,),
        limit=20,
        cost=cost(flops // 4, 4 * MIB),
    )(place, turned, target, right)

    chip = kept + met.astype(F32)
    misfit = chip + send(chip.astype(BF), near).astype(F32)
    mates_misfit = send(misfit.astype(BF), mate)
    own_left = call(
        own_kernel,
        size((3, double, half_len), BF),
        count=3,
        limit=20,
        cost=cost(flops // 4, 4 * MIB),
    )(own_far, misfit, right)

    piece_shape = size((2, piece_len, frame_len), BF)
    sent, kept_side, kept = call(
        backward_kernel,
        (size((2, 2, piece_len, frame_len), BF), piece_shape, piece_shape),
        [
            pltpu.VMEM((3, double, frame_len), BF),
            pltpu.VMEM((2, frame_len, frame_len), BF),
            pltpu.VMEM((4 * piece_len, frame_len), BF),
        ],
        count=6,
        smem=(0,),
        limit=20,
        cost=cost(3 * flops // 4, 12 * MIB),
    )(place, mates_far, whole_probe, mates_misfit, own_left, right)
    met = send(sent, mate)
    add = lambda a, b: (a.astype(F32) + b.astype(F32)).astype(BF)
    kept_side, kept = add(kept_side, met[0]), add(kept, met[1])
    data = add(send(kept, home), send(kept_side, beside))

    devices = regions * members
    moved = 4 * 2 * piece_len * tile_len
    old_row = call(
        old_kernel,
        size((1, LANES), F32),
        [pltpu.VMEM((OLD_PAIRS, 8, LANES), F32)],
        count=2,
        limit=12,
        cost=cost(22 * moved, 7 * moved),
    )(past_steps, past_changes)
    gradient, row = call(
        gradient_kernel,
        (size(transmission.shape, F32), size((devices, LANES), F32)),
        [pltpu.VMEM((len(PAIRS) - OLD_PAIRS, 8, LANES), F32)],
        count=7,
        smem=(0,),
        limit=12,
        cost=cost(16 * moved, 10 * moved),
    )(positions, data, transmission, old_gradient, past_steps, past_changes, old_row)
    all_rows = lax.all_to_all(
        row.reshape(devices, 1, LANES), AXES, split_axis=0, concat_axis=0, tiled=True
    ).reshape(devices, LANES)
    return call(
        update_kernel,
        (size(transmission.shape, F32), size(transmission.shape, F32)),
        [pltpu.VMEM(transmission.shape, F32), pltpu.SemaphoreType.DMA((3,))],
        count=6,
        limit=12,
        cost=cost(10 * moved, 11 * moved),
        out_space=pl.ANY,
    )(all_rows, transmission, gradient, old_gradient, past_steps, past_changes)


def solution(mesh):
    split = mesh.shape["grp"] == 4 and mesh.shape["region"] == 8

    def shards(*args):
        probe, positions, past_steps = args[1], args[3], args[4]
        sized = probe.shape[1] == 8 and positions.shape[0] == 1 and past_steps.shape[0] == HIST
        if split and sized:
            return fast(mesh, *args)
        return general(*args)

    return jax.shard_map(
        shards,
        mesh=mesh,
        in_specs=(
            P(None, "grp", "region"),
            P(None, None, "grp", None),
            P("region", "grp", None),
            P("region", None),
            P(None, None, "grp", "region"),
            P(None, None, "grp", "region"),
            P(None, "grp", "region"),
        ),
        out_specs=(P(None, "grp", "region"), P(None, "grp", "region")),
        check_vma=False,
    )
```

```python
import math

import jax
import jax.numpy as jnp
import ml_dtypes
import numpy as np
from jax import lax
from jax.experimental import pallas as pl
from jax.experimental.pallas import tpu as pltpu
from jax.sharding import PartitionSpec as P

TWO_PI = 2.0 * math.pi
CURVE_FLOOR = 0.25
TIKHONOV = 0.5
EPSILON = 1e-06
BF = jnp.bfloat16
F32 = jnp.float32
AXES = ("region", "grp")
LANES = 128
MIB = 1 << 20
HIST = 4


def dft_tables(count):
    index = jnp.arange(count, dtype=jnp.int32)
    phase = (index[:, None] * index[None, :] % count).astype(jnp.float32) * (TWO_PI / count)
    factor = 1.0 / math.sqrt(count)
    return (
        (jnp.cos(phase) * factor).astype(jnp.bfloat16),
        (-jnp.sin(phase) * factor).astype(jnp.bfloat16),
    )


def chirp_table(count):
    index = jnp.arange(count, dtype=jnp.int32)
    wavenumber = (index + count // 2) % count - count // 2
    phase = (wavenumber * wavenumber % (4 * count)).astype(jnp.float32) * (TWO_PI / (4 * count))
    return (jnp.cos(phase), -jnp.sin(phase))


def rotate(real_part, imag_part, turn_real, turn_imag):
    return (
        real_part * turn_real - imag_part * turn_imag,
        real_part * turn_imag + imag_part * turn_real,
    )


def narrow(pair):
    return jnp.stack([pair[0], pair[1]]).astype(jnp.bfloat16)


def right_product(field, matrix_real, matrix_imag):

    def single(left, right):
        return jnp.einsum("...k,kj->...j", left, right, preferred_element_type=jnp.float32)

    return (
        single(field[0], matrix_real) - single(field[1], matrix_imag),
        single(field[0], matrix_imag) + single(field[1], matrix_real),
    )


def left_product(matrix_real, matrix_imag, field):

    def single(left, right):
        return jnp.einsum("jk,...kc->...jc", left, right, preferred_element_type=jnp.float32)

    return (
        single(matrix_real, field[0]) - single(matrix_imag, field[1]),
        single(matrix_real, field[1]) + single(matrix_imag, field[0]),
    )


def general(transmission, probe, measured, positions, past_steps, past_changes, old_gradient):
    member = lax.axis_index("grp")
    frame_len = probe.shape[3]
    rows_here = probe.shape[2]
    tile_len = transmission.shape[2]
    anchor = jnp.zeros((), jnp.int32)
    fwd_real, fwd_imag = dft_tables(frame_len)
    inv_imag = -fwd_imag
    chirp_real, chirp_imag = chirp_table(frame_len)
    probe_wide = probe.astype(jnp.float32)
    tile = lax.all_gather(transmission.astype(jnp.bfloat16), "grp", axis=1, tiled=True)
    frame = 0
    first_row = positions[frame, 0] + member * rows_here
    window = jnp.swapaxes(
        lax.dynamic_slice(
            tile, (anchor, positions[frame, 1], first_row), (2, frame_len, rows_here)
        ),
        1,
        2,
    ).astype(jnp.float32)
    wave = narrow(rotate(probe_wide[0], probe_wide[1], window[0], window[1]))
    section = narrow(rotate(*right_product(wave, fwd_real, fwd_imag), chirp_real, chirp_imag))
    spread = narrow(right_product(section, fwd_real, inv_imag))
    section = narrow(
        rotate(
            *left_product(
                fwd_real,
                fwd_imag,
                lax.all_to_all(spread, "grp", split_axis=3, concat_axis=2, tiled=True),
            ),
            chirp_real[:, None],
            chirp_imag[:, None]
        )
    )
    far_field = narrow(left_product(fwd_real, inv_imag, section))
    near_rows = lax.all_to_all(far_field, "grp", split_axis=2, concat_axis=3, tiled=True)
    field_wide = near_rows.astype(jnp.float32)
    misfit = (
        jnp.sum(field_wide[0] * field_wide[0] + field_wide[1] * field_wide[1], axis=0)
        - measured[frame]
    )
    weighted = (misfit * field_wide).astype(jnp.bfloat16)
    section = narrow(
        rotate(
            *left_product(
                fwd_real,
                fwd_imag,
                lax.all_to_all(weighted, "grp", split_axis=3, concat_axis=2, tiled=True),
            ),
            chirp_real[:, None],
            -chirp_imag[:, None]
        )
    )
    returned = narrow(left_product(fwd_real, inv_imag, section))
    section = narrow(
        rotate(
            *right_product(
                lax.all_to_all(returned, "grp", split_axis=2, concat_axis=3, tiled=True),
                fwd_real,
                fwd_imag,
            ),
            chirp_real,
            -chirp_imag
        )
    )
    back_wave = jnp.stack(right_product(section, fwd_real, inv_imag))
    grad_real = 4.0 * jnp.sum(probe_wide[0] * back_wave[0] + probe_wide[1] * back_wave[1], axis=0)
    grad_imag = 4.0 * jnp.sum(probe_wide[0] * back_wave[1] - probe_wide[1] * back_wave[0], axis=0)
    frame_grads = [jnp.stack([grad_real, grad_imag])]
    scattered = jnp.zeros((2, tile_len, tile_len), jnp.float32)
    frame = 0
    corner = (anchor, positions[frame, 1], positions[frame, 0] + member * rows_here)
    scattered = lax.dynamic_update_slice(scattered, jnp.swapaxes(frame_grads[frame], 1, 2), corner)
    data_grad = lax.psum_scatter(
        scattered.astype(jnp.bfloat16), "grp", scatter_dimension=1, tiled=True
    ).astype(jnp.float32)
    gradient = data_grad + TIKHONOV * transmission
    depth = past_steps.shape[0]
    last = depth - 1
    change_new = gradient - old_gradient
    steps_list = [past_steps[index] for index in range(depth)]
    changes = [past_changes[index] for index in range(depth - 1)] + [change_new]
    alphas = [None] * depth
    curvature, self_dots, change_norm = lax.psum(
        (
            jnp.stack([jnp.sum(steps_list[index] * changes[index]) for index in range(depth)]),
            jnp.sum(past_steps * past_steps, axis=(1, 2, 3)),
            jnp.sum(change_new * change_new),
        ),
        ("region", "grp"),
    )
    weights = [
        1.0 / jnp.maximum(curvature[index], CURVE_FLOOR * self_dots[index])
        for index in range(depth)
    ]
    direction = gradient
    for index in reversed(range(depth)):
        alphas[index] = weights[index] * lax.psum(
            jnp.sum(steps_list[index] * direction), ("region", "grp")
        )
        direction = direction - alphas[index] * changes[index]
    scale = jnp.maximum(curvature[last], CURVE_FLOOR * self_dots[last]) / (change_norm + EPSILON)
    direction = scale * direction
    for index in range(depth):
        beta = weights[index] * lax.psum(jnp.sum(changes[index] * direction), ("region", "grp"))
        direction = direction + (alphas[index] - beta) * steps_list[index]
    return (transmission - direction, gradient)


def propagator(count):
    index = np.arange(count, dtype=np.int64)
    phase = (index[:, None] * index[None, :] % count).astype(np.float32) * np.float32(TWO_PI / count)
    factor = np.float32(1.0 / math.sqrt(count))
    table = (np.cos(phase) * factor).astype(ml_dtypes.bfloat16).astype(np.float64) + 1j * (
        -np.sin(phase) * factor
    ).astype(ml_dtypes.bfloat16).astype(np.float64)
    wavenumber = (index + count // 2) % count - count // 2
    chirp = np.exp(-1j * (wavenumber * wavenumber % (4 * count)) * (TWO_PI / (4 * count)))
    folded = (table * chirp[None, :]) @ np.conj(table)
    folded = 0.5 * (folded + folded.T)
    real, imag = folded.real, folded.imag
    return np.stack([real, imag - real, real + imag]).astype(ml_dtypes.bfloat16)


def dot(left, right, dims=((1,), (0,))):
    return lax.dot_general(left, right, (dims, ((), ())), preferred_element_type=F32)


def join(sums, reals, imags):
    return sums - imags, sums + reals


def summed(real, imag):
    return (real.astype(F32) + imag.astype(F32)).astype(BF)


def shift_table(rows, columns, row_base, column_base):
    row = lax.broadcasted_iota(jnp.int32, (rows, columns), 0) + row_base
    column = lax.broadcasted_iota(jnp.int32, (rows, columns), 1) + column_base
    return jnp.where(row == column, 1.0, 0.0).astype(BF)


def cut_kernel(pos_ref, tile_ref, out_ref):
    tile_len, frame_len = tile_ref.shape[2], out_ref.shape[2]
    table = shift_table(tile_len, frame_len, 0, pos_ref[0, 0])
    for part in range(2):
        out_ref[part] = dot(tile_ref[part].astype(BF), table).astype(BF)


def probe_kernel(place_ref, all_ref, q0_ref, q1_ref, q2_ref, q3a_ref, q3b_ref, probe_ref, sem):
    core, place, line, half = (place_ref[index] for index in range(4))
    chunk = all_ref.shape[2]

    def rows_of(step):
        return pl.ds(pl.multiple_of(lax.bitwise_xor(place, step) * chunk, chunk), chunk)

    copies = [
        pltpu.make_async_copy(
            all_ref.at[part, 4 * core + 2 * half + mode], probe_ref.at[part, mode, rows_of(0), :], sem.at[part, mode]
        )
        for part in range(2)
        for mode in range(2)
    ]
    for copy in copies:
        copy.start()
    cut = q3a_ref.shape[0]
    for turn, ref in ((0, q0_ref), (1, q1_ref), (2, q2_ref), (3, None)):
        combo = lax.bitwise_xor(line, turn)
        part, mode = lax.rem(combo, 2), lax.div(combo, 2)
        for step in range(1, 4):
            start = (step - 1) * chunk
            if ref is not None:
                value = ref[start : start + chunk]
            elif start + chunk <= cut:
                value = q3a_ref[start : start + chunk]
            elif start >= cut:
                value = q3b_ref[start - cut : start - cut + chunk]
            else:
                value = jnp.concatenate([q3a_ref[start:cut], q3b_ref[: start + chunk - cut]], axis=0)
            probe_ref[part, mode, rows_of(step), :] = value
    for copy in copies:
        copy.wait()


def forward_kernel(
    place_ref, own_ref, side_ref, mate_own_ref, mate_side_ref, probe_ref, measured_ref,
    right_ref, turned_ref, far_ref, send_ref, tile, window_ref, wave, total,
):
    core, half = place_ref[0], place_ref[3]
    chunk, frame_len = measured_ref.shape
    piece_len = own_ref.shape[1]
    piece = 2 * core + half
    for step, ref in enumerate((own_ref, side_ref, mate_own_ref, mate_side_ref)):
        base = pl.multiple_of(lax.bitwise_xor(piece, step) * piece_len, piece_len)
        for part in range(2):
            tile[part, pl.ds(base, piece_len), :] = ref[part]
    column = place_ref[4]
    table = shift_table(tile.shape[1], frame_len, 0, column)
    for part in range(2):
        window_ref[part] = dot(tile[part], table, ((0,), (0,))).astype(BF)

    block = frame_len // 2
    for mode in range(2):
        rows = slice(mode * frame_len, (mode + 1) * frame_len)
        pr, pi = probe_ref[0, mode].astype(F32), probe_ref[1, mode].astype(F32)
        wr, wi = window_ref[0].astype(F32), window_ref[1].astype(F32)
        real, imag = (pr * wr - pi * wi).astype(BF), (pr * wi + pi * wr).astype(BF)
        wave[0, rows], wave[1, rows], wave[2, rows] = summed(real, imag), real, imag
    for cell in range(2):
        columns = slice(cell * block, (cell + 1) * block)
        real, imag = join(*(dot(wave[index], right_ref[index, :, columns]) for index in range(3)))
        real, imag = real.astype(BF), imag.astype(BF)
        total_part = summed(real, imag)
        for mode in range(2):
            rows = slice(mode * frame_len, (mode + 1) * frame_len)
            for index, value in enumerate((total_part, real, imag)):
                turned_ref[mode, cell, index] = value[rows]
    far_columns(1 - core, turned_ref, right_ref, far_ref, total)
    subtract(core, half, 1 - core, measured_ref, total)
    send_ref[...] = total[...].astype(BF)


def far_columns(cell, turned_ref, right_ref, far_ref, total):
    frame_len = total.shape[0]
    power = 0.0
    for mode in range(2):
        real, imag = join(*(dot(right_ref[index], turned_ref[mode, cell, index]) for index in range(3)))
        real, imag = real.astype(BF), imag.astype(BF)
        far_ref[mode, 0] = real
        far_ref[mode, 1] = imag
        real, imag = real.astype(F32), imag.astype(F32)
        power = power + (real * real + imag * imag)
    total[...] = power


def subtract(core, half, cell, measured_ref, total):
    chunk, block = measured_ref.shape[0], total.shape[1]
    rows = pl.ds(pl.multiple_of((2 * core + half) * chunk, chunk), chunk)
    wanted = jnp.where(cell == 0, measured_ref[:, :block], measured_ref[:, block:])
    total[rows, :] = total[rows, :] - wanted.astype(F32)


def rest_kernel(place_ref, turned_ref, measured_ref, right_ref, far_ref, total):
    core, half = place_ref[0], place_ref[3]
    far_columns(core, turned_ref, right_ref, far_ref, total)
    subtract(core, half, core, measured_ref, total)


def left_columns(misfit, far_ref, right_ref, store):
    for mode in range(2):
        real = (misfit * far_ref[mode, 0].astype(F32)).astype(BF)
        imag = (-misfit * far_ref[mode, 1].astype(F32)).astype(BF)
        pieces = (summed(real, imag), real, imag)
        real, imag = join(*(dot(right_ref[index], value) for index, value in enumerate(pieces)))
        real, imag = real.astype(BF), imag.astype(BF)
        for index, value in enumerate((summed(real, imag), real, imag)):
            store(mode, index, value)


def own_kernel(far_ref, mine_ref, right_ref, out_ref):
    frame_len = mine_ref.shape[0]

    def store(mode, part, value):
        out_ref[part, mode * frame_len : (mode + 1) * frame_len, :] = value

    left_columns(mine_ref[...], far_ref, right_ref, store)


def backward_kernel(
    place_ref, far_ref, probe_ref, mates_ref, own_ref, right_ref,
    send_ref, side_ref, keep_ref, turned, grad, table,
):
    core, half = place_ref[0], place_ref[3]
    column = place_ref[4]
    frame_len, block = mates_ref.shape
    piece_len = keep_ref.shape[1]

    def lanes(cell):
        return pl.ds(pl.multiple_of(cell * block, block), block)

    def store(mode, index, value):
        turned[index, mode * frame_len : (mode + 1) * frame_len, lanes(1 - core)] = value

    left_columns(mates_ref[...].astype(F32), far_ref, right_ref, store)
    for index in range(3):
        turned[index, :, lanes(core)] = own_ref[index]
    for cell in range(2):
        columns = slice(cell * block, (cell + 1) * block)
        back = join(*(dot(turned[index], right_ref[index, :, columns]) for index in range(3)))
        real, imag = 0.0, 0.0
        for mode in range(2):
            br, bi = (value[mode * frame_len : (mode + 1) * frame_len] for value in back)
            pr, pi = probe_ref[0, mode, :, columns].astype(F32), probe_ref[1, mode, :, columns].astype(F32)
            real = real + (pr * br - pi * bi)
            imag = imag + (pr * bi + pi * br)
        grad[0, :, columns] = (4.0 * real).astype(BF)
        grad[1, :, columns] = (-4.0 * imag).astype(BF)

    slots = [(1 - core, 1), (1 - core, 0), (core, 1), (core, 0)]
    for index, (pair, flip) in enumerate(slots):
        base = (2 * pair + lax.bitwise_xor(half, flip)) * piece_len
        table[index * piece_len : (index + 1) * piece_len, :] = shift_table(piece_len, frame_len, base, column)
    for part in range(2):
        value = dot(table[...], grad[part], ((1,), (1,))).astype(BF)
        send_ref[0, part] = value[:piece_len]
        send_ref[1, part] = value[piece_len : 2 * piece_len]
        side_ref[part] = value[2 * piece_len : 3 * piece_len]
        keep_ref[part] = value[3 * piece_len :]


PAIRS = [("sy", i, j) for j in range(HIST - 1) for i in range(HIST)]
PAIRS += [("ss", i, i) for i in range(HIST)]
PAIRS += [("yy", i, j) for j in range(HIST - 1) for i in range(j + 1)]
OLD_PAIRS = len(PAIRS)
PAIRS += [("sy", i, HIST - 1) for i in range(HIST)]
PAIRS += [("yy", i, HIST - 1) for i in range(HIST)]
PAIRS += [("sg", i, i) for i in range(HIST)]
PAIRS += [("yg", i, i) for i in range(HIST)]
SLOT = {pair: index for index, pair in enumerate(PAIRS)}


def folded(value):
    parts, rows, columns = value.shape
    total = jnp.sum(value.reshape(parts * rows // 8, 8, columns), axis=0)
    return sum(total[:, start : start + LANES] for start in range(0, columns, LANES))


def add_products(sums, first, slots, vectors):
    for slot, pair in slots:
        kind, i, j = pair
        left = vectors[kind[0]][i]
        right = vectors["g"][0] if kind[1] == "g" else vectors[kind[1]][j]
        value = folded(left * right)
        sums[slot] = value if first else sums[slot] + value


def lane_row(sums, count):
    rows = [jnp.sum(sums[slot], axis=0, keepdims=True) for slot in range(count)]
    square = jnp.concatenate(rows + [jnp.zeros((LANES - count, LANES), F32)], axis=0)
    return jnp.sum(square.T, axis=0, keepdims=True)


BLOCK = 32


def column_blocks(ref):
    return range(0, ref.shape[-2], BLOCK)


def old_kernel(steps_ref, changes_ref, out_ref, sums):
    for start in column_blocks(steps_ref):
        columns = slice(start, start + BLOCK)
        vectors = {
            "s": [steps_ref[index, :, columns] for index in range(HIST)],
            "y": [changes_ref[index, :, columns] for index in range(HIST - 1)],
        }
        add_products(sums, start == 0, enumerate(PAIRS[:OLD_PAIRS]), vectors)
    out_ref[...] = lane_row(sums, OLD_PAIRS)


def gradient_kernel(
    pos_ref, data_ref, transmission_ref, old_ref, steps_ref, changes_ref, row_ref, gradient_ref, out_ref, sums
):
    table = shift_table(data_ref.shape[2], transmission_ref.shape[2], pos_ref[0, 0], 0)
    parts, piece_len, frame_len = data_ref.shape
    placed = dot(data_ref[...].reshape(parts * piece_len, frame_len), table)
    gradient_ref[...] = placed.reshape(transmission_ref.shape) + TIKHONOV * transmission_ref[...]
    for start in column_blocks(transmission_ref):
        columns = slice(start, start + BLOCK)
        gradient = gradient_ref[:, columns]
        vectors = {
            "s": [steps_ref[index, :, columns] for index in range(HIST)],
            "y": [changes_ref[index, :, columns] for index in range(HIST - 1)]
            + [gradient - old_ref[:, columns]],
            "g": [gradient],
        }
        add_products(sums, start == 0, enumerate(PAIRS[OLD_PAIRS:]), vectors)
    fresh = pltpu.roll(lane_row(sums, len(PAIRS) - OLD_PAIRS), OLD_PAIRS, 1)
    out_ref[...] = jnp.broadcast_to(fresh + row_ref[...], out_ref.shape)


def update_kernel(
    rows_ref, transmission_ref, gradient_ref, old_ref, steps_ref, changes_ref, updated_ref, copy_ref, out_ref, sem
):
    copies = [pltpu.make_async_copy(gradient_ref, copy_ref, sem.at[2])]
    copies[0].start()
    row = jnp.sum(rows_ref[...], axis=0, keepdims=True)
    lane = lax.broadcasted_iota(jnp.int32, row.shape, 1)

    def get(kind, i, j):
        if kind == "yy" and i > j:
            i, j = j, i
        picked = jnp.where(lane == SLOT[(kind, i, j)], row, 0.0)
        return jnp.broadcast_to(jnp.sum(picked, axis=1, keepdims=True), row.shape)

    last = HIST - 1
    floors = [
        jnp.maximum(get("sy", index, index), CURVE_FLOOR * get("ss", index, index)) for index in range(HIST)
    ]
    weights = [1.0 / floor for floor in floors]
    alphas = [None] * HIST
    for index in reversed(range(HIST)):
        value = get("sg", index, index)
        for later in range(index + 1, HIST):
            value = value - alphas[later] * get("sy", index, later)
        alphas[index] = weights[index] * value
    scale = floors[last] / (get("yy", last, last) + EPSILON)
    moves = []
    for index in range(HIST):
        value = get("yg", index, index)
        for other in range(HIST):
            value = value - alphas[other] * get("yy", index, other)
        value = scale * value
        for before in range(index):
            value = value + moves[before] * get("sy", before, index)
        moves.append(alphas[index] - weights[index] * value)
    repeat = out_ref.shape[-1] // LANES
    wide = lambda value: jnp.concatenate([value] * repeat, axis=1)
    scale_row = wide(scale)
    change_rows = [wide(-scale * alpha) for alpha in alphas]
    step_rows = [wide(move) for move in moves]
    for part in range(2):
        for start in column_blocks(out_ref):
            columns = slice(start, start + BLOCK)
            gradient = gradient_ref[part, columns]
            total = scale_row * gradient + change_rows[last] * (gradient - old_ref[part, columns])
            for index in range(HIST - 1):
                total = total + change_rows[index] * changes_ref[index, part, columns]
            for index in range(HIST):
                total = total + step_rows[index] * steps_ref[index, part, columns]
            out_ref[part, columns] = transmission_ref[part, columns] - total
        copies.append(pltpu.make_async_copy(out_ref.at[part], updated_ref.at[part], sem.at[part]))
        copies[-1].start()
    for copy in copies:
        copy.wait()


def call(body, outs, scratch=(), limit=48, smem=(), far=(), count=0, cost=None, out_space=pltpu.VMEM):
    space = lambda index: pltpu.SMEM if index in smem else pl.ANY if index in far else pltpu.VMEM
    specs = [pl.BlockSpec(memory_space=space(index)) for index in range(count)]
    return pl.pallas_call(
        body,
        out_shape=outs,
        in_specs=specs,
        out_specs=jax.tree.map(lambda _: pl.BlockSpec(memory_space=out_space), outs),
        scratch_shapes=list(scratch),
        compiler_params=pltpu.CompilerParams(vmem_limit_bytes=limit * MIB),
        cost_estimate=cost,
    )


def cost(flops, moved):
    return pl.CostEstimate(flops=int(flops), bytes_accessed=int(moved), transcendentals=0)


def home(region, member):
    return (region, member) if at_home(region, member) else (region ^ 1, member ^ 2)


def at_home(region, member):
    return region % 2 == member // 2


def beside(region, member):
    return (region, member ^ 1) if at_home(region, member) else (region ^ 1, member ^ 3)


def fast(mesh, transmission, probe, measured, positions, past_steps, past_changes, old_gradient):
    regions, members = mesh.shape["region"], mesh.shape["grp"]
    barrier = lax.optimization_barrier

    def send(value, target):
        pairs = []
        for region in range(regions):
            for member in range(members):
                to_region, to_member = target(region, member)
                pairs.append((region * members + member, to_region * members + to_member))
        return lax.ppermute(value, AXES, pairs)

    near = lambda region, member: (region, member ^ 1)
    far = lambda region, member: (region, member ^ 2)
    cross = lambda region, member: (region, member ^ 3)
    mate = lambda region, member: (region ^ 1, member)
    along_x = lambda region, member: (region ^ 2, member)
    along_y = lambda region, member: (region ^ 4, member)
    diagonal = lambda region, member: (region ^ 6, member)

    region, member = lax.axis_index("region"), lax.axis_index("grp")
    core, half, line = region & 1, member & 1, (region >> 1) & 3
    is_home = core == (member >> 1)
    chunk, frame_len = probe.shape[2], probe.shape[3]
    piece_len, tile_len = transmission.shape[1], transmission.shape[2]
    size = jax.ShapeDtypeStruct

    part, which = line & 1, line >> 1
    base = 4 * core + 2 * half
    other_base = 4 * core + 2 * (1 - half)

    def block(mode):
        return lax.dynamic_slice(probe, (part, mode, 0, 0), (1, 1, chunk, frame_len)).reshape(chunk, frame_len)

    same_block, flip_block = block(base + which), block(other_base + which)
    from_far = send(same_block, far)
    from_cross = send(flip_block, cross)
    mate_positions = send(positions, mate)
    piece = call(cut_kernel, size((2, piece_len, frame_len), BF), count=2, smem=(0,), limit=16)(
        positions, transmission
    )
    flip_block, piece = barrier((flip_block, piece))
    from_near = send(flip_block, near)
    target = send(measured[0].astype(BF), home)
    q0 = jnp.concatenate([from_near, from_far, from_cross], axis=0)
    column = jnp.where(is_home, positions[0, 1], mate_positions[0, 1])
    place = jnp.stack([core, member, line, half, column]).astype(jnp.int32)
    piece, place, target, q0 = barrier((piece, place, target, q0))
    q1, q2 = send(q0, along_x), send(q0, along_y)
    own = send(piece, home)
    side = send(piece, beside)
    cut = q0.shape[0] // 2
    q3a, q3b = send(q2[:cut], along_x), send(q1[cut:], along_y)
    own, side, q3a, q3b = barrier((own, side, q3a, q3b))
    mate_own, mate_side = send(own, mate), send(side, mate)
    whole_probe = call(
        probe_kernel,
        size((2, 2, frame_len, frame_len), BF),
        [pltpu.SemaphoreType.DMA((2, 2))],
        count=7,
        smem=(0,),
        far=(1,),
        limit=16,
    )(place, probe, q0, q1, q2, q3a, q3b)

    right = jnp.asarray(propagator(frame_len))
    double = 2 * frame_len
    flops = 2 * 2 * double**3
    half_len = frame_len // 2
    half_field = size((2, 2, frame_len, half_len), BF)
    turned, mates_far, sent = call(
        forward_kernel,
        (size((2, 2, 3, frame_len, half_len), BF), half_field, size((frame_len, half_len), BF)),
        [
            pltpu.VMEM((2, tile_len, frame_len), BF),
            pltpu.VMEM((2, frame_len, frame_len), BF),
            pltpu.VMEM((3, double, frame_len), BF),
            pltpu.VMEM((frame_len, half_len), F32),
        ],
        count=8,
        smem=(0,),
        limit=24,
        cost=cost(3 * flops // 4, 16 * MIB),
    )(place, own, side, mate_own, mate_side, whole_probe, target, right)
    met = send(sent, mate)
    own_far, kept = call(
        rest_kernel,
        (half_field, size((frame_len, half_len), F32)),
        count=4,
        smem=(0,),
        limit=24,
        cost=cost(flops // 4, 4 * MIB),
    )(place, turned, target, right)

    chip = kept + met.astype(F32)
    misfit = chip + send(chip.astype(BF), near).astype(F32)
    mates_misfit = send(misfit.astype(BF), mate)
    own_left = call(
        own_kernel,
        size((3, double, half_len), BF),
        count=3,
        limit=24,
        cost=cost(flops // 4, 4 * MIB),
    )(own_far, misfit, right)

    piece_shape = size((2, piece_len, frame_len), BF)
    sent, kept_side, kept = call(
        backward_kernel,
        (size((2, 2, piece_len, frame_len), BF), piece_shape, piece_shape),
        [
            pltpu.VMEM((3, double, frame_len), BF),
            pltpu.VMEM((2, frame_len, frame_len), BF),
            pltpu.VMEM((4 * piece_len, frame_len), BF),
        ],
        count=6,
        smem=(0,),
        limit=24,
        cost=cost(3 * flops // 4, 12 * MIB),
    )(place, mates_far, whole_probe, mates_misfit, own_left, right)
    met = send(sent, mate)
    add = lambda a, b: (a.astype(F32) + b.astype(F32)).astype(BF)
    kept_side, kept = add(kept_side, met[0]), add(kept, met[1])
    data = add(send(kept, home), send(kept_side, beside))

    devices = regions * members
    moved = 4 * 2 * piece_len * tile_len
    old_row = call(
        old_kernel,
        size((1, LANES), F32),
        [pltpu.VMEM((OLD_PAIRS, 8, LANES), F32)],
        count=2,
        limit=16,
        cost=cost(22 * moved, 7 * moved),
    )(past_steps, past_changes)
    gradient, row = call(
        gradient_kernel,
        (size(transmission.shape, F32), size((devices, LANES), F32)),
        [pltpu.VMEM((len(PAIRS) - OLD_PAIRS, 8, LANES), F32)],
        count=7,
        smem=(0,),
        limit=16,
        cost=cost(16 * moved, 10 * moved),
    )(positions, data, transmission, old_gradient, past_steps, past_changes, old_row)
    all_rows = lax.all_to_all(
        row.reshape(devices, 1, LANES), AXES, split_axis=0, concat_axis=0, tiled=True
    ).reshape(devices, LANES)
    return call(
        update_kernel,
        (size(transmission.shape, F32), size(transmission.shape, F32)),
        [pltpu.VMEM(transmission.shape, F32), pltpu.SemaphoreType.DMA((3,))],
        count=6,
        limit=16,
        cost=cost(10 * moved, 11 * moved),
        out_space=pl.ANY,
    )(all_rows, transmission, gradient, old_gradient, past_steps, past_changes)


def solution(mesh):
    split = mesh.shape["grp"] == 4 and mesh.shape["region"] == 8

    def shards(*args):
        probe, positions, past_steps = args[1], args[3], args[4]
        sized = probe.shape[1] == 8 and positions.shape[0] == 1 and past_steps.shape[0] == HIST
        if split and sized:
            return fast(mesh, *args)
        return general(*args)

    return jax.shard_map(
        shards,
        mesh=mesh,
        in_specs=(
            P(None, "grp", "region"),
            P(None, None, "grp", None),
            P("region", "grp", None),
            P("region", None),
            P(None, None, "grp", "region"),
            P(None, None, "grp", "region"),
            P(None, "grp", "region"),
        ),
        out_specs=(P(None, "grp", "region"), P(None, "grp", "region")),
        check_vma=False,
    )
```

```python
import math

import jax
import jax.numpy as jnp
import ml_dtypes
import numpy as np
from jax import lax
from jax.experimental import pallas as pl
from jax.experimental.pallas import tpu as pltpu
from jax.sharding import PartitionSpec as P

TWO_PI = 2.0 * math.pi
CURVE_FLOOR = 0.25
TIKHONOV = 0.5
EPSILON = 1e-06
BF = jnp.bfloat16
F32 = jnp.float32
AXES = ("region", "grp")
LANES = 128
MIB = 1 << 20
HIST = 4


def dft_tables(count):
    index = jnp.arange(count, dtype=jnp.int32)
    phase = (index[:, None] * index[None, :] % count).astype(jnp.float32) * (TWO_PI / count)
    factor = 1.0 / math.sqrt(count)
    return (
        (jnp.cos(phase) * factor).astype(jnp.bfloat16),
        (-jnp.sin(phase) * factor).astype(jnp.bfloat16),
    )


def chirp_table(count):
    index = jnp.arange(count, dtype=jnp.int32)
    wavenumber = (index + count // 2) % count - count // 2
    phase = (wavenumber * wavenumber % (4 * count)).astype(jnp.float32) * (TWO_PI / (4 * count))
    return (jnp.cos(phase), -jnp.sin(phase))


def rotate(real_part, imag_part, turn_real, turn_imag):
    return (
        real_part * turn_real - imag_part * turn_imag,
        real_part * turn_imag + imag_part * turn_real,
    )


def narrow(pair):
    return jnp.stack([pair[0], pair[1]]).astype(jnp.bfloat16)


def right_product(field, matrix_real, matrix_imag):

    def single(left, right):
        return jnp.einsum("...k,kj->...j", left, right, preferred_element_type=jnp.float32)

    return (
        single(field[0], matrix_real) - single(field[1], matrix_imag),
        single(field[0], matrix_imag) + single(field[1], matrix_real),
    )


def left_product(matrix_real, matrix_imag, field):

    def single(left, right):
        return jnp.einsum("jk,...kc->...jc", left, right, preferred_element_type=jnp.float32)

    return (
        single(matrix_real, field[0]) - single(matrix_imag, field[1]),
        single(matrix_real, field[1]) + single(matrix_imag, field[0]),
    )


def general(transmission, probe, measured, positions, past_steps, past_changes, old_gradient):
    member = lax.axis_index("grp")
    frame_len = probe.shape[3]
    rows_here = probe.shape[2]
    tile_len = transmission.shape[2]
    anchor = jnp.zeros((), jnp.int32)
    fwd_real, fwd_imag = dft_tables(frame_len)
    inv_imag = -fwd_imag
    chirp_real, chirp_imag = chirp_table(frame_len)
    probe_wide = probe.astype(jnp.float32)
    tile = lax.all_gather(transmission.astype(jnp.bfloat16), "grp", axis=1, tiled=True)
    frame = 0
    first_row = positions[frame, 0] + member * rows_here
    window = jnp.swapaxes(
        lax.dynamic_slice(
            tile, (anchor, positions[frame, 1], first_row), (2, frame_len, rows_here)
        ),
        1,
        2,
    ).astype(jnp.float32)
    wave = narrow(rotate(probe_wide[0], probe_wide[1], window[0], window[1]))
    section = narrow(rotate(*right_product(wave, fwd_real, fwd_imag), chirp_real, chirp_imag))
    spread = narrow(right_product(section, fwd_real, inv_imag))
    section = narrow(
        rotate(
            *left_product(
                fwd_real,
                fwd_imag,
                lax.all_to_all(spread, "grp", split_axis=3, concat_axis=2, tiled=True),
            ),
            chirp_real[:, None],
            chirp_imag[:, None]
        )
    )
    far_field = narrow(left_product(fwd_real, inv_imag, section))
    near_rows = lax.all_to_all(far_field, "grp", split_axis=2, concat_axis=3, tiled=True)
    field_wide = near_rows.astype(jnp.float32)
    misfit = (
        jnp.sum(field_wide[0] * field_wide[0] + field_wide[1] * field_wide[1], axis=0)
        - measured[frame]
    )
    weighted = (misfit * field_wide).astype(jnp.bfloat16)
    section = narrow(
        rotate(
            *left_product(
                fwd_real,
                fwd_imag,
                lax.all_to_all(weighted, "grp", split_axis=3, concat_axis=2, tiled=True),
            ),
            chirp_real[:, None],
            -chirp_imag[:, None]
        )
    )
    returned = narrow(left_product(fwd_real, inv_imag, section))
    section = narrow(
        rotate(
            *right_product(
                lax.all_to_all(returned, "grp", split_axis=2, concat_axis=3, tiled=True),
                fwd_real,
                fwd_imag,
            ),
            chirp_real,
            -chirp_imag
        )
    )
    back_wave = jnp.stack(right_product(section, fwd_real, inv_imag))
    grad_real = 4.0 * jnp.sum(probe_wide[0] * back_wave[0] + probe_wide[1] * back_wave[1], axis=0)
    grad_imag = 4.0 * jnp.sum(probe_wide[0] * back_wave[1] - probe_wide[1] * back_wave[0], axis=0)
    frame_grads = [jnp.stack([grad_real, grad_imag])]
    scattered = jnp.zeros((2, tile_len, tile_len), jnp.float32)
    frame = 0
    corner = (anchor, positions[frame, 1], positions[frame, 0] + member * rows_here)
    scattered = lax.dynamic_update_slice(scattered, jnp.swapaxes(frame_grads[frame], 1, 2), corner)
    data_grad = lax.psum_scatter(
        scattered.astype(jnp.bfloat16), "grp", scatter_dimension=1, tiled=True
    ).astype(jnp.float32)
    gradient = data_grad + TIKHONOV * transmission
    depth = past_steps.shape[0]
    last = depth - 1
    change_new = gradient - old_gradient
    steps_list = [past_steps[index] for index in range(depth)]
    changes = [past_changes[index] for index in range(depth - 1)] + [change_new]
    alphas = [None] * depth
    curvature, self_dots, change_norm = lax.psum(
        (
            jnp.stack([jnp.sum(steps_list[index] * changes[index]) for index in range(depth)]),
            jnp.sum(past_steps * past_steps, axis=(1, 2, 3)),
            jnp.sum(change_new * change_new),
        ),
        ("region", "grp"),
    )
    weights = [
        1.0 / jnp.maximum(curvature[index], CURVE_FLOOR * self_dots[index])
        for index in range(depth)
    ]
    direction = gradient
    for index in reversed(range(depth)):
        alphas[index] = weights[index] * lax.psum(
            jnp.sum(steps_list[index] * direction), ("region", "grp")
        )
        direction = direction - alphas[index] * changes[index]
    scale = jnp.maximum(curvature[last], CURVE_FLOOR * self_dots[last]) / (change_norm + EPSILON)
    direction = scale * direction
    for index in range(depth):
        beta = weights[index] * lax.psum(jnp.sum(changes[index] * direction), ("region", "grp"))
        direction = direction + (alphas[index] - beta) * steps_list[index]
    return (transmission - direction, gradient)


def propagator(count):
    index = np.arange(count, dtype=np.int64)
    phase = (index[:, None] * index[None, :] % count).astype(np.float32) * np.float32(TWO_PI / count)
    factor = np.float32(1.0 / math.sqrt(count))
    table = (np.cos(phase) * factor).astype(ml_dtypes.bfloat16).astype(np.float64) + 1j * (
        -np.sin(phase) * factor
    ).astype(ml_dtypes.bfloat16).astype(np.float64)
    wavenumber = (index + count // 2) % count - count // 2
    chirp = np.exp(-1j * (wavenumber * wavenumber % (4 * count)) * (TWO_PI / (4 * count)))
    folded = (table * chirp[None, :]) @ np.conj(table)
    folded = 0.5 * (folded + folded.T)
    real, imag = folded.real, folded.imag
    return np.stack([real, imag - real, real + imag]).astype(ml_dtypes.bfloat16)


def dot(left, right, dims=((1,), (0,))):
    return lax.dot_general(left, right, (dims, ((), ())), preferred_element_type=F32)


def join(sums, reals, imags):
    return sums - imags, sums + reals


def summed(real, imag):
    return (real.astype(F32) + imag.astype(F32)).astype(BF)


def shift_table(rows, columns, row_base, column_base):
    row = lax.broadcasted_iota(jnp.int32, (rows, columns), 0) + row_base
    column = lax.broadcasted_iota(jnp.int32, (rows, columns), 1) + column_base
    return jnp.where(row == column, 1.0, 0.0).astype(BF)


def cut_kernel(pos_ref, tile_ref, out_ref):
    tile_len, frame_len = tile_ref.shape[2], out_ref.shape[2]
    table = shift_table(tile_len, frame_len, 0, pos_ref[0, 0])
    for part in range(2):
        out_ref[part] = dot(tile_ref[part].astype(BF), table).astype(BF)


def probe_kernel(place_ref, all_ref, q0_ref, q1_ref, q2_ref, q3a_ref, q3b_ref, probe_ref, sem):
    core, place, line, half = (place_ref[index] for index in range(4))
    chunk = all_ref.shape[2]

    def rows_of(step):
        return pl.ds(pl.multiple_of(lax.bitwise_xor(place, step) * chunk, chunk), chunk)

    copies = [
        pltpu.make_async_copy(
            all_ref.at[part, 4 * core + 2 * half + mode], probe_ref.at[part, mode, rows_of(0), :], sem.at[part, mode]
        )
        for part in range(2)
        for mode in range(2)
    ]
    for copy in copies:
        copy.start()
    cut = q3a_ref.shape[0]
    for turn, ref in ((0, q0_ref), (1, q1_ref), (2, q2_ref), (3, None)):
        combo = lax.bitwise_xor(line, turn)
        part, mode = lax.rem(combo, 2), lax.div(combo, 2)
        for step in range(1, 4):
            start = (step - 1) * chunk
            if ref is not None:
                value = ref[start : start + chunk]
            elif start + chunk <= cut:
                value = q3a_ref[start : start + chunk]
            elif start >= cut:
                value = q3b_ref[start - cut : start - cut + chunk]
            else:
                value = jnp.concatenate([q3a_ref[start:cut], q3b_ref[: start + chunk - cut]], axis=0)
            probe_ref[part, mode, rows_of(step), :] = value
    for copy in copies:
        copy.wait()


def forward_kernel(
    place_ref, own_ref, side_ref, mate_own_ref, mate_side_ref, probe_ref, measured_ref,
    right_ref, turned_ref, far_ref, send_ref, tile, window_ref, wave, total,
):
    core, half = place_ref[0], place_ref[3]
    chunk, frame_len = measured_ref.shape
    piece_len = own_ref.shape[1]
    piece = 2 * core + half
    for step, ref in enumerate((own_ref, side_ref, mate_own_ref, mate_side_ref)):
        base = pl.multiple_of(lax.bitwise_xor(piece, step) * piece_len, piece_len)
        for part in range(2):
            tile[part, pl.ds(base, piece_len), :] = ref[part]
    column = place_ref[4]
    table = shift_table(tile.shape[1], frame_len, 0, column)
    for part in range(2):
        window_ref[part] = dot(tile[part], table, ((0,), (0,))).astype(BF)

    block = frame_len // 2
    for mode in range(2):
        rows = slice(mode * frame_len, (mode + 1) * frame_len)
        pr, pi = probe_ref[0, mode].astype(F32), probe_ref[1, mode].astype(F32)
        wr, wi = window_ref[0].astype(F32), window_ref[1].astype(F32)
        real, imag = (pr * wr - pi * wi).astype(BF), (pr * wi + pi * wr).astype(BF)
        wave[0, rows], wave[1, rows], wave[2, rows] = summed(real, imag), real, imag
    for cell in range(2):
        columns = slice(cell * block, (cell + 1) * block)
        real, imag = join(*(dot(wave[index], right_ref[index, :, columns]) for index in range(3)))
        real, imag = real.astype(BF), imag.astype(BF)
        total_part = summed(real, imag)
        for mode in range(2):
            rows = slice(mode * frame_len, (mode + 1) * frame_len)
            for index, value in enumerate((total_part, real, imag)):
                turned_ref[mode, cell, index] = value[rows]
    far_columns(1 - core, turned_ref, right_ref, far_ref, total)
    subtract(core, half, 1 - core, measured_ref, total)
    send_ref[...] = total[...].astype(BF)


def far_columns(cell, turned_ref, right_ref, far_ref, total):
    frame_len = total.shape[0]
    power = 0.0
    for mode in range(2):
        real, imag = join(*(dot(right_ref[index], turned_ref[mode, cell, index]) for index in range(3)))
        real, imag = real.astype(BF), imag.astype(BF)
        far_ref[mode, 0] = real
        far_ref[mode, 1] = imag
        real, imag = real.astype(F32), imag.astype(F32)
        power = power + (real * real + imag * imag)
    total[...] = power


def subtract(core, half, cell, measured_ref, total):
    chunk, block = measured_ref.shape[0], total.shape[1]
    rows = pl.ds(pl.multiple_of((2 * core + half) * chunk, chunk), chunk)
    wanted = jnp.where(cell == 0, measured_ref[:, :block], measured_ref[:, block:])
    total[rows, :] = total[rows, :] - wanted.astype(F32)


def rest_kernel(place_ref, turned_ref, measured_ref, right_ref, far_ref, total):
    core, half = place_ref[0], place_ref[3]
    far_columns(core, turned_ref, right_ref, far_ref, total)
    subtract(core, half, core, measured_ref, total)


def left_columns(misfit, far_ref, right_ref, store):
    for mode in range(2):
        real = (misfit * far_ref[mode, 0].astype(F32)).astype(BF)
        imag = (-misfit * far_ref[mode, 1].astype(F32)).astype(BF)
        pieces = (summed(real, imag), real, imag)
        real, imag = join(*(dot(right_ref[index], value) for index, value in enumerate(pieces)))
        real, imag = real.astype(BF), imag.astype(BF)
        for index, value in enumerate((summed(real, imag), real, imag)):
            store(mode, index, value)


def own_kernel(far_ref, mine_ref, right_ref, out_ref):
    frame_len = mine_ref.shape[0]

    def store(mode, part, value):
        out_ref[part, mode * frame_len : (mode + 1) * frame_len, :] = value

    left_columns(mine_ref[...], far_ref, right_ref, store)


def backward_kernel(
    place_ref, far_ref, probe_ref, mates_ref, own_ref, right_ref,
    send_ref, side_ref, keep_ref, turned, grad, table,
):
    core, half = place_ref[0], place_ref[3]
    column = place_ref[4]
    frame_len, block = mates_ref.shape
    piece_len = keep_ref.shape[1]

    def lanes(cell):
        return pl.ds(pl.multiple_of(cell * block, block), block)

    def store(mode, index, value):
        turned[index, mode * frame_len : (mode + 1) * frame_len, lanes(1 - core)] = value

    left_columns(mates_ref[...].astype(F32), far_ref, right_ref, store)
    for index in range(3):
        turned[index, :, lanes(core)] = own_ref[index]
    for cell in range(2):
        columns = slice(cell * block, (cell + 1) * block)
        back = join(*(dot(turned[index], right_ref[index, :, columns]) for index in range(3)))
        real, imag = 0.0, 0.0
        for mode in range(2):
            br, bi = (value[mode * frame_len : (mode + 1) * frame_len] for value in back)
            pr, pi = probe_ref[0, mode, :, columns].astype(F32), probe_ref[1, mode, :, columns].astype(F32)
            real = real + (pr * br - pi * bi)
            imag = imag + (pr * bi + pi * br)
        grad[0, :, columns] = (4.0 * real).astype(BF)
        grad[1, :, columns] = (-4.0 * imag).astype(BF)

    slots = [(1 - core, 1), (1 - core, 0), (core, 1), (core, 0)]
    for index, (pair, flip) in enumerate(slots):
        base = (2 * pair + lax.bitwise_xor(half, flip)) * piece_len
        table[index * piece_len : (index + 1) * piece_len, :] = shift_table(piece_len, frame_len, base, column)
    for part in range(2):
        value = dot(table[...], grad[part], ((1,), (1,))).astype(BF)
        send_ref[0, part] = value[:piece_len]
        send_ref[1, part] = value[piece_len : 2 * piece_len]
        side_ref[part] = value[2 * piece_len : 3 * piece_len]
        keep_ref[part] = value[3 * piece_len :]


PAIRS = [("sy", i, j) for j in range(HIST - 1) for i in range(HIST)]
PAIRS += [("ss", i, i) for i in range(HIST)]
PAIRS += [("yy", i, j) for j in range(HIST - 1) for i in range(j + 1)]
OLD_PAIRS = len(PAIRS)
PAIRS += [("sy", i, HIST - 1) for i in range(HIST)]
PAIRS += [("yy", i, HIST - 1) for i in range(HIST)]
PAIRS += [("sg", i, i) for i in range(HIST)]
PAIRS += [("yg", i, i) for i in range(HIST)]
SLOT = {pair: index for index, pair in enumerate(PAIRS)}


def folded(value):
    parts, rows, columns = value.shape
    total = jnp.sum(value.reshape(parts * rows // 8, 8, columns), axis=0)
    return sum(total[:, start : start + LANES] for start in range(0, columns, LANES))


def add_products(sums, first, slots, vectors):
    for slot, pair in slots:
        kind, i, j = pair
        left = vectors[kind[0]][i]
        right = vectors["g"][0] if kind[1] == "g" else vectors[kind[1]][j]
        value = folded(left * right)
        sums[slot] = value if first else sums[slot] + value


def lane_row(sums, count):
    rows = [jnp.sum(sums[slot], axis=0, keepdims=True) for slot in range(count)]
    square = jnp.concatenate(rows + [jnp.zeros((LANES - count, LANES), F32)], axis=0)
    return jnp.sum(square.T, axis=0, keepdims=True)


BLOCK = 32


def column_blocks(ref):
    return range(0, ref.shape[-2], BLOCK)


def old_kernel(steps_ref, changes_ref, out_ref, sums):
    for start in column_blocks(steps_ref):
        columns = slice(start, start + BLOCK)
        vectors = {
            "s": [steps_ref[index, :, columns] for index in range(HIST)],
            "y": [changes_ref[index, :, columns] for index in range(HIST - 1)],
        }
        add_products(sums, start == 0, enumerate(PAIRS[:OLD_PAIRS]), vectors)
    out_ref[...] = lane_row(sums, OLD_PAIRS)


def gradient_kernel(
    pos_ref, data_ref, transmission_ref, old_ref, steps_ref, changes_ref, row_ref, gradient_ref, out_ref, sums
):
    table = shift_table(data_ref.shape[2], transmission_ref.shape[2], pos_ref[0, 0], 0)
    parts, piece_len, frame_len = data_ref.shape
    placed = dot(data_ref[...].reshape(parts * piece_len, frame_len), table)
    gradient_ref[...] = placed.reshape(transmission_ref.shape) + TIKHONOV * transmission_ref[...]
    for start in column_blocks(transmission_ref):
        columns = slice(start, start + BLOCK)
        gradient = gradient_ref[:, columns]
        vectors = {
            "s": [steps_ref[index, :, columns] for index in range(HIST)],
            "y": [changes_ref[index, :, columns] for index in range(HIST - 1)]
            + [gradient - old_ref[:, columns]],
            "g": [gradient],
        }
        add_products(sums, start == 0, enumerate(PAIRS[OLD_PAIRS:]), vectors)
    fresh = pltpu.roll(lane_row(sums, len(PAIRS) - OLD_PAIRS), OLD_PAIRS, 1)
    out_ref[...] = jnp.broadcast_to(fresh + row_ref[...], out_ref.shape)


def update_kernel(
    rows_ref, transmission_ref, gradient_ref, old_ref, steps_ref, changes_ref, updated_ref, copy_ref, out_ref, sem
):
    copies = [pltpu.make_async_copy(gradient_ref, copy_ref, sem.at[2])]
    copies[0].start()
    row = jnp.sum(rows_ref[...], axis=0, keepdims=True)
    lane = lax.broadcasted_iota(jnp.int32, row.shape, 1)

    def get(kind, i, j):
        if kind == "yy" and i > j:
            i, j = j, i
        picked = jnp.where(lane == SLOT[(kind, i, j)], row, 0.0)
        return jnp.broadcast_to(jnp.sum(picked, axis=1, keepdims=True), row.shape)

    last = HIST - 1
    floors = [
        jnp.maximum(get("sy", index, index), CURVE_FLOOR * get("ss", index, index)) for index in range(HIST)
    ]
    weights = [1.0 / floor for floor in floors]
    alphas = [None] * HIST
    for index in reversed(range(HIST)):
        value = get("sg", index, index)
        for later in range(index + 1, HIST):
            value = value - alphas[later] * get("sy", index, later)
        alphas[index] = weights[index] * value
    scale = floors[last] / (get("yy", last, last) + EPSILON)
    moves = []
    for index in range(HIST):
        value = get("yg", index, index)
        for other in range(HIST):
            value = value - alphas[other] * get("yy", index, other)
        value = scale * value
        for before in range(index):
            value = value + moves[before] * get("sy", before, index)
        moves.append(alphas[index] - weights[index] * value)
    repeat = out_ref.shape[-1] // LANES
    wide = lambda value: jnp.concatenate([value] * repeat, axis=1)
    scale_row = wide(scale)
    change_rows = [wide(-scale * alpha) for alpha in alphas]
    step_rows = [wide(move) for move in moves]
    for part in range(2):
        for start in column_blocks(out_ref):
            columns = slice(start, start + BLOCK)
            gradient = gradient_ref[part, columns]
            total = scale_row * gradient + change_rows[last] * (gradient - old_ref[part, columns])
            for index in range(HIST - 1):
                total = total + change_rows[index] * changes_ref[index, part, columns]
            for index in range(HIST):
                total = total + step_rows[index] * steps_ref[index, part, columns]
            out_ref[part, columns] = transmission_ref[part, columns] - total
        copies.append(pltpu.make_async_copy(out_ref.at[part], updated_ref.at[part], sem.at[part]))
        copies[-1].start()
    for copy in copies:
        copy.wait()


def call(body, outs, scratch=(), limit=48, smem=(), far=(), count=0, cost=None, out_space=pltpu.VMEM):
    space = lambda index: pltpu.SMEM if index in smem else pl.ANY if index in far else pltpu.VMEM
    specs = [pl.BlockSpec(memory_space=space(index)) for index in range(count)]
    return pl.pallas_call(
        body,
        out_shape=outs,
        in_specs=specs,
        out_specs=jax.tree.map(lambda _: pl.BlockSpec(memory_space=out_space), outs),
        scratch_shapes=list(scratch),
        compiler_params=pltpu.CompilerParams(vmem_limit_bytes=limit * MIB),
        cost_estimate=cost,
    )


def cost(flops, moved):
    return pl.CostEstimate(flops=int(flops), bytes_accessed=int(moved), transcendentals=0)


def home(region, member):
    return (region, member) if at_home(region, member) else (region ^ 1, member ^ 2)


def at_home(region, member):
    return region % 2 == member // 2


def beside(region, member):
    return (region, member ^ 1) if at_home(region, member) else (region ^ 1, member ^ 3)


def fast(mesh, transmission, probe, measured, positions, past_steps, past_changes, old_gradient):
    regions, members = mesh.shape["region"], mesh.shape["grp"]
    barrier = lax.optimization_barrier

    def send(value, target):
        pairs = []
        for region in range(regions):
            for member in range(members):
                to_region, to_member = target(region, member)
                pairs.append((region * members + member, to_region * members + to_member))
        return lax.ppermute(value, AXES, pairs)

    near = lambda region, member: (region, member ^ 1)
    far = lambda region, member: (region, member ^ 2)
    cross = lambda region, member: (region, member ^ 3)
    mate = lambda region, member: (region ^ 1, member)
    along_x = lambda region, member: (region ^ 2, member)
    along_y = lambda region, member: (region ^ 4, member)
    diagonal = lambda region, member: (region ^ 6, member)

    region, member = lax.axis_index("region"), lax.axis_index("grp")
    core, half, line = region & 1, member & 1, (region >> 1) & 3
    is_home = core == (member >> 1)
    chunk, frame_len = probe.shape[2], probe.shape[3]
    piece_len, tile_len = transmission.shape[1], transmission.shape[2]
    size = jax.ShapeDtypeStruct

    part, which = line & 1, line >> 1
    base = 4 * core + 2 * half
    other_base = 4 * core + 2 * (1 - half)

    def block(mode):
        return lax.dynamic_slice(probe, (part, mode, 0, 0), (1, 1, chunk, frame_len)).reshape(chunk, frame_len)

    same_block, flip_block = block(base + which), block(other_base + which)
    from_far = send(same_block, far)
    from_cross = send(flip_block, cross)
    mate_positions = send(positions, mate)
    piece = call(cut_kernel, size((2, piece_len, frame_len), BF), count=2, smem=(0,), limit=16)(
        positions, transmission
    )
    flip_block, piece = barrier((flip_block, piece))
    from_near = send(flip_block, near)
    target = send(measured[0].astype(BF), home)
    q0 = jnp.concatenate([from_near, from_far, from_cross], axis=0)
    column = jnp.where(is_home, positions[0, 1], mate_positions[0, 1])
    place = jnp.stack([core, member, line, half, column]).astype(jnp.int32)
    q1 = send(q0, along_x)
    piece, place, target, q0 = barrier((piece, place, target, q0))
    q2 = send(q0, along_y)
    own = send(piece, home)
    side = send(piece, beside)
    cut = q0.shape[0] // 2
    q3a, q3b = send(q2[:cut], along_x), send(q1[cut:], along_y)
    own, side, q3a, q3b = barrier((own, side, q3a, q3b))
    mate_own, mate_side = send(own, mate), send(side, mate)
    whole_probe = call(
        probe_kernel,
        size((2, 2, frame_len, frame_len), BF),
        [pltpu.SemaphoreType.DMA((2, 2))],
        count=7,
        smem=(0,),
        far=(1,),
        limit=16,
    )(place, probe, q0, q1, q2, q3a, q3b)

    right = jnp.asarray(propagator(frame_len))
    double = 2 * frame_len
    flops = 2 * 2 * double**3
    half_len = frame_len // 2
    half_field = size((2, 2, frame_len, half_len), BF)
    turned, mates_far, sent = call(
        forward_kernel,
        (size((2, 2, 3, frame_len, half_len), BF), half_field, size((frame_len, half_len), BF)),
        [
            pltpu.VMEM((2, tile_len, frame_len), BF),
            pltpu.VMEM((2, frame_len, frame_len), BF),
            pltpu.VMEM((3, double, frame_len), BF),
            pltpu.VMEM((frame_len, half_len), F32),
        ],
        count=8,
        smem=(0,),
        limit=24,
        cost=cost(3 * flops // 4, 16 * MIB),
    )(place, own, side, mate_own, mate_side, whole_probe, target, right)
    met = send(sent, mate)
    own_far, kept = call(
        rest_kernel,
        (half_field, size((frame_len, half_len), F32)),
        count=4,
        smem=(0,),
        limit=24,
        cost=cost(flops // 4, 4 * MIB),
    )(place, turned, target, right)

    chip = kept + met.astype(F32)
    misfit = chip + send(chip.astype(BF), near).astype(F32)
    mates_misfit = send(misfit.astype(BF), mate)
    own_left = call(
        own_kernel,
        size((3, double, half_len), BF),
        count=3,
        limit=24,
        cost=cost(flops // 4, 4 * MIB),
    )(own_far, misfit, right)

    piece_shape = size((2, piece_len, frame_len), BF)
    sent, kept_side, kept = call(
        backward_kernel,
        (size((2, 2, piece_len, frame_len), BF), piece_shape, piece_shape),
        [
            pltpu.VMEM((3, double, frame_len), BF),
            pltpu.VMEM((2, frame_len, frame_len), BF),
            pltpu.VMEM((4 * piece_len, frame_len), BF),
        ],
        count=6,
        smem=(0,),
        limit=24,
        cost=cost(3 * flops // 4, 12 * MIB),
    )(place, mates_far, whole_probe, mates_misfit, own_left, right)
    met = send(sent, mate)
    add = lambda a, b: (a.astype(F32) + b.astype(F32)).astype(BF)
    kept_side, kept = add(kept_side, met[0]), add(kept, met[1])
    data = add(send(kept, home), send(kept_side, beside))

    devices = regions * members
    moved = 4 * 2 * piece_len * tile_len
    old_row = call(
        old_kernel,
        size((1, LANES), F32),
        [pltpu.VMEM((OLD_PAIRS, 8, LANES), F32)],
        count=2,
        limit=16,
        cost=cost(22 * moved, 7 * moved),
    )(past_steps, past_changes)
    gradient, row = call(
        gradient_kernel,
        (size(transmission.shape, F32), size((devices, LANES), F32)),
        [pltpu.VMEM((len(PAIRS) - OLD_PAIRS, 8, LANES), F32)],
        count=7,
        smem=(0,),
        limit=16,
        cost=cost(16 * moved, 10 * moved),
    )(positions, data, transmission, old_gradient, past_steps, past_changes, old_row)
    all_rows = lax.all_to_all(
        row.reshape(devices, 1, LANES), AXES, split_axis=0, concat_axis=0, tiled=True
    ).reshape(devices, LANES)
    return call(
        update_kernel,
        (size(transmission.shape, F32), size(transmission.shape, F32)),
        [pltpu.VMEM(transmission.shape, F32), pltpu.SemaphoreType.DMA((3,))],
        count=6,
        limit=16,
        cost=cost(10 * moved, 11 * moved),
        out_space=pl.ANY,
    )(all_rows, transmission, gradient, old_gradient, past_steps, past_changes)


def solution(mesh):
    split = mesh.shape["grp"] == 4 and mesh.shape["region"] == 8

    def shards(*args):
        probe, positions, past_steps = args[1], args[3], args[4]
        sized = probe.shape[1] == 8 and positions.shape[0] == 1 and past_steps.shape[0] == HIST
        if split and sized:
            return fast(mesh, *args)
        return general(*args)

    return jax.shard_map(
        shards,
        mesh=mesh,
        in_specs=(
            P(None, "grp", "region"),
            P(None, None, "grp", None),
            P("region", "grp", None),
            P("region", None),
            P(None, None, "grp", "region"),
            P(None, None, "grp", "region"),
            P(None, "grp", "region"),
        ),
        out_specs=(P(None, "grp", "region"), P(None, "grp", "region")),
        check_vma=False,
    )
```
